32 devices in a mesh: ctx: 8 (over z, y), head: 4 (over x, core).
Axes of the slice: x: 2, y: 2, z: 4, core: 2. Of those that a mesh axis runs over, the one named last changes fastest.
Arguments:
- stream: bfloat16 [4096, 2048], P(('ctx', 'head')), may hold values from -6 to 6
- moe_gain: float32 [2048], replicated, may hold values from 0.5 to 1.5
- router: bfloat16 [2048, 64], replicated, may hold values from -0.125 to 0.125
- expert_ids: int32 [4096, 10], P(('ctx', 'head')), may hold values from 0 to 63, all different within a row; in each aligned block of 128 rows (0 to 127, 128 to 255, ...) at most 22 rows name the same one
- expert_gate: bfloat16 [64, 2048, 512], P(('ctx', 'head')), may hold values from -0.125 to 0.125
- expert_up: bfloat16 [64, 2048, 512], P(('ctx', 'head')), may hold values from -0.125 to 0.125
- expert_down: bfloat16 [64, 512, 2048], P(('ctx', 'head')), may hold values from -1 to 1
- mixer_gain: float32 [2048], replicated, may hold values from 0.5 to 1.5
- query_weight: bfloat16 [2048, 1024], P(None, 'head'), may hold values from -0.125 to 0.125
- key_weight: bfloat16 [2048, 1024], P(None, 'head'), may hold values from -0.125 to 0.125
- value_weight: bfloat16 [2048, 2048], P(None, 'head'), may hold values from -0.125 to 0.125
- output_gate: bfloat16 [2048, 2048], P(None, 'head'), may hold values from -0.125 to 0.125
- beta_weight: bfloat16 [2048, 16], P(None, 'head'), may hold values from -0.125 to 0.125
- decay_weight: bfloat16 [2048, 16], P(None, 'head'), may hold values from -0.5 to 0.5
- query_conv: float32 [4, 1024], P(None, 'head'), may hold values from -3 to 3
- key_conv: float32 [4, 1024], P(None, 'head'), may hold values from -3 to 3
- value_conv: float32 [4, 2048], P(None, 'head'), may hold values from -3 to 3
- decay_log: float32 [16], P('head'), may hold values from -12 to -2.5
- decay_bias: float32 [16], P('head'), may hold values from -2 to 1
- head_gain: float32 [128], replicated, may hold values from 0.5 to 1.5
- out_weight: bfloat16 [2048, 2048], P('head'), may hold values from -0.125 to 0.125
Outputs:
- moe_out: bfloat16 [4096, 2048], P(('ctx', 'head'))
- mixer_out: bfloat16 [4096, 2048], P(('ctx', 'head'))
The draws below stay inside these ranges and needn't reach their ends.
Inputs may be any that keep to these rules, and one draw needn't show every extreme that they name: `expert_ids`: each row names 10 different experts; in each aligned block of 128 rows (the rows of one device) no expert is named by more than 22 rows, a bound that some block reaches.
All inputs are finite; a program needn't handle non-finite values.
Results may differ from the reference program's by a relative error of at most 0.017.
Values may be sent and summed in bfloat16 or wider, within the bound.
No kernel may reach another device: no remote copies, remote signals or barrier semaphores. Data moves between devices by JAX's collectives and lax.ppermute only.
A program may use at most 128 MiB of HBM per device.

```python
import math
import jax
import jax.numpy as jnp
import numpy as np
from jax import lax

D = 2048
EH = 512
VH = 16
KH = 8
DK = 128
DV = 128
TOPK = 10
KCONV = 4
TOK_DEV = 128
EXPERTS = 64
CAP = 22
TOKENS = 4096
N_CTX = 8
N_HEAD = 4


def draw_decay_log(key, part):
    drawn = jax.random.uniform(key, (VH,), jnp.float32, -11.0, -2.5)
    return drawn


def steps_of(key, extent, pieces, smallest, largest):
    level = 1.0
    for position, blocks in pieces:
        steps = jax.random.uniform(jax.random.fold_in(jax.random.fold_in(key, 6), position), (blocks,), jnp.float32, smallest / len(pieces), largest / len(pieces))
        level = level * jnp.repeat(jnp.exp(steps), extent[position] // blocks).reshape((-1,) + (1,) * (len(extent) - 1 - position))
    return level


def routed_block(rng, own, number, rows, count, top, most, skew):
    sequence = jax.random.permutation(rng, count)
    heavy_load, ordinary = shares(count, rows * top, most, skew, True), shares(count, rows * top, most, skew, False)
    places = jnp.arange(count)

    def named(tallies, offset_by):
        used = int((tallies > 0).sum())
        fixed = max(1, used // 4)
        moved = fixed + (places - fixed + offset_by * (used - fixed)) % max(1, count - fixed)
        return jnp.zeros((count,), jnp.int32).at[sequence[jnp.where(places < fixed, places, moved)]].set(jnp.asarray(tallies, jnp.int32))

    tallies = jnp.where(number % 4 == 0, named(heavy_load, number // 4), named(ordinary, number - number // 4 - 1))
    mixed = jax.random.permutation(jax.random.fold_in(own, 3), count)
    source_of, sink = mixed[0:count // 2 * 2:2], mixed[1:count // 2 * 2:2]
    slack = jnp.minimum(tallies[source_of] - 1, most - tallies[sink]) // 2
    slack = jnp.where((source_of == sequence[0]) | (sink == sequence[0]) | (tallies[sink] == 0), 0, jnp.maximum(slack, 0))
    moved = jax.random.randint(jax.random.fold_in(own, 4), (count // 2,), 0, 1 << 20) % (slack + 1)
    tallies = tallies.at[source_of].add(-moved).at[sink].add(moved)
    members = jnp.searchsorted(jnp.cumsum(tallies), jnp.arange(rows * top), side="right").astype(jnp.int32)
    table = members.reshape(top, rows).T
    table = table[jax.random.permutation(jax.random.fold_in(own, 1), rows)]
    offset_by = jax.random.randint(jax.random.fold_in(own, 2), (rows, 1), 0, top)
    return jnp.take_along_axis(table, (jnp.arange(top)[None, :] + offset_by) % top, axis=1)


def shares(number_of, total, reach, skew, full):
    loads = [(1 << 20) // math.isqrt(standing ** skew) + 1 for standing in range(1, number_of + 1)]
    largest = reach if full else min(reach, max(-(-total // number_of), total * loads[0] // sum(loads)))
    least = 1 if total - largest >= number_of - 1 else 0
    given, surplus = [largest] + [least] * (number_of - 1), total - largest - least * (number_of - 1)
    while surplus > 0:
        movable = [i for i in range(1, number_of) if given[i] < largest] or [i for i in range(1, number_of) if given[i] < reach]
        whole, left = sum([loads[i] for i in movable]), surplus
        for i in movable:
            addition = min(reach - given[i], max(1, left * loads[i] // whole), surplus)
            given[i] = given[i] + addition
            surplus = surplus - addition
    return np.array(given)


def bell_draw(stream_key, shape, deviation, reach, cuts=(), kind=jnp.bfloat16):
    level = steps_of(stream_key, shape, cuts, -0.22, 0.18) if cuts else 1.0
    entries = jax.random.normal(stream_key, shape, jnp.float32) * deviation * level
    return jnp.minimum(jnp.maximum(entries, -reach), reach).astype(kind)


def setup_inputs(seed: int = 0) -> dict:
    streams_of = jax.random.split(jax.random.key(seed), 22)
    stream = bell_draw(streams_of[0], (TOKENS, D), 1.0, 6.0, ((0, 32),))
    moe_gain = jnp.clip(1.0 + 0.1 * jax.random.normal(streams_of[1], (D,), jnp.float32), 0.5, 1.5)
    router = bell_draw(streams_of[2], (D, EXPERTS), D ** -0.5, 0.125)
    expert_ids_keys = jax.random.split(jax.random.fold_in(streams_of[3], 1), TOKENS // TOK_DEV)
    expert_ids_turns = jax.random.permutation(jax.random.fold_in(streams_of[3], 3), TOKENS // TOK_DEV)
    expert_ids = jax.vmap(lambda own, number: routed_block(jax.random.fold_in(streams_of[3], 2), own, number, TOK_DEV, EXPERTS, TOPK, CAP, 1))(expert_ids_keys, expert_ids_turns).reshape((TOKENS, TOPK))
    expert_gate = bell_draw(streams_of[4], (EXPERTS, D, EH), D ** -0.5, 0.125, ((0, 32),))
    expert_up = bell_draw(streams_of[5], (EXPERTS, D, EH), D ** -0.5, 0.125, ((0, 32),))
    expert_down = bell_draw(streams_of[6], (EXPERTS, EH, D), (EH // 16) ** -0.5, 1.0, ((0, 32),))
    mixer_gain = jnp.clip(1.0 + 0.1 * jax.random.normal(streams_of[7], (D,), jnp.float32), 0.5, 1.5)
    query_weight = bell_draw(streams_of[8], (D, KH * DK), D ** -0.5, 0.125, ((1, 4),))
    key_weight = bell_draw(streams_of[9], (D, KH * DK), D ** -0.5, 0.125, ((1, 4),))
    value_weight = bell_draw(streams_of[10], (D, VH * DV), D ** -0.5, 0.125, ((1, 4),))
    output_gate = bell_draw(streams_of[11], (D, VH * DV), D ** -0.5, 0.125, ((1, 4),))
    beta_weight = bell_draw(streams_of[12], (D, VH), D ** -0.5, 0.125, ((1, 4),))
    decay_weight = bell_draw(streams_of[13], (D, VH), (D // 16) ** -0.5, 0.5, ((1, 4),))
    query_conv = bell_draw(streams_of[14], (KCONV, KH * DK), 0.5, 3.0, ((1, 4),), jnp.float32)
    key_conv = bell_draw(streams_of[15], (KCONV, KH * DK), 0.5, 3.0, ((1, 4),), jnp.float32)
    value_conv = bell_draw(streams_of[16], (KCONV, VH * DV), 0.5, 3.0, ((1, 4),), jnp.float32)
    decay_log = draw_decay_log(jax.random.fold_in(streams_of[21], 71), 0)
    decay_bias = jnp.clip(-2.0 + 3.0 * jax.random.uniform(streams_of[18], (VH,), jnp.float32) ** steps_of(streams_of[18], (VH,), ((0, 4),), -0.2, 0.2), -2.0, 1.0)
    head_gain = jnp.clip(1.0 + 0.1 * jax.random.normal(streams_of[19], (DV,), jnp.float32), 0.5, 1.5)
    out_weight = bell_draw(streams_of[20], (VH * DV, D), (VH * DV) ** -0.5, 0.125, ((0, 4),))
    return dict(stream=stream, moe_gain=moe_gain, router=router, expert_ids=expert_ids, expert_gate=expert_gate, expert_up=expert_up, expert_down=expert_down, mixer_gain=mixer_gain, query_weight=query_weight, key_weight=key_weight, value_weight=value_weight, output_gate=output_gate, beta_weight=beta_weight, decay_weight=decay_weight, query_conv=query_conv, key_conv=key_conv, value_conv=value_conv, decay_log=decay_log, decay_bias=decay_bias, head_gain=head_gain, out_weight=out_weight)


epsilon = 1e-06
exact_precision = lax.Precision.HIGHEST

def rms_rows(values, gain):
    values = values.astype(jnp.float32)
    scale = lax.rsqrt(lax.optimization_barrier(jnp.mean(values * values, axis=-1, keepdims=True)) + epsilon)
    return values * scale * gain.astype(jnp.float32)

def block_terms(queries, key_rows, values, strength, decays):
    length = queries.shape[0]
    cumulative = jnp.cumsum(decays)
    spread = cumulative[:, None] - cumulative[None, :]
    positions = jnp.arange(length, dtype=jnp.int32)
    strict = positions[:, None] > positions[None, :]
    inclusive = positions[:, None] >= positions[None, :]
    fall_strict = jnp.where(strict, jnp.exp(jnp.where(strict, spread, 0.0)), 0.0)
    fall_inclusive = jnp.where(inclusive, jnp.exp(jnp.where(inclusive, spread, 0.0)), 0.0)
    key_dots = jnp.dot(key_rows, key_rows.T, precision=exact_precision)
    strict_part = strength[:, None] * fall_strict * key_dots
    system = jnp.eye(length, dtype=jnp.float32) + strict_part
    targets = strength[:, None] * jnp.concatenate([values, jnp.exp(cumulative)[:, None] * key_rows], axis=1)
    solved = jax.scipy.linalg.solve_triangular(system, targets, lower=True, unit_diagonal=True)
    value_width = values.shape[1]
    w_values = solved[:, :value_width]
    w_keys = solved[:, value_width:]
    mixing = fall_inclusive * jnp.dot(queries, key_rows.T, precision=exact_precision)
    q_decayed = jnp.exp(cumulative)[:, None] * queries
    k_decayed = jnp.exp(cumulative[-1] - cumulative)[:, None] * key_rows
    closing = jnp.exp(cumulative[-1])
    return (w_values, w_keys, mixing, q_decayed, k_decayed, closing)

def delta_head(queries, key_rows, values, strength, decays):
    length = queries.shape[0]
    block_len = math.gcd(length, 64)
    block_count = length // block_len

    def split_blocks(array):
        return array.reshape((block_count, block_len) + array.shape[1:])
    terms = jax.vmap(block_terms)(split_blocks(queries), split_blocks(key_rows), split_blocks(values), split_blocks(strength), split_blocks(decays))

    def advance(state_now, block_term):
        w_values, w_keys, mixing, q_decayed, k_decayed, closing = block_term
        update = w_values - jnp.dot(w_keys, state_now, precision=exact_precision)
        result = jnp.dot(q_decayed, state_now, precision=exact_precision) + jnp.dot(mixing, update, precision=exact_precision)
        state_now = closing * state_now + jnp.dot(k_decayed.T, update, precision=exact_precision)
        return (state_now, result)
    initial = jnp.zeros((key_rows.shape[1], values.shape[1]), jnp.float32)
    final_state, results = lax.scan(advance, initial, terms)
    return results.reshape(length, values.shape[1])

def unit_heads(array, heads):
    reshaped_rows = array.reshape(array.shape[0], heads, -1)
    return reshaped_rows * lax.rsqrt(lax.optimization_barrier(jnp.sum(reshaped_rows * reshaped_rows, axis=-1, keepdims=True)) + epsilon)

def causal_conv(raw_rows, taps):
    row_count = raw_rows.shape[0]
    extended = jnp.concatenate([jnp.zeros((KCONV - 1, raw_rows.shape[1]), jnp.float32), raw_rows.astype(jnp.float32)], axis=0)
    summed = jnp.zeros((row_count, raw_rows.shape[1]), jnp.float32)
    for shift_index in range(KCONV):
        summed = summed + taps[shift_index][None, :] * extended[shift_index:shift_index + row_count]
    return jax.nn.silu(summed)

def reference(stream, moe_gain, router, expert_ids, expert_gate, expert_up, expert_down, mixer_gain, query_weight, key_weight, value_weight, output_gate, beta_weight, decay_weight, query_conv, key_conv, value_conv, decay_log, decay_bias, head_gain, out_weight):
    sources = N_CTX * N_HEAD
    normed = rms_rows(stream, moe_gain).astype(jnp.bfloat16)
    logits = jnp.dot(normed.astype(jnp.float32), router.astype(jnp.float32), preferred_element_type=jnp.float32)
    chosen = jnp.take_along_axis(logits, expert_ids, axis=1)
    raised = jnp.exp(chosen)
    weights = raised / lax.optimization_barrier(jnp.sum(raised, axis=1, keepdims=True))
    block_ids = expert_ids.reshape(sources, TOK_DEV * TOPK)

    def rank_block(ids_row):
        matches = (ids_row[:, None] == jnp.arange(EXPERTS, dtype=jnp.int32)[None, :]).astype(jnp.int32)
        ranks = jnp.cumsum(matches, axis=0) - 1
        return lax.optimization_barrier(jnp.sum(ranks * matches, axis=1)).astype(jnp.int32)
    slot_index = lax.map(rank_block, block_ids)
    source_index = jnp.arange(sources, dtype=jnp.int32)[:, None]
    places = (block_ids * (sources * CAP) + source_index * CAP + slot_index).reshape(-1).astype(jnp.int32)
    token_index = (jnp.arange(TOKENS * TOPK, dtype=jnp.int32) // TOPK).astype(jnp.int32)
    slot_table = jnp.full((EXPERTS * sources * CAP,), TOKENS, jnp.int32).at[places].set(token_index)
    slot_weights = jnp.zeros((EXPERTS * sources * CAP,), jnp.float32).at[places].set(weights.reshape(-1))
    padded = jnp.concatenate([normed, jnp.zeros((1, D), jnp.bfloat16)], axis=0)

    def one_expert(summed, packed):
        row_index, row_weights, gate_matrix, up_matrix, down_matrix = packed
        inputs = padded[row_index]
        gate_part = jnp.dot(inputs.astype(jnp.float32), gate_matrix.astype(jnp.float32), preferred_element_type=jnp.float32)
        up_part = jnp.dot(inputs.astype(jnp.float32), up_matrix.astype(jnp.float32), preferred_element_type=jnp.float32)
        hidden = (jax.nn.silu(gate_part) * up_part).astype(jnp.bfloat16)
        output_list = jnp.dot(hidden.astype(jnp.float32), down_matrix.astype(jnp.float32), preferred_element_type=jnp.float32).astype(jnp.bfloat16)
        summed = summed.at[row_index].add(row_weights[:, None] * output_list.astype(jnp.float32))
        return (summed, None)
    start_sum = jnp.zeros((TOKENS + 1, D), jnp.float32)
    summed, unused = lax.scan(one_expert, start_sum, (slot_table.reshape(EXPERTS, sources * CAP), slot_weights.reshape(EXPERTS, sources * CAP), expert_gate, expert_up, expert_down))
    moe_out = summed[:TOKENS].astype(jnp.bfloat16)
    mixer_in = rms_rows(stream.astype(jnp.float32) + moe_out.astype(jnp.float32), mixer_gain).astype(jnp.bfloat16)
    query_raw = jnp.dot(mixer_in.astype(jnp.float32), query_weight.astype(jnp.float32), preferred_element_type=jnp.float32).astype(jnp.bfloat16)
    key_raw = jnp.dot(mixer_in.astype(jnp.float32), key_weight.astype(jnp.float32), preferred_element_type=jnp.float32).astype(jnp.bfloat16)
    value_raw = jnp.dot(mixer_in.astype(jnp.float32), value_weight.astype(jnp.float32), preferred_element_type=jnp.float32).astype(jnp.bfloat16)
    gate_raw = jnp.dot(mixer_in.astype(jnp.float32), output_gate.astype(jnp.float32), preferred_element_type=jnp.float32).astype(jnp.bfloat16)
    beta_raw = jnp.dot(mixer_in.astype(jnp.float32), beta_weight.astype(jnp.float32), preferred_element_type=jnp.float32)
    decay_raw = jnp.dot(mixer_in.astype(jnp.float32), decay_weight.astype(jnp.float32), preferred_element_type=jnp.float32)
    queries = unit_heads(causal_conv(query_raw, query_conv), KH) * DK ** (-0.5)
    key_rows = unit_heads(causal_conv(key_raw, key_conv), KH)
    values = causal_conv(value_raw, value_conv).reshape(TOKENS, VH, DV)
    strength = jax.nn.sigmoid(beta_raw)
    decays = -jnp.exp(decay_log)[None, :] * jax.nn.softplus(decay_raw + decay_bias[None, :])
    group_size = VH // KH
    query_heads = jnp.repeat(queries, group_size, axis=1).transpose(1, 0, 2)
    key_heads = jnp.repeat(key_rows, group_size, axis=1).transpose(1, 0, 2)

    def run_head(packed):
        return delta_head(packed[0], packed[1], packed[2], packed[3], packed[4])
    delta_core_output = lax.map(run_head, (query_heads, key_heads, values.transpose(1, 0, 2), strength.T, decays.T))
    delta_core_output = delta_core_output.transpose(1, 0, 2)
    normal = delta_core_output * lax.rsqrt(lax.optimization_barrier(jnp.mean(delta_core_output * delta_core_output, axis=-1, keepdims=True)) + epsilon) * head_gain
    gate_values = gate_raw.astype(jnp.float32).reshape(TOKENS, VH, DV)
    gated_out = (normal * jax.nn.silu(gate_values)).astype(jnp.bfloat16).reshape(TOKENS, VH * DV)
    mixer_out = jnp.dot(gated_out.astype(jnp.float32), out_weight.astype(jnp.float32), preferred_element_type=jnp.float32).astype(jnp.bfloat16)
    return (moe_out, mixer_out)
```

```python
import functools
import math

import jax
import jax.numpy as jnp
from jax import lax
from jax.experimental import pallas as pl
from jax.experimental.pallas import tpu as pltpu
from jax.sharding import PartitionSpec as P

DK = 128
CHUNK = 128
GROUP = 256
GATHER_LIMIT = 32 << 20


epsilon = 1e-06
f32 = jnp.float32
bf16 = jnp.bfloat16


def passed_along(value, axis, steps):
    count = lax.axis_size(axis)
    first, last = (max(0, -steps), min(count, count - steps))
    return lax.ppermute(value, axis, [(source, source + steps) for source in range(first, last)])


def rms_rows(values, gain):
    values = values.astype(jnp.float32)
    scale = lax.rsqrt(jnp.mean(values * values, axis=-1, keepdims=True) + epsilon)
    return values * scale * gain


def whole_ref(array):
    return pl.BlockSpec(array.shape, lambda *_: (0,) * array.ndim)


def contract(a, b, dims, precision=None):
    return lax.dot_general(
        a, b, (dims, ((), ())), precision=precision, preferred_element_type=f32
    )


def parts(values):
    high = values.astype(bf16)
    return high, (values - high.astype(f32)).astype(bf16)


def contract_close(a, b, dims):
    (a_high, a_low), (b_high, b_low) = parts(a), parts(b)
    return (
        contract(a_high, b_high, dims)
        + contract(a_high, b_low, dims)
        + contract(a_low, b_high, dims)
    )


def group_routes(weight_cols, picker, local_experts, slots):
    rows = weight_cols.shape[0]
    weight_rows = contract(picker, weight_cols, ((1,), (1,)))
    named = weight_rows > 0
    earlier = lax.broadcasted_iota(jnp.int32, (rows, rows), 0) < lax.broadcasted_iota(
        jnp.int32, (rows, rows), 1
    )
    rank = contract(
        jnp.where(named, 1.0, 0.0).astype(bf16),
        jnp.where(earlier, 1.0, 0.0).astype(bf16),
        ((1,), (0,)),
    )
    rank = jnp.where(named, rank, -1.0).astype(jnp.int32)
    slot = lax.broadcasted_iota(jnp.int32, (slots, rows), 0)
    picks, slot_weights = [], []
    for expert in range(local_experts):
        pick = jnp.where(slot == rank[expert : expert + 1], 1.0, 0.0)
        picks.append(pick)
        slot_weights.append(
            jnp.sum(pick * weight_rows[expert : expert + 1], axis=1, keepdims=True)
        )
    return jnp.concatenate(picks, axis=0).astype(bf16), slot_weights


def collect_kernel(rows_ref, picker_ref, out_ref):
    local_experts, slots, width = out_ref.shape
    picks, _ = group_routes(rows_ref[:, width:], picker_ref[...], local_experts, slots)
    taken = contract(picks, rows_ref[:, :width], ((1,), (0,)))
    out_ref[...] = taken.astype(bf16).reshape(out_ref.shape)


def spread_kernel(cols_ref, picker_ref, result_ref, out_ref):
    local_experts, slots, _ = result_ref.shape
    picks, slot_weights = group_routes(cols_ref[...], picker_ref[...], local_experts, slots)
    scaled = jnp.concatenate(
        [
            (result_ref[expert].astype(f32) * slot_weights[expert]).astype(bf16)
            for expert in range(local_experts)
        ],
        axis=0,
    )
    out_ref[...] = contract(picks, scaled, ((0,), (0,))).astype(bf16)


def expert_layer_gathered(
    stream, moe_gain, router, expert_ids, expert_gate, expert_up, expert_down, place, sources
):
    tok_rows, width = stream.shape
    local_experts = expert_gate.shape[0]
    experts_all = local_experts * sources
    normed = rms_rows(stream, moe_gain).astype(bf16)
    logits = jnp.dot(normed, router, preferred_element_type=f32)
    named = jnp.any(
        expert_ids[:, :, None] == jnp.arange(experts_all, dtype=jnp.int32)[None, None, :], axis=1
    )
    raised = jnp.where(named, jnp.exp(logits), 0.0)
    weights = raised / jnp.sum(raised, axis=1, keepdims=True)
    coarse = lax.reduce_precision(weights, 8, 7)
    fine = weights - coarse
    packet = jnp.concatenate([normed, coarse.astype(bf16), fine.astype(bf16)], axis=1)
    everything = lax.all_gather(packet, ("ctx", "head"), axis=0, tiled=True)

    tokens = tok_rows * sources
    groups = tokens // GROUP
    capacity = (11 * tok_rows * expert_ids.shape[1] + 10 * experts_all - 1) // (10 * experts_all)
    slots = -(-(capacity * (GROUP // tok_rows)) // 16) * 16
    column = jnp.arange(2 * experts_all, dtype=jnp.int32)[None, :] % experts_all
    line = jnp.arange(16, dtype=jnp.int32)[:, None]
    picker = ((line < local_experts) & (column == place * local_experts + line)).astype(bf16)
    collected = pl.pallas_call(
        collect_kernel,
        grid=(groups,),
        in_specs=[
            pl.BlockSpec((GROUP, packet.shape[1]), lambda g: (g, 0)),
            whole_ref(picker),
        ],
        out_specs=pl.BlockSpec((local_experts, slots, width), lambda g: (0, g, 0)),
        out_shape=jax.ShapeDtypeStruct((local_experts, slots * groups, width), bf16),
        compiler_params=pltpu.CompilerParams(vmem_limit_bytes=48 << 20),
        name="collect",
    )(everything, picker)
    gate_part = jnp.einsum("esd,edh->esh", collected, expert_gate, preferred_element_type=f32)
    up_part = jnp.einsum("esd,edh->esh", collected, expert_up, preferred_element_type=f32)
    hidden = (jax.nn.silu(gate_part) * up_part).astype(bf16)
    results = jnp.einsum("esh,ehd->esd", hidden, expert_down, preferred_element_type=f32).astype(
        bf16
    )
    partial = pl.pallas_call(
        spread_kernel,
        grid=(groups,),
        in_specs=[
            pl.BlockSpec(
                (GROUP, 2 * experts_all), lambda g: (g, width // (2 * experts_all))
            ),
            whole_ref(picker),
            pl.BlockSpec((local_experts, slots, width), lambda g: (0, g, 0)),
        ],
        out_specs=pl.BlockSpec((GROUP, width), lambda g: (g, 0)),
        out_shape=jax.ShapeDtypeStruct((tokens, width), bf16),
        compiler_params=pltpu.CompilerParams(vmem_limit_bytes=48 << 20),
        name="spread",
    )(everything, picker, results)
    return lax.psum_scatter(partial, ("ctx", "head"), scatter_dimension=0, tiled=True)


def expert_layer_sent(
    stream, moe_gain, router, expert_ids, expert_gate, expert_up, expert_down, sources
):
    tok_rows, model_width = stream.shape
    top_count = expert_ids.shape[1]
    local_experts = expert_gate.shape[0]
    experts_all = local_experts * sources
    capacity = (11 * tok_rows * top_count + 10 * experts_all - 1) // (10 * experts_all)
    normed = rms_rows(stream, moe_gain).astype(jnp.bfloat16)
    logits = jnp.dot(normed, router, preferred_element_type=jnp.float32)
    chosen = jnp.take_along_axis(logits, expert_ids, axis=1)
    raised = jnp.exp(chosen)
    weights = raised / jnp.sum(raised, axis=1, keepdims=True)
    flat_ids = expert_ids.reshape(-1)
    matches = (flat_ids[:, None] == jnp.arange(experts_all, dtype=jnp.int32)[None, :]).astype(
        jnp.int32
    )
    slot_index = jnp.sum((jnp.cumsum(matches, axis=0) - 1) * matches, axis=1)
    places = flat_ids * capacity + slot_index
    token_rows = jnp.arange(tok_rows * top_count, dtype=jnp.int32) // top_count
    outgoing = (
        jnp.zeros((experts_all * capacity, model_width), jnp.bfloat16)
        .at[places]
        .set(normed[token_rows])
    )
    outgoing = outgoing.reshape(sources, local_experts, capacity, model_width)
    received = lax.all_to_all(outgoing, ("ctx", "head"), split_axis=0, concat_axis=0, tiled=True)
    gate_part = jnp.einsum(
        "nesd,edh->nesh", received, expert_gate, preferred_element_type=jnp.float32
    )
    up_part = jnp.einsum("nesd,edh->nesh", received, expert_up, preferred_element_type=jnp.float32)
    hidden = (jax.nn.silu(gate_part) * up_part).astype(jnp.bfloat16)
    returned = lax.all_to_all(
        jnp.einsum(
            "nesh,ehd->nesd", hidden, expert_down, preferred_element_type=jnp.float32
        ).astype(jnp.bfloat16),
        ("ctx", "head"),
        split_axis=0,
        concat_axis=0,
        tiled=True,
    )
    gathered_rows = returned.reshape(experts_all * capacity, model_width)[places].reshape(
        tok_rows, top_count, model_width
    )
    return jnp.sum(weights[:, :, None] * gathered_rows.astype(jnp.float32), axis=1).astype(
        jnp.bfloat16
    )


def unit_inverse(strict_part):
    size = strict_part.shape[0]
    row = lax.broadcasted_iota(jnp.int32, (size, size), 0)
    col = lax.broadcasted_iota(jnp.int32, (size, size), 1)
    inverse = jnp.where(row == col, 1.0, 0.0)
    half = 1
    while half < size:
        joining = (row // (2 * half) == col // (2 * half)) & (row // half != col // half)
        corner = jnp.where(joining, strict_part, 0.0)
        if half == 1:
            inverse = inverse - corner
        else:
            step = contract_close(corner, inverse, ((1,), (0,)))
            inverse = inverse - contract_close(inverse, step, ((1,), (0,)))
        half *= 2
    return inverse


def unit_rows(rows):
    return rows * lax.rsqrt(jnp.sum(rows * rows, axis=-1, keepdims=True) + epsilon)


def delta_kernel(
    raw_ref,
    rim_ref,
    taps_ref,
    beta_ref,
    decay_ref,
    rate_ref,
    core_ref,
    reading_ref,
    moved_ref,
    extended,
    mixed,
    strengths,
    falls,
    carried,
    *,
    key_heads,
    chunk,
):
    rows, conv_cols = raw_ref.shape
    heads = moved_ref.shape[0]
    group = heads // key_heads
    tap_count = taps_ref.shape[0]
    rim = rim_ref.shape[0]
    extended[0:rim, :] = rim_ref[...]
    extended[rim : rim + rows, :] = raw_ref[...].astype(f32)
    key_at, value_at = key_heads * DK, 2 * key_heads * DK
    for start in range(0, rows, chunk):
        for first in range(0, conv_cols, DK):
            columns = slice(first, first + DK)
            summed = jnp.zeros((chunk, DK), f32)
            for tap in range(tap_count):
                offset = rim - (tap_count - 1) + start + tap
                summed += taps_ref[tap : tap + 1, columns] * extended[
                    offset : offset + chunk, columns
                ]
            value = summed / (1.0 + jnp.exp(-summed))
            if first < key_at:
                value = unit_rows(value) * DK**-0.5
            elif first < value_at:
                value = unit_rows(value)
            mixed[start : start + chunk, columns] = value
    beta = beta_ref[...]
    strengths[...] = 1.0 / (1.0 + jnp.exp(-beta))
    shifted = decay_ref[...] + rate_ref[1:2, :]
    softened = jnp.maximum(shifted, 0.0) + jnp.log1p(jnp.exp(-jnp.abs(shifted)))
    falls[...] = -jnp.exp(rate_ref[0:1, :]) * softened

    row = lax.broadcasted_iota(jnp.int32, (chunk, chunk), 0)
    col = lax.broadcasted_iota(jnp.int32, (chunk, chunk), 1)
    inclusive, strict = row >= col, row > col
    lower = jnp.where(inclusive, 1.0, 0.0)
    across = lax.broadcasted_iota(jnp.int32, (DK, 2 * DK), 1)
    down = lax.broadcasted_iota(jnp.int32, (DK, 2 * DK), 0)
    carried[...] = jnp.broadcast_to(
        jnp.where(across == down + DK, 1.0, 0.0)[None], carried.shape
    )

    def advance(step, nothing):
        here = pl.ds(pl.multiple_of(step * chunk, chunk), chunk)
        fall = falls[here, :]
        strength = strengths[here, :]
        cumulative = contract(lower, fall, ((1,), (0,)), lax.Precision.HIGHEST)
        cumulative_rows = contract(fall, lower, ((0,), (1,)), lax.Precision.HIGHEST)
        for key_head in range(key_heads):
            queries = mixed[here, key_head * DK : (key_head + 1) * DK]
            keys = mixed[here, key_at + key_head * DK : key_at + (key_head + 1) * DK]
            dots = contract_close(jnp.concatenate([keys, queries], axis=0), keys, ((1,), (1,)))
            for head in range(key_head * group, (key_head + 1) * group):
                values = mixed[here, value_at + head * DK : value_at + (head + 1) * DK]
                total = cumulative[:, head : head + 1]
                spread = total - cumulative_rows[head : head + 1, :]
                kept = jnp.where(inclusive, jnp.exp(jnp.where(inclusive, spread, 0.0)), 0.0)
                own = strength[:, head : head + 1]
                solver = unit_inverse(own * jnp.where(strict, kept, 0.0) * dots[:chunk])
                risen = jnp.exp(total)
                last = total[chunk - 1 :, :]
                solved = contract_close(
                    solver,
                    own * jnp.concatenate([values, risen * keys], axis=1),
                    ((1,), (0,)),
                )
                mixing = kept * dots[chunk:]
                state = carried[head]
                read = contract_close(
                    jnp.concatenate([solved[:, DK:], risen * queries], axis=0),
                    state,
                    ((1,), (0,)),
                )
                update = (
                    jnp.concatenate([solved[:, :DK], jnp.zeros((chunk, DK), f32)], axis=1)
                    - read[:chunk]
                )
                result = read[chunk:] + contract_close(mixing, update, ((1,), (0,)))
                core_ref[here, head * DK : (head + 1) * DK] = result[:, :DK]
                reading_ref[here, head * DK : (head + 1) * DK] = result[:, DK:]
                carried[head] = jnp.exp(last) * state + contract_close(
                    jnp.exp(last - total) * keys, update, ((0,), (0,)))
        return nothing

    lax.fori_loop(0, rows // chunk, advance, 0)
    moved_ref[...] = carried[...].astype(bf16)


def finish_kernel(
    place_ref, moved_ref, core_ref, reading_ref, gate_ref, gain_ref, weight_ref, out_ref, gated
):
    heads = moved_ref.shape[1]

    def join(earlier, states):
        return tuple(
            contract_close(moved_ref[earlier, head, :, DK:].astype(f32), state, ((1,), (0,)))
            + moved_ref[earlier, head, :, :DK].astype(f32)
            for head, state in enumerate(states)
        )

    states = lax.fori_loop(
        0, place_ref[0], join, tuple(jnp.zeros((DK, DK), f32) for _ in range(heads))
    )
    for head, state in enumerate(states):
        columns = slice(head * DK, (head + 1) * DK)
        core = core_ref[:, columns] + contract_close(
            reading_ref[:, columns], state, ((1,), (0,)))
        normal = (
            core
            * lax.rsqrt(jnp.mean(core * core, axis=-1, keepdims=True) + epsilon)
            * gain_ref[...]
        )
        gate = gate_ref[:, columns].astype(f32)
        gated[:, columns] = (normal * (gate / (1.0 + jnp.exp(-gate)))).astype(bf16)
    out_ref[...] = contract(gated[...], weight_ref[...], ((1,), (0,))).astype(bf16)


def on_device(
    stream,
    moe_gain,
    router,
    expert_ids,
    expert_gate,
    expert_up,
    expert_down,
    mixer_gain,
    query_weight,
    key_weight,
    value_weight,
    output_gate,
    beta_weight,
    decay_weight,
    query_conv,
    key_conv,
    value_conv,
    decay_log,
    decay_bias,
    head_gain,
    out_weight,
):
    ctx_count = lax.axis_size("ctx")
    head_count = lax.axis_size("head")
    sources = ctx_count * head_count
    ctx_place = lax.axis_index("ctx")
    experts = (stream, moe_gain, router, expert_ids, expert_gate, expert_up, expert_down)
    if 2 * sources * stream.size <= GATHER_LIMIT:
        place = ctx_place * head_count + lax.axis_index("head")
        moe_out = expert_layer_gathered(*experts, place, sources)
    else:
        moe_out = expert_layer_sent(*experts, sources)
    mixer_in = rms_rows(
        stream.astype(jnp.float32) + moe_out.astype(jnp.float32), mixer_gain
    ).astype(jnp.bfloat16)
    piece_rows = lax.all_gather(mixer_in, "head", axis=0, tiled=True)

    def project(*matrices):
        return jnp.concatenate(
            [jnp.dot(piece_rows, matrix, preferred_element_type=f32) for matrix in matrices], axis=1
        )

    qkv_raw = project(query_weight, key_weight, value_weight).astype(bf16)
    gate_raw = project(output_gate).astype(bf16)
    beta_raw = project(beta_weight)
    decay_raw = project(decay_weight)
    rows, conv_cols = qkv_raw.shape
    key_heads = query_weight.shape[1] // DK
    heads = beta_weight.shape[1]
    value_cols = value_weight.shape[1]
    taps = jnp.concatenate([query_conv, key_conv, value_conv], axis=1)
    rim_len = taps.shape[0] - 1
    rim = passed_along(qkv_raw[rows - rim_len :], "ctx", 1)
    rim = jnp.concatenate([jnp.zeros((8 - rim_len, conv_cols), f32), rim.astype(f32)], axis=0)
    rates = jnp.stack([decay_log, decay_bias])
    chunk = math.gcd(rows, CHUNK)
    core, reading, moved = pl.pallas_call(
        functools.partial(delta_kernel, key_heads=key_heads, chunk=chunk),
        out_shape=(
            jax.ShapeDtypeStruct((rows, value_cols), f32),
            jax.ShapeDtypeStruct((rows, value_cols), f32),
            jax.ShapeDtypeStruct((heads, DK, 2 * DK), bf16),
        ),
        scratch_shapes=[
            pltpu.VMEM((rows + 8, conv_cols), f32),
            pltpu.VMEM((rows, conv_cols), f32),
            pltpu.VMEM((rows, heads), f32),
            pltpu.VMEM((rows, heads), f32),
            pltpu.VMEM((heads, DK, 2 * DK), f32),
        ],
        compiler_params=pltpu.CompilerParams(vmem_limit_bytes=48 << 20),
        name="delta",
    )(qkv_raw, rim, taps, beta_raw, decay_raw, rates)
    everything = lax.all_gather(moved, "ctx")
    in_vmem = pl.BlockSpec(memory_space=pltpu.VMEM)
    partial = pl.pallas_call(
        finish_kernel,
        in_specs=[pl.BlockSpec(memory_space=pltpu.SMEM)] + [in_vmem] * 6,
        out_shape=jax.ShapeDtypeStruct((rows, out_weight.shape[1]), bf16),
        scratch_shapes=[pltpu.VMEM((rows, value_cols), bf16)],
        compiler_params=pltpu.CompilerParams(vmem_limit_bytes=48 << 20),
        name="finish",
    )(
        ctx_place.reshape(1),
        everything,
        core,
        reading,
        gate_raw,
        head_gain.reshape(1, -1),
        out_weight,
    )
    mixer_out = lax.psum_scatter(partial, "head", scatter_dimension=0, tiled=True)
    return (moe_out, mixer_out)


def solution(mesh):
    return jax.shard_map(
        on_device,
        mesh=mesh,
        in_specs=(
            P(("ctx", "head"), None),
            P(),
            P(),
            P(("ctx", "head"), None),
            P(("ctx", "head"), None, None),
            P(("ctx", "head"), None, None),
            P(("ctx", "head"), None, None),
            P(),
            P(None, "head"),
            P(None, "head"),
            P(None, "head"),
            P(None, "head"),
            P(None, "head"),
            P(None, "head"),
            P(None, "head"),
            P(None, "head"),
            P(None, "head"),
            P("head"),
            P("head"),
            P(),
            P("head", None),
        ),
        out_specs=(P(("ctx", "head"), None), P(("ctx", "head"), None)),
        check_vma=False,
    )
```

```python
import functools
import math

import jax
import jax.numpy as jnp
from jax import lax
from jax.experimental import pallas as pl
from jax.experimental.pallas import tpu as pltpu
from jax.sharding import PartitionSpec as P

DK = 128
CHUNK = 128
GROUP = 256
GATHER_LIMIT = 32 << 20


epsilon = 1e-06
f32 = jnp.float32
bf16 = jnp.bfloat16


def passed_along(value, axis, steps):
    count = lax.axis_size(axis)
    first, last = (max(0, -steps), min(count, count - steps))
    return lax.ppermute(value, axis, [(source, source + steps) for source in range(first, last)])


def rms_rows(values, gain):
    values = values.astype(jnp.float32)
    scale = lax.rsqrt(jnp.mean(values * values, axis=-1, keepdims=True) + epsilon)
    return values * scale * gain


def whole_ref(array):
    return pl.BlockSpec(array.shape, lambda *_: (0,) * array.ndim)


def contract(a, b, dims, precision=None):
    return lax.dot_general(
        a, b, (dims, ((), ())), precision=precision, preferred_element_type=f32
    )


def parts(values):
    high = values.astype(bf16)
    return high, (values - high.astype(f32)).astype(bf16)


def contract_close(a, b, dims):
    (a_high, a_low), (b_high, b_low) = parts(a), parts(b)
    return (
        contract(a_high, b_high, dims)
        + contract(a_high, b_low, dims)
        + contract(a_low, b_high, dims)
    )


def collect_kernel(rows_ref, picker_ref, *out_refs, tok_rows, slots):
    width = out_refs[0].shape[1]
    rows = rows_ref.shape[0]
    blocks = rows // tok_rows
    weight_rows = contract(picker_ref[...], rows_ref[:, width:], ((1,), (1,)))
    named = weight_rows > 0
    before = lax.broadcasted_iota(jnp.int32, (rows, rows), 0)
    after = lax.broadcasted_iota(jnp.int32, (rows, rows), 1)
    earlier = (before < after) & (before // tok_rows == after // tok_rows)
    rank = contract(
        jnp.where(named, 1.0, 0.0).astype(bf16),
        jnp.where(earlier, 1.0, 0.0).astype(bf16),
        ((1,), (0,)),
    )
    rank = jnp.where(named, rank, -1.0).astype(jnp.int32)
    slot = lax.broadcasted_iota(jnp.int32, (blocks * slots, rows), 0)
    block = lax.broadcasted_iota(jnp.int32, (blocks * slots, rows), 1) // tok_rows
    picks = [
        jnp.where(
            (slot - block * slots == rank[expert : expert + 1]) & (slot // slots == block), 1.0, 0.0
        )
        for expert in range(len(out_refs))
    ]
    taken = contract(
        jnp.concatenate(picks, axis=0).astype(bf16), rows_ref[:, :width], ((1,), (0,))
    )
    for expert, out_ref in enumerate(out_refs):
        out_ref[...] = taken[expert * blocks * slots : (expert + 1) * blocks * slots].astype(bf16)


def expert_kernel(core_ref, own_ref, other_ref, gate_ref, up_ref, down_ref, out_ref):
    def apply(rows_ref):
        rows = rows_ref[...]
        gate = contract(rows, gate_ref[0], ((1,), (0,)))
        up = contract(rows, up_ref[0], ((1,), (0,)))
        hidden = (gate / (1.0 + jnp.exp(-gate)) * up).astype(bf16)
        out_ref[...] = contract(hidden, down_ref[0], ((1,), (0,))).astype(bf16)

    pl.when(pl.program_id(0) == 0)(lambda: apply(own_ref))
    pl.when(pl.program_id(0) == 1)(lambda: apply(other_ref))


def combine_kernel(
    stream_ref, weights_ref, gain_ref, *refs, sources, slots
):
    *result_refs, moe_ref, mixer_ref = refs
    tok_rows, experts_all = weights_ref.shape
    local_experts = len(result_refs)
    weights = weights_ref[...]
    named = jnp.where(weights > 0, 1.0, 0.0)
    before = lax.broadcasted_iota(jnp.int32, (tok_rows, tok_rows), 1)
    after = lax.broadcasted_iota(jnp.int32, (tok_rows, tok_rows), 0)
    rank = contract(
        jnp.where(before < after, 1.0, 0.0).astype(bf16), named.astype(bf16), ((1,), (0,))
    )
    rank = jnp.where(named > 0, rank, -1.0).astype(bf16)
    high, low = parts(weights)
    column = lax.broadcasted_iota(jnp.int32, (experts_all, sources * slots), 1)
    line = lax.broadcasted_iota(jnp.int32, (experts_all, sources * slots), 0)
    half = sources // 2
    origin = column // slots
    origin = 2 * (origin % half) + origin // half
    slot = lax.broadcasted_iota(jnp.int32, (tok_rows, sources * slots), 1) % slots
    summed = jnp.zeros(moe_ref.shape, f32)
    for expert, result_ref in enumerate(result_refs):
        widen = jnp.where(line == origin * local_experts + expert, 1.0, 0.0).astype(bf16)
        chosen = contract(rank, widen, ((1,), (0,))).astype(jnp.int32) == slot
        for part in (high, low):
            spread = jnp.where(chosen, contract(part, widen, ((1,), (0,))), 0.0).astype(bf16)
            summed += contract(spread, result_ref[...], ((1,), (0,)))
    moe = summed.astype(bf16)
    moe_ref[...] = moe
    total = stream_ref[...].astype(f32) + moe.astype(f32)
    scale = lax.rsqrt(jnp.mean(total * total, axis=-1, keepdims=True) + epsilon)
    mixer_ref[...] = (total * scale * gain_ref[...]).astype(bf16)


def expert_layer_gathered(
    stream,
    moe_gain,
    router,
    expert_ids,
    expert_gate,
    expert_up,
    expert_down,
    mixer_gain,
    sources,
    head_count,
):
    tok_rows, width = stream.shape
    local_experts, _, hidden_width = expert_gate.shape
    experts_all = local_experts * sources
    half = sources // 2
    head = lax.axis_index("head")
    core = head % 2
    place = lax.axis_index("ctx") * head_count + head
    normed = rms_rows(stream, moe_gain).astype(bf16)
    logits = jnp.dot(normed, router, preferred_element_type=f32)
    named = jnp.any(
        expert_ids[:, :, None] == jnp.arange(experts_all, dtype=jnp.int32)[None, None, :], axis=1
    )
    raised = jnp.where(named, jnp.exp(logits), 0.0)
    weights = raised / jnp.sum(raised, axis=1, keepdims=True)
    coarse = lax.reduce_precision(weights, 8, 7)
    fine = lax.reduce_precision(weights - coarse, 8, 7)
    weights = coarse + fine
    packet = jnp.concatenate([normed, coarse.astype(bf16), fine.astype(bf16)], axis=1)
    same_core = [[2 * chip + side for chip in range(half)] for side in range(2)]
    own = lax.all_gather(
        packet, ("ctx", "head"), axis=0, tiled=True, axis_index_groups=same_core
    )
    other = lax.ppermute(own, "head", [(source, source ^ 1) for source in range(head_count)])

    capacity = (11 * tok_rows * expert_ids.shape[1] + 10 * experts_all - 1) // (10 * experts_all)
    slots = -(-capacity // 8) * 8
    column = jnp.arange(2 * experts_all, dtype=jnp.int32)[None, :] % experts_all
    line = jnp.arange(16, dtype=jnp.int32)[:, None]
    picker = ((line < local_experts) & (column == place * local_experts + line)).astype(bf16)
    groups = half * tok_rows // GROUP
    taken = GROUP // tok_rows * slots

    def collect(rows):
        return pl.pallas_call(
            functools.partial(collect_kernel, tok_rows=tok_rows, slots=slots),
            grid=(groups,),
            in_specs=[
                pl.BlockSpec((GROUP, packet.shape[1]), lambda g: (g, 0)),
                whole_ref(picker),
            ],
            out_specs=[pl.BlockSpec((taken, width), lambda g: (g, 0))] * local_experts,
            out_shape=[jax.ShapeDtypeStruct((taken * groups, width), bf16)] * local_experts,
            compiler_params=pltpu.CompilerParams(vmem_limit_bytes=48 << 20),
            name="collect",
        )(rows, picker)

    own_rows, other_rows = collect(own), collect(other)
    order = [sum(same_core, [])]
    returned = []
    for expert in range(local_experts):
        here = lambda j, core_ref, expert=expert: (expert, 0, 0)
        results = pl.pallas_call(
            expert_kernel,
            grid_spec=pltpu.PrefetchScalarGridSpec(
                num_scalar_prefetch=1,
                grid=(2,),
                in_specs=[
                    whole_ref(own_rows[expert]),
                    whole_ref(other_rows[expert]),
                    pl.BlockSpec((1, width, hidden_width), here),
                    pl.BlockSpec((1, width, hidden_width), here),
                    pl.BlockSpec((1, hidden_width, width), here),
                ],
                out_specs=pl.BlockSpec(
                    (taken * groups, width), lambda j, core_ref: (core_ref[0] ^ j, 0)
                ),
            ),
            out_shape=jax.ShapeDtypeStruct((2 * taken * groups, width), bf16),
            compiler_params=pltpu.CompilerParams(vmem_limit_bytes=48 << 20),
            name="experts",
        )(core.reshape(1), own_rows[expert], other_rows[expert], expert_gate, expert_up, expert_down)
        returned.append(
            lax.all_to_all(
                results.reshape(sources, slots, width),
                ("ctx", "head"),
                split_axis=0,
                concat_axis=0,
                tiled=True,
                axis_index_groups=order,
            ).reshape(sources * slots, width)
        )
    in_vmem = pl.BlockSpec(memory_space=pltpu.VMEM)
    return pl.pallas_call(
        functools.partial(combine_kernel, sources=sources, slots=slots),
        in_specs=[in_vmem] * (3 + local_experts),
        out_shape=[jax.ShapeDtypeStruct(stream.shape, bf16)] * 2,
        compiler_params=pltpu.CompilerParams(vmem_limit_bytes=48 << 20),
        name="combine",
    )(stream, weights, mixer_gain.reshape(1, -1), *returned)


def expert_layer_sent(
    stream, moe_gain, router, expert_ids, expert_gate, expert_up, expert_down, sources
):
    tok_rows, model_width = stream.shape
    top_count = expert_ids.shape[1]
    local_experts = expert_gate.shape[0]
    experts_all = local_experts * sources
    capacity = (11 * tok_rows * top_count + 10 * experts_all - 1) // (10 * experts_all)
    normed = rms_rows(stream, moe_gain).astype(jnp.bfloat16)
    logits = jnp.dot(normed, router, preferred_element_type=jnp.float32)
    chosen = jnp.take_along_axis(logits, expert_ids, axis=1)
    raised = jnp.exp(chosen)
    weights = raised / jnp.sum(raised, axis=1, keepdims=True)
    flat_ids = expert_ids.reshape(-1)
    matches = (flat_ids[:, None] == jnp.arange(experts_all, dtype=jnp.int32)[None, :]).astype(
        jnp.int32
    )
    slot_index = jnp.sum((jnp.cumsum(matches, axis=0) - 1) * matches, axis=1)
    places = flat_ids * capacity + slot_index
    token_rows = jnp.arange(tok_rows * top_count, dtype=jnp.int32) // top_count
    outgoing = (
        jnp.zeros((experts_all * capacity, model_width), jnp.bfloat16)
        .at[places]
        .set(normed[token_rows])
    )
    outgoing = outgoing.reshape(sources, local_experts, capacity, model_width)
    received = lax.all_to_all(outgoing, ("ctx", "head"), split_axis=0, concat_axis=0, tiled=True)
    gate_part = jnp.einsum(
        "nesd,edh->nesh", received, expert_gate, preferred_element_type=jnp.float32
    )
    up_part = jnp.einsum("nesd,edh->nesh", received, expert_up, preferred_element_type=jnp.float32)
    hidden = (jax.nn.silu(gate_part) * up_part).astype(jnp.bfloat16)
    returned = lax.all_to_all(
        jnp.einsum(
            "nesh,ehd->nesd", hidden, expert_down, preferred_element_type=jnp.float32
        ).astype(jnp.bfloat16),
        ("ctx", "head"),
        split_axis=0,
        concat_axis=0,
        tiled=True,
    )
    gathered_rows = returned.reshape(experts_all * capacity, model_width)[places].reshape(
        tok_rows, top_count, model_width
    )
    return jnp.sum(weights[:, :, None] * gathered_rows.astype(jnp.float32), axis=1).astype(
        jnp.bfloat16
    )


def unit_inverse(strict_part):
    size = strict_part.shape[0]
    row = lax.broadcasted_iota(jnp.int32, (size, size), 0)
    col = lax.broadcasted_iota(jnp.int32, (size, size), 1)
    inverse = jnp.where(row == col, 1.0, 0.0)
    half = 1
    while half < size:
        joining = (row // (2 * half) == col // (2 * half)) & (row // half != col // half)
        corner = jnp.where(joining, strict_part, 0.0)
        if half == 1:
            inverse = inverse - corner
        else:
            step = contract_close(corner, inverse, ((1,), (0,)))
            inverse = inverse - contract_close(inverse, step, ((1,), (0,)))
        half *= 2
    return inverse


def unit_rows(rows):
    return rows * lax.rsqrt(jnp.sum(rows * rows, axis=-1, keepdims=True) + epsilon)


def delta_kernel(
    raw_ref,
    rim_ref,
    taps_ref,
    beta_ref,
    decay_ref,
    rate_ref,
    core_ref,
    reading_ref,
    moved_ref,
    extended,
    mixed,
    strengths,
    falls,
    carried,
    *,
    key_heads,
    chunk,
):
    rows, conv_cols = raw_ref.shape
    heads = moved_ref.shape[0]
    group = heads // key_heads
    tap_count = taps_ref.shape[0]
    rim = rim_ref.shape[0]
    extended[0:rim, :] = rim_ref[...]
    extended[rim : rim + rows, :] = raw_ref[...].astype(f32)
    key_at, value_at = key_heads * DK, 2 * key_heads * DK
    for start in range(0, rows, chunk):
        for first in range(0, conv_cols, DK):
            columns = slice(first, first + DK)
            summed = jnp.zeros((chunk, DK), f32)
            for tap in range(tap_count):
                offset = rim - (tap_count - 1) + start + tap
                summed += taps_ref[tap : tap + 1, columns] * extended[
                    offset : offset + chunk, columns
                ]
            value = summed / (1.0 + jnp.exp(-summed))
            if first < key_at:
                value = unit_rows(value) * DK**-0.5
            elif first < value_at:
                value = unit_rows(value)
            mixed[start : start + chunk, columns] = value
    beta = beta_ref[...]
    strengths[...] = 1.0 / (1.0 + jnp.exp(-beta))
    shifted = decay_ref[...] + rate_ref[1:2, :]
    softened = jnp.maximum(shifted, 0.0) + jnp.log1p(jnp.exp(-jnp.abs(shifted)))
    falls[...] = -jnp.exp(rate_ref[0:1, :]) * softened

    row = lax.broadcasted_iota(jnp.int32, (chunk, chunk), 0)
    col = lax.broadcasted_iota(jnp.int32, (chunk, chunk), 1)
    inclusive, strict = row >= col, row > col
    lower = jnp.where(inclusive, 1.0, 0.0)
    across = lax.broadcasted_iota(jnp.int32, (DK, 2 * DK), 1)
    down = lax.broadcasted_iota(jnp.int32, (DK, 2 * DK), 0)
    carried[...] = jnp.broadcast_to(
        jnp.where(across == down + DK, 1.0, 0.0)[None], carried.shape
    )

    def advance(step, nothing):
        here = pl.ds(pl.multiple_of(step * chunk, chunk), chunk)
        fall = falls[here, :]
        strength = strengths[here, :]
        cumulative = contract(lower, fall, ((1,), (0,)), lax.Precision.HIGHEST)
        cumulative_rows = contract(fall, lower, ((0,), (1,)), lax.Precision.HIGHEST)
        for key_head in range(key_heads):
            queries = mixed[here, key_head * DK : (key_head + 1) * DK]
            keys = mixed[here, key_at + key_head * DK : key_at + (key_head + 1) * DK]
            dots = contract_close(jnp.concatenate([keys, queries], axis=0), keys, ((1,), (1,)))
            for head in range(key_head * group, (key_head + 1) * group):
                values = mixed[here, value_at + head * DK : value_at + (head + 1) * DK]
                total = cumulative[:, head : head + 1]
                spread = total - cumulative_rows[head : head + 1, :]
                kept = jnp.where(inclusive, jnp.exp(jnp.where(inclusive, spread, 0.0)), 0.0)
                own = strength[:, head : head + 1]
                solver = unit_inverse(own * jnp.where(strict, kept, 0.0) * dots[:chunk])
                risen = jnp.exp(total)
                last = total[chunk - 1 :, :]
                solved = contract_close(
                    solver,
                    own * jnp.concatenate([values, risen * keys], axis=1),
                    ((1,), (0,)),
                )
                mixing = kept * dots[chunk:]
                state = carried[head]
                read = contract_close(
                    jnp.concatenate([solved[:, DK:], risen * queries], axis=0),
                    state,
                    ((1,), (0,)),
                )
                update = (
                    jnp.concatenate([solved[:, :DK], jnp.zeros((chunk, DK), f32)], axis=1)
                    - read[:chunk]
                )
                result = read[chunk:] + contract_close(mixing, update, ((1,), (0,)))
                core_ref[here, head * DK : (head + 1) * DK] = result[:, :DK]
                reading_ref[here, head * DK : (head + 1) * DK] = result[:, DK:]
                carried[head] = jnp.exp(last) * state + contract_close(
                    jnp.exp(last - total) * keys, update, ((0,), (0,)))
        return nothing

    lax.fori_loop(0, rows // chunk, advance, 0)
    moved_ref[...] = carried[...].astype(bf16)


def finish_kernel(
    place_ref, moved_ref, core_ref, reading_ref, gate_ref, gain_ref, weight_ref, out_ref, gated
):
    heads = moved_ref.shape[1]

    def join(earlier, states):
        return tuple(
            contract_close(moved_ref[earlier, head, :, DK:].astype(f32), state, ((1,), (0,)))
            + moved_ref[earlier, head, :, :DK].astype(f32)
            for head, state in enumerate(states)
        )

    states = lax.fori_loop(
        0, place_ref[0], join, tuple(jnp.zeros((DK, DK), f32) for _ in range(heads))
    )
    for head, state in enumerate(states):
        columns = slice(head * DK, (head + 1) * DK)
        core = core_ref[:, columns] + contract_close(
            reading_ref[:, columns], state, ((1,), (0,)))
        normal = (
            core
            * lax.rsqrt(jnp.mean(core * core, axis=-1, keepdims=True) + epsilon)
            * gain_ref[...]
        )
        gate = gate_ref[:, columns].astype(f32)
        gated[:, columns] = (normal * (gate / (1.0 + jnp.exp(-gate)))).astype(bf16)
    out_ref[...] = contract(gated[...], weight_ref[...], ((1,), (0,))).astype(bf16)


def on_device(
    stream,
    moe_gain,
    router,
    expert_ids,
    expert_gate,
    expert_up,
    expert_down,
    mixer_gain,
    query_weight,
    key_weight,
    value_weight,
    output_gate,
    beta_weight,
    decay_weight,
    query_conv,
    key_conv,
    value_conv,
    decay_log,
    decay_bias,
    head_gain,
    out_weight,
):
    ctx_count = lax.axis_size("ctx")
    head_count = lax.axis_size("head")
    sources = ctx_count * head_count
    ctx_place = lax.axis_index("ctx")
    experts = (stream, moe_gain, router, expert_ids, expert_gate, expert_up, expert_down)
    if 2 * sources * stream.size <= GATHER_LIMIT:
        moe_out, mixer_in = expert_layer_gathered(*experts, mixer_gain, sources, head_count)
    else:
        moe_out = expert_layer_sent(*experts, sources)
        mixer_in = rms_rows(
            stream.astype(jnp.float32) + moe_out.astype(jnp.float32), mixer_gain
        ).astype(jnp.bfloat16)
    piece_rows = lax.all_gather(mixer_in, "head", axis=0, tiled=True)

    def project(*matrices):
        return jnp.concatenate(
            [jnp.dot(piece_rows, matrix, preferred_element_type=f32) for matrix in matrices], axis=1
        )

    qkv_raw = project(query_weight, key_weight, value_weight).astype(bf16)
    gate_raw = project(output_gate).astype(bf16)
    beta_raw = project(beta_weight)
    decay_raw = project(decay_weight)
    rows, conv_cols = qkv_raw.shape
    key_heads = query_weight.shape[1] // DK
    heads = beta_weight.shape[1]
    value_cols = value_weight.shape[1]
    taps = jnp.concatenate([query_conv, key_conv, value_conv], axis=1)
    rim_len = taps.shape[0] - 1
    rim = passed_along(qkv_raw[rows - rim_len :], "ctx", 1)
    rim = jnp.concatenate([jnp.zeros((8 - rim_len, conv_cols), f32), rim.astype(f32)], axis=0)
    rates = jnp.stack([decay_log, decay_bias])
    chunk = math.gcd(rows, CHUNK)
    core, reading, moved = pl.pallas_call(
        functools.partial(delta_kernel, key_heads=key_heads, chunk=chunk),
        out_shape=(
            jax.ShapeDtypeStruct((rows, value_cols), f32),
            jax.ShapeDtypeStruct((rows, value_cols), f32),
            jax.ShapeDtypeStruct((heads, DK, 2 * DK), bf16),
        ),
        scratch_shapes=[
            pltpu.VMEM((rows + 8, conv_cols), f32),
            pltpu.VMEM((rows, conv_cols), f32),
            pltpu.VMEM((rows, heads), f32),
            pltpu.VMEM((rows, heads), f32),
            pltpu.VMEM((heads, DK, 2 * DK), f32),
        ],
        compiler_params=pltpu.CompilerParams(vmem_limit_bytes=48 << 20),
        name="delta",
    )(qkv_raw, rim, taps, beta_raw, decay_raw, rates)
    everything = lax.all_gather(moved, "ctx")
    in_vmem = pl.BlockSpec(memory_space=pltpu.VMEM)
    partial = pl.pallas_call(
        finish_kernel,
        in_specs=[pl.BlockSpec(memory_space=pltpu.SMEM)] + [in_vmem] * 6,
        out_shape=jax.ShapeDtypeStruct((rows, out_weight.shape[1]), bf16),
        scratch_shapes=[pltpu.VMEM((rows, value_cols), bf16)],
        compiler_params=pltpu.CompilerParams(vmem_limit_bytes=48 << 20),
        name="finish",
    )(
        ctx_place.reshape(1),
        everything,
        core,
        reading,
        gate_raw,
        head_gain.reshape(1, -1),
        out_weight,
    )
    mixer_out = lax.psum_scatter(partial, "head", scatter_dimension=0, tiled=True)
    return (moe_out, mixer_out)


def solution(mesh):
    return jax.shard_map(
        on_device,
        mesh=mesh,
        in_specs=(
            P(("ctx", "head"), None),
            P(),
            P(),
            P(("ctx", "head"), None),
            P(("ctx", "head"), None, None),
            P(("ctx", "head"), None, None),
            P(("ctx", "head"), None, None),
            P(),
            P(None, "head"),
            P(None, "head"),
            P(None, "head"),
            P(None, "head"),
            P(None, "head"),
            P(None, "head"),
            P(None, "head"),
            P(None, "head"),
            P(None, "head"),
            P("head"),
            P("head"),
            P(),
            P("head", None),
        ),
        out_specs=(P(("ctx", "head"), None), P(("ctx", "head"), None)),
        check_vma=False,
    )
```

```python
import functools
import math

import jax
import jax.numpy as jnp
from jax import lax
from jax.experimental import pallas as pl
from jax.experimental.pallas import tpu as pltpu
from jax.sharding import PartitionSpec as P

DK = 128
CHUNK = 128
GATHER_LIMIT = 32 << 20


epsilon = 1e-06
f32 = jnp.float32
bf16 = jnp.bfloat16


def passed_along(value, axis, steps):
    count = lax.axis_size(axis)
    first, last = (max(0, -steps), min(count, count - steps))
    return lax.ppermute(value, axis, [(source, source + steps) for source in range(first, last)])


def rms_rows(values, gain):
    values = values.astype(jnp.float32)
    scale = lax.rsqrt(jnp.mean(values * values, axis=-1, keepdims=True) + epsilon)
    return values * scale * gain


def whole_ref(array):
    return pl.BlockSpec(array.shape, lambda *_: (0,) * array.ndim)


def contract(a, b, dims, precision=None):
    return lax.dot_general(
        a, b, (dims, ((), ())), precision=precision, preferred_element_type=f32
    )


def parts(values):
    high = values.astype(bf16)
    return high, (values - high.astype(f32)).astype(bf16)


def contract_close(a, b, dims):
    (a_high, a_low), (b_high, b_low) = parts(a), parts(b)
    return (
        contract(a_high, b_high, dims)
        + contract(a_high, b_low, dims)
        + contract(a_low, b_high, dims)
    )


def pair_routes(cols, picker, lines, tok_rows, slots):
    rows = cols.shape[0]
    weight_rows = contract(picker, cols, ((1,), (1,)))
    named = weight_rows > 0
    before = lax.broadcasted_iota(jnp.int32, (rows, rows), 0)
    after = lax.broadcasted_iota(jnp.int32, (rows, rows), 1)
    earlier = (before < after) & (before // tok_rows == after // tok_rows)
    rank = contract(
        jnp.where(named, 1.0, 0.0).astype(bf16),
        jnp.where(earlier, 1.0, 0.0).astype(bf16),
        ((1,), (0,)),
    )
    first_slot = lax.broadcasted_iota(jnp.int32, rank.shape, 1) // tok_rows * slots
    rank = jnp.where(named, rank.astype(jnp.int32) + first_slot, -1)
    slot = lax.broadcasted_iota(jnp.int32, (rows // tok_rows * slots, rows), 0)
    picks = [jnp.where(slot == rank[line : line + 1], 1.0, 0.0) for line in range(lines)]
    return weight_rows, picks


def collect_kernel(block_00, block_10, block_01, block_11, picker_ref, own_ref, send_ref, *, slots):
    local_experts, taken, width = own_ref.shape
    tok_rows = block_00.shape[0]
    pair = taken // 2
    for at, pair_refs in enumerate(((block_01, block_11), (block_00, block_10))):
        rows = jnp.concatenate([ref[...] for ref in pair_refs], axis=0)
        _, picks = pair_routes(
            rows[:, width:], picker_ref[...], 2 * local_experts, tok_rows, slots
        )
        picked = contract(
            jnp.concatenate(picks, axis=0).astype(bf16), rows[:, :width], ((1,), (0,))
        ).astype(bf16)
        for expert in range(local_experts):
            there = slice(at * pair, (at + 1) * pair)
            own_ref[expert, there, :] = picked[expert * pair : (expert + 1) * pair]
            line = local_experts + expert
            send_ref[expert, there, :] = picked[line * pair : (line + 1) * pair]


def expert_kernel(*refs):
    *row_refs, gate_ref, up_ref, down_ref, own_ref, send_ref = refs
    half = len(row_refs) // 2
    for sources, out_ref in ((row_refs[half:], send_ref), (row_refs[:half], own_ref)):
        rows = jnp.concatenate([ref[0] for ref in sources], axis=0)
        gate = contract(rows, gate_ref[0], ((1,), (0,)))
        up = contract(rows, up_ref[0], ((1,), (0,)))
        hidden = (gate / (1.0 + jnp.exp(-gate)) * up).astype(bf16)
        out_ref[0] = contract(hidden, down_ref[0], ((1,), (0,))).astype(bf16)


def spread_kernel(
    cols_00, cols_10, cols_01, cols_11, picker_ref, own_ref, got_ref, far_ref, near_ref, here_ref, *, slots
):
    local_experts, taken, _ = own_ref.shape
    tok_rows = cols_00.shape[0]
    pair = taken // 2
    for at, pair_refs in enumerate(((cols_01, cols_11), (cols_00, cols_10))):
        cols = jnp.concatenate([ref[...] for ref in pair_refs], axis=0)
        weight_rows, picks = pair_routes(
            cols, picker_ref[...], 2 * local_experts, tok_rows, slots
        )
        scaled = []
        for line, pick in enumerate(picks):
            result_ref = (own_ref, got_ref)[line // local_experts]
            result = result_ref[line % local_experts, at * pair : (at + 1) * pair, :]
            weight = jnp.sum(pick * weight_rows[line : line + 1], axis=1, keepdims=True)
            scaled.append((result.astype(f32) * weight).astype(bf16))
        summed = contract(
            jnp.concatenate(picks, axis=0).astype(bf16),
            jnp.concatenate(scaled, axis=0),
            ((0,), (0,)),
        ).astype(bf16)
        if at == 0:
            far_ref[...] = summed
        else:
            here_ref[...] = summed[:tok_rows]
            near_ref[...] = summed[tok_rows:]


def expert_layer_gathered(
    stream,
    moe_gain,
    router,
    expert_ids,
    expert_gate,
    expert_up,
    expert_down,
    sources,
):
    tok_rows, width = stream.shape
    local_experts, _, hidden_width = expert_gate.shape
    experts_all = local_experts * sources
    depth = sources // 8
    place = lax.axis_index(("ctx", "head"))

    def sent(value, move):
        pairs = []
        for device in range(sources):
            z, y, x, core = device // 8, device // 4 % 2, device // 2 % 2, device % 2
            z, y, x, core = move(z, y, x, core)
            pairs.append((device, ((z * 2 + y) * 2 + x) * 2 + core))
        return lax.ppermute(value, ("ctx", "head"), pairs)

    def lifted(value, steps):
        return sent(value, lambda z, y, x, core: ((z + steps) % depth, y, x, core))

    def first(value):
        return sent(value, lambda z, y, x, core: (z, y ^ (1 - core), x ^ core, core))

    def second(value):
        return sent(value, lambda z, y, x, core: (z, y ^ core, x ^ (1 - core), core))

    def swapped(value):
        return sent(value, lambda z, y, x, core: (z, y, x, 1 - core))

    normed = rms_rows(stream, moe_gain).astype(bf16)
    logits = jnp.dot(normed, router, preferred_element_type=f32)
    named = jnp.any(
        expert_ids[:, :, None] == jnp.arange(experts_all, dtype=jnp.int32)[None, None, :], axis=1
    )
    raised = jnp.where(named, jnp.exp(logits), 0.0)
    weights = raised / jnp.sum(raised, axis=1, keepdims=True)
    coarse = lax.reduce_precision(weights, 8, 7)
    packet = jnp.concatenate(
        [normed, coarse.astype(bf16), (weights - coarse).astype(bf16)], axis=1
    )

    capacity = (11 * tok_rows * expert_ids.shape[1] + 10 * experts_all - 1) // (10 * experts_all)
    slots = -(-capacity // 8) * 8
    taken = 4 * slots
    column = jnp.arange(2 * experts_all, dtype=jnp.int32)[None, :] % experts_all
    line = jnp.arange(16, dtype=jnp.int32)[:, None]
    owner = jnp.where(line < local_experts, place, place ^ 1)
    picker = (
        (line < 2 * local_experts) & (column == owner * local_experts + line % local_experts)
    ).astype(bf16)

    lines = [packet] + [lifted(packet, steps) for steps in range(1, depth)]
    blocks, own_rows, got_rows = [], [], []
    for mine in lines:
        near = first(mine)
        blocks.append((mine, near, second(mine), second(near)))
    for four in blocks:
        own, send = pl.pallas_call(
            functools.partial(collect_kernel, slots=slots),
            out_shape=[jax.ShapeDtypeStruct((local_experts, taken, width), bf16)] * 2,
            compiler_params=pltpu.CompilerParams(vmem_limit_bytes=48 << 20),
            name="collect",
        )(*four, picker)
        own_rows.append(own)
        got_rows.append(swapped(send))

    row_spec = pl.BlockSpec((1, taken, width), lambda e: (e, 0, 0))
    out_spec = pl.BlockSpec((1, depth * taken, width), lambda e: (e, 0, 0))
    results, send_back = pl.pallas_call(
        expert_kernel,
        grid=(local_experts,),
        in_specs=[row_spec] * (2 * depth)
        + [
            pl.BlockSpec((1, width, hidden_width), lambda e: (e, 0, 0)),
            pl.BlockSpec((1, width, hidden_width), lambda e: (e, 0, 0)),
            pl.BlockSpec((1, hidden_width, width), lambda e: (e, 0, 0)),
        ],
        out_specs=[out_spec] * 2,
        out_shape=[jax.ShapeDtypeStruct((local_experts, depth * taken, width), bf16)] * 2,
        compiler_params=pltpu.CompilerParams(vmem_limit_bytes=56 << 20),
        name="experts",
    )(*own_rows, *got_rows, expert_gate, expert_up, expert_down)
    got_back = swapped(send_back)

    total = None
    for steps in [*range(1, depth), 0]:
        result_spec = pl.BlockSpec(
            (local_experts, taken, width), lambda g, steps=steps: (0, steps, 0)
        )
        cols_spec = pl.BlockSpec(
            (tok_rows, 2 * experts_all), lambda g: (0, width // (2 * experts_all))
        )
        row_shape = jax.ShapeDtypeStruct((tok_rows, width), bf16)
        far_shape = jax.ShapeDtypeStruct((2 * tok_rows, width), bf16)
        far, near, here = pl.pallas_call(
            functools.partial(spread_kernel, slots=slots),
            grid=(1,),
            in_specs=[cols_spec] * 4 + [whole_ref(picker), result_spec, result_spec],
            out_specs=[whole_ref(far_shape), whole_ref(row_shape), whole_ref(row_shape)],
            out_shape=[far_shape, row_shape, row_shape],
            compiler_params=pltpu.CompilerParams(vmem_limit_bytes=48 << 20),
            name="spread",
        )(*blocks[steps], picker, results, got_back)
        across = second(far).astype(f32)
        near = first((near.astype(f32) + across[tok_rows:]).astype(bf16))
        here = here.astype(f32) + across[:tok_rows] + near.astype(f32)
        if steps:
            here = lifted(here.astype(bf16), -steps).astype(f32)
        total = here if total is None else total + here
    return total.astype(bf16)


def expert_layer_sent(
    stream, moe_gain, router, expert_ids, expert_gate, expert_up, expert_down, sources
):
    tok_rows, model_width = stream.shape
    top_count = expert_ids.shape[1]
    local_experts = expert_gate.shape[0]
    experts_all = local_experts * sources
    capacity = (11 * tok_rows * top_count + 10 * experts_all - 1) // (10 * experts_all)
    normed = rms_rows(stream, moe_gain).astype(jnp.bfloat16)
    logits = jnp.dot(normed, router, preferred_element_type=jnp.float32)
    chosen = jnp.take_along_axis(logits, expert_ids, axis=1)
    raised = jnp.exp(chosen)
    weights = raised / jnp.sum(raised, axis=1, keepdims=True)
    flat_ids = expert_ids.reshape(-1)
    matches = (flat_ids[:, None] == jnp.arange(experts_all, dtype=jnp.int32)[None, :]).astype(
        jnp.int32
    )
    slot_index = jnp.sum((jnp.cumsum(matches, axis=0) - 1) * matches, axis=1)
    places = flat_ids * capacity + slot_index
    token_rows = jnp.arange(tok_rows * top_count, dtype=jnp.int32) // top_count
    outgoing = (
        jnp.zeros((experts_all * capacity, model_width), jnp.bfloat16)
        .at[places]
        .set(normed[token_rows])
    )
    outgoing = outgoing.reshape(sources, local_experts, capacity, model_width)
    received = lax.all_to_all(outgoing, ("ctx", "head"), split_axis=0, concat_axis=0, tiled=True)
    gate_part = jnp.einsum(
        "nesd,edh->nesh", received, expert_gate, preferred_element_type=jnp.float32
    )
    up_part = jnp.einsum("nesd,edh->nesh", received, expert_up, preferred_element_type=jnp.float32)
    hidden = (jax.nn.silu(gate_part) * up_part).astype(jnp.bfloat16)
    returned = lax.all_to_all(
        jnp.einsum(
            "nesh,ehd->nesd", hidden, expert_down, preferred_element_type=jnp.float32
        ).astype(jnp.bfloat16),
        ("ctx", "head"),
        split_axis=0,
        concat_axis=0,
        tiled=True,
    )
    gathered_rows = returned.reshape(experts_all * capacity, model_width)[places].reshape(
        tok_rows, top_count, model_width
    )
    return jnp.sum(weights[:, :, None] * gathered_rows.astype(jnp.float32), axis=1).astype(
        jnp.bfloat16
    )


def unit_inverse(strict_part):
    size = strict_part.shape[0]
    row = lax.broadcasted_iota(jnp.int32, (size, size), 0)
    col = lax.broadcasted_iota(jnp.int32, (size, size), 1)
    inverse = jnp.where(row == col, 1.0, 0.0)
    half = 1
    while half < size:
        joining = (row // (2 * half) == col // (2 * half)) & (row // half != col // half)
        corner = jnp.where(joining, strict_part, 0.0)
        if half == 1:
            inverse = inverse - corner
        else:
            step = contract_close(corner, inverse, ((1,), (0,)))
            inverse = inverse - contract_close(inverse, step, ((1,), (0,)))
        half *= 2
    return inverse


def unit_rows(rows):
    return rows * lax.rsqrt(jnp.sum(rows * rows, axis=-1, keepdims=True) + epsilon)


def delta_kernel(
    raw_ref,
    rim_ref,
    taps_ref,
    beta_ref,
    decay_ref,
    rate_ref,
    core_ref,
    reading_ref,
    moved_ref,
    extended,
    mixed,
    strengths,
    falls,
    carried,
    *,
    key_heads,
    chunk,
):
    rows, conv_cols = raw_ref.shape
    heads = moved_ref.shape[0]
    group = heads // key_heads
    tap_count = taps_ref.shape[0]
    rim = rim_ref.shape[0]
    extended[0:rim, :] = rim_ref[...]
    extended[rim : rim + rows, :] = raw_ref[...].astype(f32)
    key_at, value_at = key_heads * DK, 2 * key_heads * DK
    for start in range(0, rows, chunk):
        for first in range(0, conv_cols, DK):
            columns = slice(first, first + DK)
            summed = jnp.zeros((chunk, DK), f32)
            for tap in range(tap_count):
                offset = rim - (tap_count - 1) + start + tap
                summed += taps_ref[tap : tap + 1, columns] * extended[
                    offset : offset + chunk, columns
                ]
            value = summed / (1.0 + jnp.exp(-summed))
            if first < key_at:
                value = unit_rows(value) * DK**-0.5
            elif first < value_at:
                value = unit_rows(value)
            mixed[start : start + chunk, columns] = value
    beta = beta_ref[...]
    strengths[...] = 1.0 / (1.0 + jnp.exp(-beta))
    shifted = decay_ref[...] + rate_ref[1:2, :]
    softened = jnp.maximum(shifted, 0.0) + jnp.log1p(jnp.exp(-jnp.abs(shifted)))
    falls[...] = -jnp.exp(rate_ref[0:1, :]) * softened

    row = lax.broadcasted_iota(jnp.int32, (chunk, chunk), 0)
    col = lax.broadcasted_iota(jnp.int32, (chunk, chunk), 1)
    inclusive, strict = row >= col, row > col
    lower = jnp.where(inclusive, 1.0, 0.0)
    across = lax.broadcasted_iota(jnp.int32, (DK, 2 * DK), 1)
    down = lax.broadcasted_iota(jnp.int32, (DK, 2 * DK), 0)
    carried[...] = jnp.broadcast_to(
        jnp.where(across == down + DK, 1.0, 0.0)[None], carried.shape
    )

    def advance(step, nothing):
        here = pl.ds(pl.multiple_of(step * chunk, chunk), chunk)
        fall = falls[here, :]
        strength = strengths[here, :]
        cumulative = contract(lower, fall, ((1,), (0,)), lax.Precision.HIGHEST)
        cumulative_rows = contract(fall, lower, ((0,), (1,)), lax.Precision.HIGHEST)
        for key_head in range(key_heads):
            queries = mixed[here, key_head * DK : (key_head + 1) * DK]
            keys = mixed[here, key_at + key_head * DK : key_at + (key_head + 1) * DK]
            dots = contract_close(jnp.concatenate([keys, queries], axis=0), keys, ((1,), (1,)))
            for head in range(key_head * group, (key_head + 1) * group):
                values = mixed[here, value_at + head * DK : value_at + (head + 1) * DK]
                total = cumulative[:, head : head + 1]
                spread = total - cumulative_rows[head : head + 1, :]
                kept = jnp.where(inclusive, jnp.exp(jnp.where(inclusive, spread, 0.0)), 0.0)
                own = strength[:, head : head + 1]
                solver = unit_inverse(own * jnp.where(strict, kept, 0.0) * dots[:chunk])
                risen = jnp.exp(total)
                last = total[chunk - 1 :, :]
                solved = contract_close(
                    solver,
                    own * jnp.concatenate([values, risen * keys], axis=1),
                    ((1,), (0,)),
                )
                mixing = kept * dots[chunk:]
                state = carried[head]
                read = contract_close(
                    jnp.concatenate([solved[:, DK:], risen * queries], axis=0),
                    state,
                    ((1,), (0,)),
                )
                update = (
                    jnp.concatenate([solved[:, :DK], jnp.zeros((chunk, DK), f32)], axis=1)
                    - read[:chunk]
                )
                result = read[chunk:] + contract_close(mixing, update, ((1,), (0,)))
                core_ref[here, head * DK : (head + 1) * DK] = result[:, :DK]
                reading_ref[here, head * DK : (head + 1) * DK] = result[:, DK:]
                carried[head] = jnp.exp(last) * state + contract_close(
                    jnp.exp(last - total) * keys, update, ((0,), (0,)))
        return nothing

    lax.fori_loop(0, rows // chunk, advance, 0)
    moved_ref[...] = carried[...].astype(bf16)


def finish_kernel(
    place_ref, moved_ref, core_ref, reading_ref, gate_ref, gain_ref, weight_ref, out_ref, gated
):
    heads = moved_ref.shape[1]

    def join(earlier, states):
        return tuple(
            contract_close(moved_ref[earlier, head, :, DK:].astype(f32), state, ((1,), (0,)))
            + moved_ref[earlier, head, :, :DK].astype(f32)
            for head, state in enumerate(states)
        )

    states = lax.fori_loop(
        0, place_ref[0], join, tuple(jnp.zeros((DK, DK), f32) for _ in range(heads))
    )
    for head, state in enumerate(states):
        columns = slice(head * DK, (head + 1) * DK)
        core = core_ref[:, columns] + contract_close(
            reading_ref[:, columns], state, ((1,), (0,)))
        normal = (
            core
            * lax.rsqrt(jnp.mean(core * core, axis=-1, keepdims=True) + epsilon)
            * gain_ref[...]
        )
        gate = gate_ref[:, columns].astype(f32)
        gated[:, columns] = (normal * (gate / (1.0 + jnp.exp(-gate)))).astype(bf16)
    out_ref[...] = contract(gated[...], weight_ref[...], ((1,), (0,))).astype(bf16)


def on_device(
    stream,
    moe_gain,
    router,
    expert_ids,
    expert_gate,
    expert_up,
    expert_down,
    mixer_gain,
    query_weight,
    key_weight,
    value_weight,
    output_gate,
    beta_weight,
    decay_weight,
    query_conv,
    key_conv,
    value_conv,
    decay_log,
    decay_bias,
    head_gain,
    out_weight,
):
    ctx_count = lax.axis_size("ctx")
    head_count = lax.axis_size("head")
    sources = ctx_count * head_count
    ctx_place = lax.axis_index("ctx")
    experts = (stream, moe_gain, router, expert_ids, expert_gate, expert_up, expert_down)
    if 2 * sources * stream.size <= GATHER_LIMIT and head_count == 4 and ctx_count % 2 == 0:
        moe_out = expert_layer_gathered(*experts, sources)
    else:
        moe_out = expert_layer_sent(*experts, sources)
    mixer_in = rms_rows(
        stream.astype(jnp.float32) + moe_out.astype(jnp.float32), mixer_gain
    ).astype(jnp.bfloat16)
    piece_rows = lax.all_gather(mixer_in, "head", axis=0, tiled=True)

    def project(*matrices):
        return jnp.concatenate(
            [jnp.dot(piece_rows, matrix, preferred_element_type=f32) for matrix in matrices], axis=1
        )

    qkv_raw = project(query_weight, key_weight, value_weight).astype(bf16)
    gate_raw = project(output_gate).astype(bf16)
    beta_raw = project(beta_weight)
    decay_raw = project(decay_weight)
    rows, conv_cols = qkv_raw.shape
    key_heads = query_weight.shape[1] // DK
    heads = beta_weight.shape[1]
    value_cols = value_weight.shape[1]
    taps = jnp.concatenate([query_conv, key_conv, value_conv], axis=1)
    rim_len = taps.shape[0] - 1
    rim = passed_along(qkv_raw[rows - rim_len :], "ctx", 1)
    rim = jnp.concatenate([jnp.zeros((8 - rim_len, conv_cols), f32), rim.astype(f32)], axis=0)
    rates = jnp.stack([decay_log, decay_bias])
    chunk = math.gcd(rows, CHUNK)
    core, reading, moved = pl.pallas_call(
        functools.partial(delta_kernel, key_heads=key_heads, chunk=chunk),
        out_shape=(
            jax.ShapeDtypeStruct((rows, value_cols), f32),
            jax.ShapeDtypeStruct((rows, value_cols), f32),
            jax.ShapeDtypeStruct((heads, DK, 2 * DK), bf16),
        ),
        scratch_shapes=[
            pltpu.VMEM((rows + 8, conv_cols), f32),
            pltpu.VMEM((rows, conv_cols), f32),
            pltpu.VMEM((rows, heads), f32),
            pltpu.VMEM((rows, heads), f32),
            pltpu.VMEM((heads, DK, 2 * DK), f32),
        ],
        compiler_params=pltpu.CompilerParams(vmem_limit_bytes=48 << 20),
        name="delta",
    )(qkv_raw, rim, taps, beta_raw, decay_raw, rates)
    everything = lax.all_gather(moved, "ctx")
    in_vmem = pl.BlockSpec(memory_space=pltpu.VMEM)
    partial = pl.pallas_call(
        finish_kernel,
        in_specs=[pl.BlockSpec(memory_space=pltpu.SMEM)] + [in_vmem] * 6,
        out_shape=jax.ShapeDtypeStruct((rows, out_weight.shape[1]), bf16),
        scratch_shapes=[pltpu.VMEM((rows, value_cols), bf16)],
        compiler_params=pltpu.CompilerParams(vmem_limit_bytes=48 << 20),
        name="finish",
    )(
        ctx_place.reshape(1),
        everything,
        core,
        reading,
        gate_raw,
        head_gain.reshape(1, -1),
        out_weight,
    )
    mixer_out = lax.psum_scatter(partial, "head", scatter_dimension=0, tiled=True)
    return (moe_out, mixer_out)


def solution(mesh):
    return jax.shard_map(
        on_device,
        mesh=mesh,
        in_specs=(
            P(("ctx", "head"), None),
            P(),
            P(),
            P(("ctx", "head"), None),
            P(("ctx", "head"), None, None),
            P(("ctx", "head"), None, None),
            P(("ctx", "head"), None, None),
            P(),
            P(None, "head"),
            P(None, "head"),
            P(None, "head"),
            P(None, "head"),
            P(None, "head"),
            P(None, "head"),
            P(None, "head"),
            P(None, "head"),
            P(None, "head"),
            P("head"),
            P("head"),
            P(),
            P("head", None),
        ),
        out_specs=(P(("ctx", "head"), None), P(("ctx", "head"), None)),
        check_vma=False,
    )
```

```python
import functools
import math

import jax
import jax.numpy as jnp
from jax import lax
from jax.experimental import pallas as pl
from jax.experimental.pallas import tpu as pltpu
from jax.sharding import PartitionSpec as P

DK = 128
CHUNK = 128
GATHER_LIMIT = 32 << 20


epsilon = 1e-06
f32 = jnp.float32
bf16 = jnp.bfloat16


def passed_along(value, axis, steps):
    count = lax.axis_size(axis)
    first, last = (max(0, -steps), min(count, count - steps))
    return lax.ppermute(value, axis, [(source, source + steps) for source in range(first, last)])


def rms_rows(values, gain):
    values = values.astype(jnp.float32)
    scale = lax.rsqrt(jnp.mean(values * values, axis=-1, keepdims=True) + epsilon)
    return values * scale * gain


def after(value, earlier):
    return lax.optimization_barrier((value, earlier))[0]


def whole_ref(array):
    return pl.BlockSpec(array.shape, lambda *_: (0,) * array.ndim)


def contract(a, b, dims, precision=None):
    return lax.dot_general(
        a, b, (dims, ((), ())), precision=precision, preferred_element_type=f32
    )


def parts(values):
    high = values.astype(bf16)
    return high, (values - high.astype(f32)).astype(bf16)


def contract_close(a, b):
    a_high, a_low = parts(a)
    b_high, b_low = parts(b)
    doubled = jnp.concatenate([a_high, a_low], axis=1)
    if 2 * b.shape[1] <= 2 * DK:
        both = jnp.concatenate([b_high, b_low], axis=1)
        product = contract(doubled, jnp.concatenate([both, both], axis=0), ((1,), (0,)))
        return product[:, : b.shape[1]] + product[:, b.shape[1] :]
    return contract(
        doubled, jnp.concatenate([b_high, b_high], axis=0), ((1,), (0,))
    ) + contract(a_high, b_low, ((1,), (0,)))


def contract_rows(a, b):
    a_high, a_low = parts(a)
    b_high, b_low = parts(b)
    product = contract(
        jnp.concatenate([a_high, a_low], axis=1),
        jnp.concatenate(
            [jnp.concatenate([b_high, b_high], axis=1), jnp.concatenate([b_low, b_low], axis=1)],
            axis=0,
        ),
        ((1,), (1,)),
    )
    return product[:, : b.shape[0]] + product[:, b.shape[0] :]


def pair_routes(cols, picker, lines, tok_rows, slots):
    rows = cols.shape[0]
    weight_rows = contract(picker, cols, ((1,), (1,)))
    named = weight_rows > 0
    before = lax.broadcasted_iota(jnp.int32, (rows, rows), 0)
    after = lax.broadcasted_iota(jnp.int32, (rows, rows), 1)
    earlier = (before < after) & (before // tok_rows == after // tok_rows)
    rank = contract(
        jnp.where(named, 1.0, 0.0).astype(bf16),
        jnp.where(earlier, 1.0, 0.0).astype(bf16),
        ((1,), (0,)),
    )
    first_slot = lax.broadcasted_iota(jnp.int32, rank.shape, 1) // tok_rows * slots
    rank = jnp.where(named, rank.astype(jnp.int32) + first_slot, -1)
    slot = lax.broadcasted_iota(jnp.int32, (rows // tok_rows * slots, rows), 0)
    picks = [jnp.where(slot == rank[line : line + 1], 1.0, 0.0) for line in range(lines)]
    return weight_rows, picks


def collect_kernel(block_00, block_10, block_01, block_11, picker_ref, own_ref, send_ref, *, slots):
    local_experts, taken, width = own_ref.shape
    tok_rows = block_00.shape[0]
    pair = taken // 2
    for at, pair_refs in enumerate(((block_01, block_11), (block_00, block_10))):
        rows = jnp.concatenate([ref[...] for ref in pair_refs], axis=0)
        _, picks = pair_routes(
            rows[:, width:], picker_ref[...], 2 * local_experts, tok_rows, slots
        )
        picked = contract(
            jnp.concatenate(picks, axis=0).astype(bf16), rows[:, :width], ((1,), (0,))
        ).astype(bf16)
        for expert in range(local_experts):
            there = slice(at * pair, (at + 1) * pair)
            own_ref[expert, there, :] = picked[expert * pair : (expert + 1) * pair]
            line = local_experts + expert
            send_ref[expert, there, :] = picked[line * pair : (line + 1) * pair]


def expert_kernel(*refs):
    *row_refs, gate_ref, up_ref, down_ref, own_ref, send_ref = refs
    half = len(row_refs) // 2
    for sources, out_ref in ((row_refs[half:], send_ref), (row_refs[:half], own_ref)):
        rows = jnp.concatenate([ref[0] for ref in sources], axis=0)
        gate = contract(rows, gate_ref[0], ((1,), (0,)))
        up = contract(rows, up_ref[0], ((1,), (0,)))
        hidden = (gate / (1.0 + jnp.exp(-gate)) * up).astype(bf16)
        out_ref[0] = contract(hidden, down_ref[0], ((1,), (0,))).astype(bf16)


def spread_kernel(
    cols_00, cols_10, cols_01, cols_11, picker_ref, own_ref, got_ref, far_ref, near_ref, here_ref, *, slots
):
    local_experts, taken, _ = own_ref.shape
    tok_rows = cols_00.shape[0]
    pair = taken // 2
    for at, pair_refs in enumerate(((cols_01, cols_11), (cols_00, cols_10))):
        cols = jnp.concatenate([ref[...] for ref in pair_refs], axis=0)
        weight_rows, picks = pair_routes(
            cols, picker_ref[...], 2 * local_experts, tok_rows, slots
        )
        scaled = []
        for line, pick in enumerate(picks):
            result_ref = (own_ref, got_ref)[line // local_experts]
            result = result_ref[line % local_experts, at * pair : (at + 1) * pair, :]
            weight = jnp.sum(pick * weight_rows[line : line + 1], axis=1, keepdims=True)
            scaled.append((result.astype(f32) * weight).astype(bf16))
        summed = contract(
            jnp.concatenate(picks, axis=0).astype(bf16),
            jnp.concatenate(scaled, axis=0),
            ((0,), (0,)),
        ).astype(bf16)
        if at == 0:
            far_ref[...] = summed
        else:
            here_ref[...] = summed[:tok_rows]
            near_ref[...] = summed[tok_rows:]


def expert_layer_gathered(
    stream,
    moe_gain,
    router,
    expert_ids,
    expert_gate,
    expert_up,
    expert_down,
    sources,
):
    tok_rows, width = stream.shape
    local_experts, _, hidden_width = expert_gate.shape
    experts_all = local_experts * sources
    depth = sources // 8
    place = lax.axis_index(("ctx", "head"))

    def sent(value, move):
        pairs = []
        for device in range(sources):
            z, y, x, core = device // 8, device // 4 % 2, device // 2 % 2, device % 2
            z, y, x, core = move(z, y, x, core)
            pairs.append((device, ((z * 2 + y) * 2 + x) * 2 + core))
        return lax.ppermute(value, ("ctx", "head"), pairs)

    def lifted(value, steps):
        return sent(value, lambda z, y, x, core: ((z + steps) % depth, y, x, core))

    def first(value):
        return sent(value, lambda z, y, x, core: (z, y ^ (1 - core), x ^ core, core))

    def second(value):
        return sent(value, lambda z, y, x, core: (z, y ^ core, x ^ (1 - core), core))

    def swapped(value):
        return sent(value, lambda z, y, x, core: (z, y, x, 1 - core))

    normed = rms_rows(stream, moe_gain).astype(bf16)
    logits = jnp.dot(normed, router, preferred_element_type=f32)
    named = jnp.any(
        expert_ids[:, :, None] == jnp.arange(experts_all, dtype=jnp.int32)[None, None, :], axis=1
    )
    raised = jnp.where(named, jnp.exp(logits), 0.0)
    weights = raised / jnp.sum(raised, axis=1, keepdims=True)
    coarse = lax.reduce_precision(weights, 8, 7)
    packet = jnp.concatenate(
        [normed, coarse.astype(bf16), (weights - coarse).astype(bf16)], axis=1
    )

    capacity = (11 * tok_rows * expert_ids.shape[1] + 10 * experts_all - 1) // (10 * experts_all)
    slots = -(-capacity // 8) * 8
    taken = 4 * slots
    column = jnp.arange(2 * experts_all, dtype=jnp.int32)[None, :] % experts_all
    line = jnp.arange(16, dtype=jnp.int32)[:, None]
    owner = jnp.where(line < local_experts, place, place ^ 1)
    picker = (
        (line < 2 * local_experts) & (column == owner * local_experts + line % local_experts)
    ).astype(bf16)

    order = [0] + sorted(range(1, depth), key=lambda steps: min(steps, depth - steps))
    blocks, own_rows, got_rows = [None] * depth, [None] * depth, [None] * depth
    mine = packet
    for at, steps in enumerate(order):
        if steps:
            mine = lifted(after(packet, mine) if at > 1 else packet, steps)
        near = first(mine)
        blocks[steps] = (mine, near, second(mine), second(near))
    for steps in order:
        own, send = pl.pallas_call(
            functools.partial(collect_kernel, slots=slots),
            out_shape=[jax.ShapeDtypeStruct((local_experts, taken, width), bf16)] * 2,
            compiler_params=pltpu.CompilerParams(vmem_limit_bytes=48 << 20),
            name="collect",
        )(*blocks[steps], picker)
        own_rows[steps] = own
        got_rows[steps] = swapped(send)

    row_spec = pl.BlockSpec((1, taken, width), lambda e: (e, 0, 0))
    out_spec = pl.BlockSpec((1, depth * taken, width), lambda e: (e, 0, 0))
    results, send_back = pl.pallas_call(
        expert_kernel,
        grid=(local_experts,),
        in_specs=[row_spec] * (2 * depth)
        + [
            pl.BlockSpec((1, width, hidden_width), lambda e: (e, 0, 0)),
            pl.BlockSpec((1, width, hidden_width), lambda e: (e, 0, 0)),
            pl.BlockSpec((1, hidden_width, width), lambda e: (e, 0, 0)),
        ],
        out_specs=[out_spec] * 2,
        out_shape=[jax.ShapeDtypeStruct((local_experts, depth * taken, width), bf16)] * 2,
        compiler_params=pltpu.CompilerParams(vmem_limit_bytes=56 << 20),
        name="experts",
    )(*own_rows, *got_rows, expert_gate, expert_up, expert_down)
    got_back = swapped(send_back)

    def spread(steps):
        result_spec = pl.BlockSpec((local_experts, taken, width), lambda g: (0, steps, 0))
        cols_spec = pl.BlockSpec(
            (tok_rows, 2 * experts_all), lambda g: (0, width // (2 * experts_all))
        )
        row_shape = jax.ShapeDtypeStruct((tok_rows, width), bf16)
        far_shape = jax.ShapeDtypeStruct((2 * tok_rows, width), bf16)
        return pl.pallas_call(
            functools.partial(spread_kernel, slots=slots),
            grid=(1,),
            in_specs=[cols_spec] * 4 + [whole_ref(picker), result_spec, result_spec],
            out_specs=[whole_ref(far_shape), whole_ref(row_shape), whole_ref(row_shape)],
            out_shape=[far_shape, row_shape, row_shape],
            compiler_params=pltpu.CompilerParams(vmem_limit_bytes=48 << 20),
            name="spread",
        )(*blocks[steps], picker, results, got_back)

    back = order[:0:-1] + [0]
    heres, landed = [], []
    total = 0.0
    ready = [spread(steps) for steps in back]
    for at, steps in enumerate(back):
        far, near, here = ready[at]
        across = second(far)
        if at == 1:
            across = after(across, ready[-1][0])
        for earlier in landed[at - 2 : at] if at == depth - 1 else landed[at - 2 : at - 1]:
            across = after(across, earlier)
        across = across.astype(f32)
        near = (near.astype(f32) + across[tok_rows:]).astype(bf16)
        if at >= 2:
            near = after(near, heres[at - 1])
        here = here.astype(f32) + across[:tok_rows] + first(near).astype(f32)
        if steps:
            heres.append(here.astype(bf16))
            landed.append(lifted(heres[-1], -steps))
            here = landed[-1].astype(f32)
        total += here
    return total.astype(bf16)


def expert_layer_sent(
    stream, moe_gain, router, expert_ids, expert_gate, expert_up, expert_down, sources
):
    tok_rows, model_width = stream.shape
    top_count = expert_ids.shape[1]
    local_experts = expert_gate.shape[0]
    experts_all = local_experts * sources
    capacity = (11 * tok_rows * top_count + 10 * experts_all - 1) // (10 * experts_all)
    normed = rms_rows(stream, moe_gain).astype(jnp.bfloat16)
    logits = jnp.dot(normed, router, preferred_element_type=jnp.float32)
    chosen = jnp.take_along_axis(logits, expert_ids, axis=1)
    raised = jnp.exp(chosen)
    weights = raised / jnp.sum(raised, axis=1, keepdims=True)
    flat_ids = expert_ids.reshape(-1)
    matches = (flat_ids[:, None] == jnp.arange(experts_all, dtype=jnp.int32)[None, :]).astype(
        jnp.int32
    )
    slot_index = jnp.sum((jnp.cumsum(matches, axis=0) - 1) * matches, axis=1)
    places = flat_ids * capacity + slot_index
    token_rows = jnp.arange(tok_rows * top_count, dtype=jnp.int32) // top_count
    outgoing = (
        jnp.zeros((experts_all * capacity, model_width), jnp.bfloat16)
        .at[places]
        .set(normed[token_rows])
    )
    outgoing = outgoing.reshape(sources, local_experts, capacity, model_width)
    received = lax.all_to_all(outgoing, ("ctx", "head"), split_axis=0, concat_axis=0, tiled=True)
    gate_part = jnp.einsum(
        "nesd,edh->nesh", received, expert_gate, preferred_element_type=jnp.float32
    )
    up_part = jnp.einsum("nesd,edh->nesh", received, expert_up, preferred_element_type=jnp.float32)
    hidden = (jax.nn.silu(gate_part) * up_part).astype(jnp.bfloat16)
    returned = lax.all_to_all(
        jnp.einsum(
            "nesh,ehd->nesd", hidden, expert_down, preferred_element_type=jnp.float32
        ).astype(jnp.bfloat16),
        ("ctx", "head"),
        split_axis=0,
        concat_axis=0,
        tiled=True,
    )
    gathered_rows = returned.reshape(experts_all * capacity, model_width)[places].reshape(
        tok_rows, top_count, model_width
    )
    return jnp.sum(weights[:, :, None] * gathered_rows.astype(jnp.float32), axis=1).astype(
        jnp.bfloat16
    )


def unit_inverses(strict_parts):
    size = strict_parts[0].shape[0]
    row = lax.broadcasted_iota(jnp.int32, (size, size), 0)
    col = lax.broadcasted_iota(jnp.int32, (size, size), 1)
    unit = jnp.where(row == col, 1.0, 0.0)
    joining = (row // 2 == col // 2) & (row != col)
    inverses = [unit - jnp.where(joining, part, 0.0) for part in strict_parts]
    half = 2
    while half < size:
        joining = (row // (2 * half) == col // (2 * half)) & (row // half != col // half)
        corners = [jnp.where(joining, part, 0.0) for part in strict_parts]
        if half < 8:
            steps = [contract_close(c, inverse) for c, inverse in zip(corners, inverses)]
            moves = [contract_close(inverse, step) for inverse, step in zip(inverses, steps)]
            inverses = [inverse - move for inverse, move in zip(inverses, moves)]
        else:
            starts = range(0, size, 2 * half)

            def lower_rows(array):
                return jnp.concatenate([array[at + half : at + 2 * half] for at in starts], axis=0)

            zeros = jnp.zeros((half, size), f32)
            steps = [
                contract_close(lower_rows(c), inverse) for c, inverse in zip(corners, inverses)
            ]
            steps = [
                jnp.concatenate(
                    [
                        piece
                        for at in range(0, size // 2, half)
                        for piece in (zeros, step[at : at + half])
                    ],
                    axis=0,
                )
                for step in steps
            ]
            lowers = [lower_rows(inverse) for inverse in inverses]
            lowers = [lower - contract_close(lower, step) for lower, step in zip(lowers, steps)]
            inverses = [
                jnp.concatenate(
                    [
                        piece
                        for at in starts
                        for piece in (
                            inverse[at : at + half],
                            lower[at // 2 : at // 2 + half],
                        )
                    ],
                    axis=0,
                )
                for inverse, lower in zip(inverses, lowers)
            ]
        half *= 2
    return inverses


def unit_rows(rows):
    return rows * lax.rsqrt(jnp.sum(rows * rows, axis=-1, keepdims=True) + epsilon)


def delta_kernel(
    raw_ref,
    rim_ref,
    taps_ref,
    beta_ref,
    decay_ref,
    rate_ref,
    core_ref,
    reading_ref,
    moved_ref,
    extended,
    mixed,
    strengths,
    falls,
    carried,
    *,
    key_heads,
    chunk,
):
    rows, conv_cols = raw_ref.shape
    heads = moved_ref.shape[0]
    group = heads // key_heads
    tap_count = taps_ref.shape[0]
    rim = rim_ref.shape[0]
    extended[0:rim, :] = rim_ref[...]
    extended[rim : rim + rows, :] = raw_ref[...].astype(f32)
    key_at, value_at = key_heads * DK, 2 * key_heads * DK
    for start in range(0, rows, chunk):
        for first in range(0, conv_cols, DK):
            columns = slice(first, first + DK)
            summed = jnp.zeros((chunk, DK), f32)
            for tap in range(tap_count):
                offset = rim - (tap_count - 1) + start + tap
                summed += taps_ref[tap : tap + 1, columns] * extended[
                    offset : offset + chunk, columns
                ]
            value = summed / (1.0 + jnp.exp(-summed))
            if first < key_at:
                value = unit_rows(value) * DK**-0.5
            elif first < value_at:
                value = unit_rows(value)
            mixed[start : start + chunk, columns] = value
    beta = beta_ref[...]
    strengths[...] = 1.0 / (1.0 + jnp.exp(-beta))
    shifted = decay_ref[...] + rate_ref[1:2, :]
    softened = jnp.maximum(shifted, 0.0) + jnp.log1p(jnp.exp(-jnp.abs(shifted)))
    falls[...] = -jnp.exp(rate_ref[0:1, :]) * softened

    row = lax.broadcasted_iota(jnp.int32, (chunk, chunk), 0)
    col = lax.broadcasted_iota(jnp.int32, (chunk, chunk), 1)
    inclusive, strict = row >= col, row > col
    lower = jnp.where(inclusive, 1.0, 0.0)
    across = lax.broadcasted_iota(jnp.int32, (DK, 2 * DK), 1)
    down = lax.broadcasted_iota(jnp.int32, (DK, 2 * DK), 0)
    carried[...] = jnp.broadcast_to(
        jnp.where(across == down + DK, 1.0, 0.0)[None], carried.shape
    )

    def advance(step, nothing):
        here = pl.ds(pl.multiple_of(step * chunk, chunk), chunk)
        fall = falls[here, :]
        strength = strengths[here, :]
        cumulative = contract(lower, fall, ((1,), (0,)), lax.Precision.HIGHEST)
        cumulative_rows = contract(fall, lower, ((0,), (1,)), lax.Precision.HIGHEST)
        owners = range(heads)
        queries = [mixed[here, k * DK : (k + 1) * DK] for k in range(key_heads)]
        keys = [mixed[here, key_at + k * DK : key_at + (k + 1) * DK] for k in range(key_heads)]
        dots = [
            contract_rows(jnp.concatenate([key, query], axis=0), key)
            for key, query in zip(keys, queries)
        ]
        totals = [cumulative[:, head : head + 1] for head in owners]
        kept = [
            jnp.where(
                inclusive,
                jnp.exp(jnp.where(inclusive, totals[head] - cumulative_rows[head : head + 1, :], 0.0)),
                0.0,
            )
            for head in owners
        ]
        own = [strength[:, head : head + 1] for head in owners]
        solvers = unit_inverses(
            [
                own[head] * jnp.where(strict, kept[head], 0.0) * dots[head // group][:chunk]
                for head in owners
            ]
        )
        risen = [jnp.exp(total) for total in totals]
        solved = [
            contract_close(
                solvers[head],
                own[head]
                * jnp.concatenate(
                    [
                        mixed[here, value_at + head * DK : value_at + (head + 1) * DK],
                        risen[head] * keys[head // group],
                    ],
                    axis=1,
                ),
            )
            for head in owners
        ]
        states = [carried[head] for head in owners]
        read = [
            contract_close(
                jnp.concatenate(
                    [solved[head][:, DK:], risen[head] * queries[head // group]], axis=0
                ),
                states[head],
            )
            for head in owners
        ]
        updates = [
            jnp.concatenate([solved[head][:, :DK], jnp.zeros((chunk, DK), f32)], axis=1)
            - read[head][:chunk]
            for head in owners
        ]
        for head in owners:
            last = totals[head][chunk - 1 :, :]
            leaving = jnp.exp(last - totals[head]) * keys[head // group]
            carried[head] = jnp.exp(last) * states[head] + contract_close(
                leaving.T, updates[head]
            )
        for head in owners:
            result = read[head][chunk:] + contract_close(
                kept[head] * dots[head // group][chunk:], updates[head]
            )
            core_ref[here, head * DK : (head + 1) * DK] = result[:, :DK]
            reading_ref[here, head * DK : (head + 1) * DK] = result[:, DK:]
        return nothing

    lax.fori_loop(0, rows // chunk, advance, 0)
    moved_ref[...] = carried[...].astype(bf16)


def finish_kernel(
    place_ref, moved_ref, core_ref, reading_ref, gate_ref, gain_ref, weight_ref, out_ref, gated
):
    heads = moved_ref.shape[1]

    def join(earlier, states):
        return tuple(
            contract_close(moved_ref[earlier, head, :, DK:].astype(f32), state)
            + moved_ref[earlier, head, :, :DK].astype(f32)
            for head, state in enumerate(states)
        )

    states = lax.fori_loop(
        0, place_ref[0], join, tuple(jnp.zeros((DK, DK), f32) for _ in range(heads))
    )
    for head, state in enumerate(states):
        columns = slice(head * DK, (head + 1) * DK)
        core = core_ref[:, columns] + contract_close(reading_ref[:, columns], state)
        normal = (
            core
            * lax.rsqrt(jnp.mean(core * core, axis=-1, keepdims=True) + epsilon)
            * gain_ref[...]
        )
        gate = gate_ref[:, columns].astype(f32)
        gated[:, columns] = (normal * (gate / (1.0 + jnp.exp(-gate)))).astype(bf16)
    out_ref[...] = contract(gated[...], weight_ref[...], ((1,), (0,))).astype(bf16)


def on_device(
    stream,
    moe_gain,
    router,
    expert_ids,
    expert_gate,
    expert_up,
    expert_down,
    mixer_gain,
    query_weight,
    key_weight,
    value_weight,
    output_gate,
    beta_weight,
    decay_weight,
    query_conv,
    key_conv,
    value_conv,
    decay_log,
    decay_bias,
    head_gain,
    out_weight,
):
    ctx_count = lax.axis_size("ctx")
    head_count = lax.axis_size("head")
    sources = ctx_count * head_count
    ctx_place = lax.axis_index("ctx")
    experts = (stream, moe_gain, router, expert_ids, expert_gate, expert_up, expert_down)
    if 2 * sources * stream.size <= GATHER_LIMIT and head_count == 4 and ctx_count % 2 == 0:
        moe_out = expert_layer_gathered(*experts, sources)
    else:
        moe_out = expert_layer_sent(*experts, sources)
    mixer_in = rms_rows(
        stream.astype(jnp.float32) + moe_out.astype(jnp.float32), mixer_gain
    ).astype(jnp.bfloat16)
    piece_rows = lax.all_gather(mixer_in, "head", axis=0, tiled=True)

    def project(*matrices):
        return jnp.concatenate(
            [jnp.dot(piece_rows, matrix, preferred_element_type=f32) for matrix in matrices], axis=1
        )

    qkv_raw = project(query_weight, key_weight, value_weight).astype(bf16)
    gate_raw = project(output_gate).astype(bf16)
    beta_raw = project(beta_weight)
    decay_raw = project(decay_weight)
    rows, conv_cols = qkv_raw.shape
    key_heads = query_weight.shape[1] // DK
    heads = beta_weight.shape[1]
    value_cols = value_weight.shape[1]
    taps = jnp.concatenate([query_conv, key_conv, value_conv], axis=1)
    rim_len = taps.shape[0] - 1
    rim = passed_along(qkv_raw[rows - rim_len :], "ctx", 1)
    rim = jnp.concatenate([jnp.zeros((8 - rim_len, conv_cols), f32), rim.astype(f32)], axis=0)
    rates = jnp.stack([decay_log, decay_bias])
    chunk = math.gcd(rows, CHUNK)
    core, reading, moved = pl.pallas_call(
        functools.partial(delta_kernel, key_heads=key_heads, chunk=chunk),
        out_shape=(
            jax.ShapeDtypeStruct((rows, value_cols), f32),
            jax.ShapeDtypeStruct((rows, value_cols), f32),
            jax.ShapeDtypeStruct((heads, DK, 2 * DK), bf16),
        ),
        scratch_shapes=[
            pltpu.VMEM((rows + 8, conv_cols), f32),
            pltpu.VMEM((rows, conv_cols), f32),
            pltpu.VMEM((rows, heads), f32),
            pltpu.VMEM((rows, heads), f32),
            pltpu.VMEM((heads, DK, 2 * DK), f32),
        ],
        compiler_params=pltpu.CompilerParams(vmem_limit_bytes=48 << 20),
        name="delta",
    )(qkv_raw, rim, taps, beta_raw, decay_raw, rates)
    everything = lax.all_gather(moved, "ctx")
    in_vmem = pl.BlockSpec(memory_space=pltpu.VMEM)
    partial = pl.pallas_call(
        finish_kernel,
        in_specs=[pl.BlockSpec(memory_space=pltpu.SMEM)] + [in_vmem] * 6,
        out_shape=jax.ShapeDtypeStruct((rows, out_weight.shape[1]), bf16),
        scratch_shapes=[pltpu.VMEM((rows, value_cols), bf16)],
        compiler_params=pltpu.CompilerParams(vmem_limit_bytes=48 << 20),
        name="finish",
    )(
        ctx_place.reshape(1),
        everything,
        core,
        reading,
        gate_raw,
        head_gain.reshape(1, -1),
        out_weight,
    )
    mixer_out = lax.psum_scatter(partial, "head", scatter_dimension=0, tiled=True)
    return (moe_out, mixer_out)


def solution(mesh):
    return jax.shard_map(
        on_device,
        mesh=mesh,
        in_specs=(
            P(("ctx", "head"), None),
            P(),
            P(),
            P(("ctx", "head"), None),
            P(("ctx", "head"), None, None),
            P(("ctx", "head"), None, None),
            P(("ctx", "head"), None, None),
            P(),
            P(None, "head"),
            P(None, "head"),
            P(None, "head"),
            P(None, "head"),
            P(None, "head"),
            P(None, "head"),
            P(None, "head"),
            P(None, "head"),
            P(None, "head"),
            P("head"),
            P("head"),
            P(),
            P("head", None),
        ),
        out_specs=(P(("ctx", "head"), None), P(("ctx", "head"), None)),
        check_vma=False,
    )
```

```python
import functools
import math

import jax
import jax.numpy as jnp
from jax import lax
from jax.experimental import pallas as pl
from jax.experimental.pallas import tpu as pltpu
from jax.sharding import PartitionSpec as P

DK = 128
CHUNK = 128
GATHER_LIMIT = 32 << 20


epsilon = 1e-06
f32 = jnp.float32
bf16 = jnp.bfloat16


def passed_along(value, axis, steps):
    count = lax.axis_size(axis)
    first, last = (max(0, -steps), min(count, count - steps))
    return lax.ppermute(value, axis, [(source, source + steps) for source in range(first, last)])


def rms_rows(values, gain):
    values = values.astype(jnp.float32)
    scale = lax.rsqrt(jnp.mean(values * values, axis=-1, keepdims=True) + epsilon)
    return values * scale * gain


def after(value, *earlier):
    return lax.optimization_barrier((value, *earlier))[0]


def whole_ref(array):
    return pl.BlockSpec(array.shape, lambda *_: (0,) * array.ndim)


def worth(microseconds):
    return pl.CostEstimate(
        flops=int(microseconds * 1.15e9), bytes_accessed=int(microseconds * 1e6), transcendentals=0
    )


def contract(a, b, dims, precision=None):
    return lax.dot_general(
        a, b, (dims, ((), ())), precision=precision, preferred_element_type=f32
    )


def parts(values):
    high = values.astype(bf16)
    return high, (values - high.astype(f32)).astype(bf16)


def contract_close(a, b):
    a_high, a_low = parts(a)
    b_high, b_low = parts(b)
    doubled = jnp.concatenate([a_high, a_low], axis=1)
    if 2 * b.shape[1] <= 2 * DK:
        both = jnp.concatenate([b_high, b_low], axis=1)
        product = contract(doubled, jnp.concatenate([both, both], axis=0), ((1,), (0,)))
        return product[:, : b.shape[1]] + product[:, b.shape[1] :]
    return contract(
        doubled, jnp.concatenate([b_high, b_high], axis=0), ((1,), (0,))
    ) + contract(a_high, b_low, ((1,), (0,)))


def contract_rows(a, b):
    a_high, a_low = parts(a)
    b_high, b_low = parts(b)
    product = contract(
        jnp.concatenate([a_high, a_low], axis=1),
        jnp.concatenate(
            [jnp.concatenate([b_high, b_high], axis=1), jnp.concatenate([b_low, b_low], axis=1)],
            axis=0,
        ),
        ((1,), (1,)),
    )
    return product[:, : b.shape[0]] + product[:, b.shape[0] :]


def pair_routes(cols, picker, lines, tok_rows, slots):
    rows = cols.shape[0]
    weight_rows = contract(picker, cols, ((1,), (1,)))
    named = weight_rows > 0
    before = lax.broadcasted_iota(jnp.int32, (rows, rows), 0)
    after = lax.broadcasted_iota(jnp.int32, (rows, rows), 1)
    earlier = (before < after) & (before // tok_rows == after // tok_rows)
    rank = contract(
        jnp.where(named, 1.0, 0.0).astype(bf16),
        jnp.where(earlier, 1.0, 0.0).astype(bf16),
        ((1,), (0,)),
    )
    first_slot = lax.broadcasted_iota(jnp.int32, rank.shape, 1) // tok_rows * slots
    rank = jnp.where(named, rank.astype(jnp.int32) + first_slot, -1)
    slot = lax.broadcasted_iota(jnp.int32, (rows // tok_rows * slots, rows), 0)
    picks = [jnp.where(slot == rank[line : line + 1], 1.0, 0.0) for line in range(lines)]
    return weight_rows, picks


def collect_kernel(block_00, block_10, block_01, block_11, picker_ref, own_ref, send_ref, *, slots):
    local_experts, taken, width = own_ref.shape
    tok_rows = block_00.shape[0]
    pair = taken // 2
    for at, pair_refs in enumerate(((block_01, block_11), (block_00, block_10))):
        rows = jnp.concatenate([ref[...] for ref in pair_refs], axis=0)
        _, picks = pair_routes(
            rows[:, width:], picker_ref[...], 2 * local_experts, tok_rows, slots
        )
        picked = contract(
            jnp.concatenate(picks, axis=0).astype(bf16), rows[:, :width], ((1,), (0,))
        ).astype(bf16)
        for expert in range(local_experts):
            there = slice(at * pair, (at + 1) * pair)
            own_ref[expert, there, :] = picked[expert * pair : (expert + 1) * pair]
            line = local_experts + expert
            send_ref[expert, there, :] = picked[line * pair : (line + 1) * pair]


def expert_kernel(*refs):
    *row_refs, gate_ref, up_ref, down_ref, own_ref, send_ref = refs
    half = len(row_refs) // 2
    for sources, out_ref in ((row_refs[half:], send_ref), (row_refs[:half], own_ref)):
        rows = jnp.concatenate([ref[0] for ref in sources], axis=0)
        gate = contract(rows, gate_ref[0], ((1,), (0,)))
        up = contract(rows, up_ref[0], ((1,), (0,)))
        hidden = (gate / (1.0 + jnp.exp(-gate)) * up).astype(bf16)
        out_ref[0] = contract(hidden, down_ref[0], ((1,), (0,))).astype(bf16)


def spread_kernel(
    cols_00, cols_10, cols_01, cols_11, picker_ref, own_ref, got_ref, far_ref, near_ref, here_ref, *, slots
):
    local_experts, taken, _ = own_ref.shape
    tok_rows = cols_00.shape[0]
    pair = taken // 2
    for at, pair_refs in enumerate(((cols_01, cols_11), (cols_00, cols_10))):
        cols = jnp.concatenate([ref[...] for ref in pair_refs], axis=0)
        weight_rows, picks = pair_routes(
            cols, picker_ref[...], 2 * local_experts, tok_rows, slots
        )
        scaled = []
        for line, pick in enumerate(picks):
            result_ref = (own_ref, got_ref)[line // local_experts]
            result = result_ref[line % local_experts, at * pair : (at + 1) * pair, :]
            weight = jnp.sum(pick * weight_rows[line : line + 1], axis=1, keepdims=True)
            scaled.append((result.astype(f32) * weight).astype(bf16))
        summed = contract(
            jnp.concatenate(picks, axis=0).astype(bf16),
            jnp.concatenate(scaled, axis=0),
            ((0,), (0,)),
        ).astype(bf16)
        if at == 0:
            far_ref[...] = summed
        else:
            here_ref[...] = summed[:tok_rows]
            near_ref[...] = summed[tok_rows:]


def expert_layer_gathered(
    stream,
    moe_gain,
    router,
    expert_ids,
    expert_gate,
    expert_up,
    expert_down,
    sources,
):
    tok_rows, width = stream.shape
    local_experts, _, hidden_width = expert_gate.shape
    experts_all = local_experts * sources
    depth = sources // 8
    place = lax.axis_index(("ctx", "head"))

    def sent(value, move):
        pairs = []
        for device in range(sources):
            z, y, x, core = device // 8, device // 4 % 2, device // 2 % 2, device % 2
            z, y, x, core = move(z, y, x, core)
            pairs.append((device, ((z * 2 + y) * 2 + x) * 2 + core))
        return lax.ppermute(value, ("ctx", "head"), pairs)

    def lifted(value, steps):
        return sent(value, lambda z, y, x, core: ((z + steps) % depth, y, x, core))

    def first(value):
        return sent(value, lambda z, y, x, core: (z, y ^ (1 - core), x ^ core, core))

    def second(value):
        return sent(value, lambda z, y, x, core: (z, y ^ core, x ^ (1 - core), core))

    def swapped(value):
        return sent(value, lambda z, y, x, core: (z, y, x, 1 - core))

    normed = rms_rows(stream, moe_gain).astype(bf16)
    logits = jnp.dot(normed, router, preferred_element_type=f32)
    named = jnp.any(
        expert_ids[:, :, None] == jnp.arange(experts_all, dtype=jnp.int32)[None, None, :], axis=1
    )
    raised = jnp.where(named, jnp.exp(logits), 0.0)
    weights = raised / jnp.sum(raised, axis=1, keepdims=True)
    coarse = lax.reduce_precision(weights, 8, 7)
    packet = jnp.concatenate(
        [normed, coarse.astype(bf16), (weights - coarse).astype(bf16)], axis=1
    )

    capacity = (11 * tok_rows * expert_ids.shape[1] + 10 * experts_all - 1) // (10 * experts_all)
    slots = -(-capacity // 8) * 8
    taken = 4 * slots
    column = jnp.arange(2 * experts_all, dtype=jnp.int32)[None, :] % experts_all
    line = jnp.arange(16, dtype=jnp.int32)[:, None]
    owner = jnp.where(line < local_experts, place, place ^ 1)
    picker = (
        (line < 2 * local_experts) & (column == owner * local_experts + line % local_experts)
    ).astype(bf16)

    blocks, own_rows, got_rows = [], [], []
    for steps in range(depth):
        mine = packet
        if steps == 1:
            mine = lifted(packet, steps)
        elif steps:
            mine, near, far, last = blocks[steps - 2]
            earlier = [blocks[steps - 1][0], near, far]
            if steps > 2:
                earlier += [blocks[steps - 3][3]]
            mine = lifted(after(packet, *earlier), steps)
        near = first(mine)
        blocks.append((mine, near, second(mine), second(near)))
    def collect(steps, *earlier):
        own, send = pl.pallas_call(
            functools.partial(collect_kernel, slots=slots),
            out_shape=[jax.ShapeDtypeStruct((local_experts, taken, width), bf16)] * 2,
            compiler_params=pltpu.CompilerParams(vmem_limit_bytes=48 << 20),
            cost_estimate=worth(2),
            name="collect",
        )(after(blocks[steps][0], *earlier), *blocks[steps][1:], picker)
        own_rows.append(own)
        got_rows.append(swapped(send))

    def run_experts(members, *earlier):
        row_spec = pl.BlockSpec((1, taken, width), lambda e: (e, 0, 0))
        out_spec = pl.BlockSpec((1, len(members) * taken, width), lambda e: (e, 0, 0))
        results, send_back = pl.pallas_call(
            expert_kernel,
            grid=(local_experts,),
            in_specs=[row_spec] * (2 * len(members))
            + [
                pl.BlockSpec((1, width, hidden_width), lambda e: (e, 0, 0)),
                pl.BlockSpec((1, width, hidden_width), lambda e: (e, 0, 0)),
                pl.BlockSpec((1, hidden_width, width), lambda e: (e, 0, 0)),
            ],
            out_specs=[out_spec] * 2,
            out_shape=[jax.ShapeDtypeStruct((local_experts, len(members) * taken, width), bf16)]
            * 2,
            compiler_params=pltpu.CompilerParams(vmem_limit_bytes=56 << 20),
            cost_estimate=worth(4 + 3 * len(members)),
            name="experts",
        )(
            after(own_rows[members[0]], *earlier),
            *[own_rows[member] for member in members[1:]],
            *[got_rows[member] for member in members],
            expert_gate,
            expert_up,
            expert_down,
        )
        got_back = swapped(send_back)
        for at, member in enumerate(members):
            outcome[member] = (at, results, got_back)

    def spread(steps):
        at, results, got_back = outcome[steps]
        result_spec = pl.BlockSpec((local_experts, taken, width), lambda g: (0, at, 0))
        cols_spec = pl.BlockSpec(
            (tok_rows, 2 * experts_all), lambda g: (0, width // (2 * experts_all))
        )
        row_shape = jax.ShapeDtypeStruct((tok_rows, width), bf16)
        far_shape = jax.ShapeDtypeStruct((2 * tok_rows, width), bf16)
        return pl.pallas_call(
            functools.partial(spread_kernel, slots=slots),
            grid=(1,),
            in_specs=[cols_spec] * 4 + [whole_ref(picker), result_spec, result_spec],
            out_specs=[whole_ref(far_shape), whole_ref(row_shape), whole_ref(row_shape)],
            out_shape=[far_shape, row_shape, row_shape],
            compiler_params=pltpu.CompilerParams(vmem_limit_bytes=48 << 20),
            cost_estimate=worth(3),
            name="spread",
        )(*blocks[steps], picker, results, got_back)

    back = [*range(depth - 2, 0, -1), depth - 1, 0]
    outcome = {}
    for steps in range(depth - 1):
        collect(steps, blocks[-1][0])
    run_experts(range(depth - 1), blocks[-1][1], blocks[-1][2])
    ready = [spread(steps) for steps in back[: depth - 2]]
    collect(depth - 1, *[far for far, _, _ in ready])
    run_experts([depth - 1])
    ready += [spread(steps) for steps in back[depth - 2 :]]
    landed = []
    total = 0.0
    for at, steps in enumerate(back):
        far, near, here = ready[at]
        across = second(far)
        if at >= 2:
            across = after(across, landed[at - 2])
        across = across.astype(f32)
        near = first((near.astype(f32) + across[tok_rows:]).astype(bf16))
        if at >= 2 and steps:
            near = after(near, landed[at - 1])
        here = here.astype(f32) + across[:tok_rows] + near.astype(f32)
        if steps:
            landed.append(lifted(here.astype(bf16), -steps))
            here = landed[-1].astype(f32)
        total += here
    return total.astype(bf16)


def expert_layer_sent(
    stream, moe_gain, router, expert_ids, expert_gate, expert_up, expert_down, sources
):
    tok_rows, model_width = stream.shape
    top_count = expert_ids.shape[1]
    local_experts = expert_gate.shape[0]
    experts_all = local_experts * sources
    capacity = (11 * tok_rows * top_count + 10 * experts_all - 1) // (10 * experts_all)
    normed = rms_rows(stream, moe_gain).astype(jnp.bfloat16)
    logits = jnp.dot(normed, router, preferred_element_type=jnp.float32)
    chosen = jnp.take_along_axis(logits, expert_ids, axis=1)
    raised = jnp.exp(chosen)
    weights = raised / jnp.sum(raised, axis=1, keepdims=True)
    flat_ids = expert_ids.reshape(-1)
    matches = (flat_ids[:, None] == jnp.arange(experts_all, dtype=jnp.int32)[None, :]).astype(
        jnp.int32
    )
    slot_index = jnp.sum((jnp.cumsum(matches, axis=0) - 1) * matches, axis=1)
    places = flat_ids * capacity + slot_index
    token_rows = jnp.arange(tok_rows * top_count, dtype=jnp.int32) // top_count
    outgoing = (
        jnp.zeros((experts_all * capacity, model_width), jnp.bfloat16)
        .at[places]
        .set(normed[token_rows])
    )
    outgoing = outgoing.reshape(sources, local_experts, capacity, model_width)
    received = lax.all_to_all(outgoing, ("ctx", "head"), split_axis=0, concat_axis=0, tiled=True)
    gate_part = jnp.einsum(
        "nesd,edh->nesh", received, expert_gate, preferred_element_type=jnp.float32
    )
    up_part = jnp.einsum("nesd,edh->nesh", received, expert_up, preferred_element_type=jnp.float32)
    hidden = (jax.nn.silu(gate_part) * up_part).astype(jnp.bfloat16)
    returned = lax.all_to_all(
        jnp.einsum(
            "nesh,ehd->nesd", hidden, expert_down, preferred_element_type=jnp.float32
        ).astype(jnp.bfloat16),
        ("ctx", "head"),
        split_axis=0,
        concat_axis=0,
        tiled=True,
    )
    gathered_rows = returned.reshape(experts_all * capacity, model_width)[places].reshape(
        tok_rows, top_count, model_width
    )
    return jnp.sum(weights[:, :, None] * gathered_rows.astype(jnp.float32), axis=1).astype(
        jnp.bfloat16
    )


def unit_inverses(strict_parts):
    size = strict_parts[0].shape[0]
    row = lax.broadcasted_iota(jnp.int32, (size, size), 0)
    col = lax.broadcasted_iota(jnp.int32, (size, size), 1)
    unit = jnp.where(row == col, 1.0, 0.0)
    joining = (row // 2 == col // 2) & (row != col)
    inverses = [unit - jnp.where(joining, part, 0.0) for part in strict_parts]
    half = 2
    while half < size:
        joining = (row // (2 * half) == col // (2 * half)) & (row // half != col // half)
        corners = [jnp.where(joining, part, 0.0) for part in strict_parts]
        if half < 8:
            steps = [contract_close(c, inverse) for c, inverse in zip(corners, inverses)]
            moves = [contract_close(inverse, step) for inverse, step in zip(inverses, steps)]
            inverses = [inverse - move for inverse, move in zip(inverses, moves)]
        else:
            starts = range(0, size, 2 * half)

            def lower_rows(array):
                return jnp.concatenate([array[at + half : at + 2 * half] for at in starts], axis=0)

            zeros = jnp.zeros((half, size), f32)
            steps = [
                contract_close(lower_rows(c), inverse) for c, inverse in zip(corners, inverses)
            ]
            steps = [
                jnp.concatenate(
                    [
                        piece
                        for at in range(0, size // 2, half)
                        for piece in (zeros, step[at : at + half])
                    ],
                    axis=0,
                )
                for step in steps
            ]
            lowers = [lower_rows(inverse) for inverse in inverses]
            lowers = [lower - contract_close(lower, step) for lower, step in zip(lowers, steps)]
            inverses = [
                jnp.concatenate(
                    [
                        piece
                        for at in starts
                        for piece in (
                            inverse[at : at + half],
                            lower[at // 2 : at // 2 + half],
                        )
                    ],
                    axis=0,
                )
                for inverse, lower in zip(inverses, lowers)
            ]
        half *= 2
    return inverses


def unit_rows(rows):
    return rows * lax.rsqrt(jnp.sum(rows * rows, axis=-1, keepdims=True) + epsilon)


def delta_kernel(
    raw_ref,
    rim_ref,
    taps_ref,
    beta_ref,
    decay_ref,
    rate_ref,
    core_ref,
    reading_ref,
    moved_ref,
    extended,
    mixed,
    strengths,
    falls,
    carried,
    *,
    key_heads,
    chunk,
):
    rows, conv_cols = raw_ref.shape
    heads = moved_ref.shape[0]
    group = heads // key_heads
    tap_count = taps_ref.shape[0]
    rim = rim_ref.shape[0]
    extended[0:rim, :] = rim_ref[...]
    extended[rim : rim + rows, :] = raw_ref[...].astype(f32)
    key_at, value_at = key_heads * DK, 2 * key_heads * DK
    for start in range(0, rows, chunk):
        for first in range(0, conv_cols, DK):
            columns = slice(first, first + DK)
            summed = jnp.zeros((chunk, DK), f32)
            for tap in range(tap_count):
                offset = rim - (tap_count - 1) + start + tap
                summed += taps_ref[tap : tap + 1, columns] * extended[
                    offset : offset + chunk, columns
                ]
            value = summed / (1.0 + jnp.exp(-summed))
            if first < key_at:
                value = unit_rows(value) * DK**-0.5
            elif first < value_at:
                value = unit_rows(value)
            mixed[start : start + chunk, columns] = value
    beta = beta_ref[...]
    strengths[...] = 1.0 / (1.0 + jnp.exp(-beta))
    shifted = decay_ref[...] + rate_ref[1:2, :]
    softened = jnp.maximum(shifted, 0.0) + jnp.log1p(jnp.exp(-jnp.abs(shifted)))
    falls[...] = -jnp.exp(rate_ref[0:1, :]) * softened

    row = lax.broadcasted_iota(jnp.int32, (chunk, chunk), 0)
    col = lax.broadcasted_iota(jnp.int32, (chunk, chunk), 1)
    inclusive, strict = row >= col, row > col
    lower = jnp.where(inclusive, 1.0, 0.0)
    across = lax.broadcasted_iota(jnp.int32, (DK, 2 * DK), 1)
    down = lax.broadcasted_iota(jnp.int32, (DK, 2 * DK), 0)
    carried[...] = jnp.broadcast_to(
        jnp.where(across == down + DK, 1.0, 0.0)[None], carried.shape
    )

    def advance(step, nothing):
        here = pl.ds(pl.multiple_of(step * chunk, chunk), chunk)
        fall = falls[here, :]
        strength = strengths[here, :]
        cumulative = contract(lower, fall, ((1,), (0,)), lax.Precision.HIGHEST)
        cumulative_rows = contract(fall, lower, ((0,), (1,)), lax.Precision.HIGHEST)
        owners = range(heads)
        queries = [mixed[here, k * DK : (k + 1) * DK] for k in range(key_heads)]
        keys = [mixed[here, key_at + k * DK : key_at + (k + 1) * DK] for k in range(key_heads)]
        dots = [
            contract_rows(jnp.concatenate([key, query], axis=0), key)
            for key, query in zip(keys, queries)
        ]
        totals = [cumulative[:, head : head + 1] for head in owners]
        kept = [
            jnp.where(
                inclusive,
                jnp.exp(jnp.where(inclusive, totals[head] - cumulative_rows[head : head + 1, :], 0.0)),
                0.0,
            )
            for head in owners
        ]
        own = [strength[:, head : head + 1] for head in owners]
        solvers = unit_inverses(
            [
                own[head] * jnp.where(strict, kept[head], 0.0) * dots[head // group][:chunk]
                for head in owners
            ]
        )
        risen = [jnp.exp(total) for total in totals]
        solved = [
            contract_close(
                solvers[head],
                own[head]
                * jnp.concatenate(
                    [
                        mixed[here, value_at + head * DK : value_at + (head + 1) * DK],
                        risen[head] * keys[head // group],
                    ],
                    axis=1,
                ),
            )
            for head in owners
        ]
        states = [carried[head] for head in owners]
        read = [
            contract_close(
                jnp.concatenate(
                    [solved[head][:, DK:], risen[head] * queries[head // group]], axis=0
                ),
                states[head],
            )
            for head in owners
        ]
        updates = [
            jnp.concatenate([solved[head][:, :DK], jnp.zeros((chunk, DK), f32)], axis=1)
            - read[head][:chunk]
            for head in owners
        ]
        for head in owners:
            last = totals[head][chunk - 1 :, :]
            leaving = jnp.exp(last - totals[head]) * keys[head // group]
            carried[head] = jnp.exp(last) * states[head] + contract_close(
                leaving.T, updates[head]
            )
        for head in owners:
            result = read[head][chunk:] + contract_close(
                kept[head] * dots[head // group][chunk:], updates[head]
            )
            core_ref[here, head * DK : (head + 1) * DK] = result[:, :DK]
            reading_ref[here, head * DK : (head + 1) * DK] = result[:, DK:]
        return nothing

    lax.fori_loop(0, rows // chunk, advance, 0)
    moved_ref[...] = carried[...].astype(bf16)


def finish_kernel(
    place_ref, moved_ref, core_ref, reading_ref, gate_ref, gain_ref, gated_ref
):
    heads = moved_ref.shape[1]

    def join(earlier, states):
        return tuple(
            contract_close(moved_ref[earlier, head, :, DK:].astype(f32), state)
            + moved_ref[earlier, head, :, :DK].astype(f32)
            for head, state in enumerate(states)
        )

    states = lax.fori_loop(
        0, place_ref[0], join, tuple(jnp.zeros((DK, DK), f32) for _ in range(heads))
    )
    for head, state in enumerate(states):
        columns = slice(head * DK, (head + 1) * DK)
        core = core_ref[:, columns] + contract_close(reading_ref[:, columns], state)
        normal = (
            core
            * lax.rsqrt(jnp.mean(core * core, axis=-1, keepdims=True) + epsilon)
            * gain_ref[...]
        )
        gate = gate_ref[:, columns].astype(f32)
        gated_ref[:, columns] = (normal * (gate / (1.0 + jnp.exp(-gate)))).astype(bf16)


def output_kernel(*refs):
    *pairs, out_ref = refs
    half = len(pairs) // 2
    out_ref[...] = sum(
        contract(rows_ref[...], weight_ref[...], ((1,), (0,)))
        for rows_ref, weight_ref in zip(pairs[:half], pairs[half:])
    ).astype(bf16)


def on_device(
    stream,
    moe_gain,
    router,
    expert_ids,
    expert_gate,
    expert_up,
    expert_down,
    mixer_gain,
    query_weight,
    key_weight,
    value_weight,
    output_gate,
    beta_weight,
    decay_weight,
    query_conv,
    key_conv,
    value_conv,
    decay_log,
    decay_bias,
    head_gain,
    out_weight,
):
    ctx_count = lax.axis_size("ctx")
    head_count = lax.axis_size("head")
    sources = ctx_count * head_count
    ctx_place = lax.axis_index("ctx")
    experts = (stream, moe_gain, router, expert_ids, expert_gate, expert_up, expert_down)
    if 2 * sources * stream.size <= GATHER_LIMIT and head_count == 4 and ctx_count % 2 == 0:
        moe_out = expert_layer_gathered(*experts, sources)
    else:
        moe_out = expert_layer_sent(*experts, sources)
    mixer_in = rms_rows(
        stream.astype(jnp.float32) + moe_out.astype(jnp.float32), mixer_gain
    ).astype(jnp.bfloat16)
    piece_rows = lax.all_gather(mixer_in, "head", axis=0, tiled=True)

    def project(*matrices):
        return jnp.concatenate(
            [jnp.dot(piece_rows, matrix, preferred_element_type=f32) for matrix in matrices], axis=1
        )

    qkv_raw = project(query_weight, key_weight, value_weight).astype(bf16)
    gate_raw = project(output_gate).astype(bf16)
    beta_raw = project(beta_weight)
    decay_raw = project(decay_weight)
    rows, conv_cols = qkv_raw.shape
    key_heads = query_weight.shape[1] // DK
    heads = beta_weight.shape[1]
    value_cols = value_weight.shape[1]
    taps = jnp.concatenate([query_conv, key_conv, value_conv], axis=1)
    rim_len = taps.shape[0] - 1
    rim = passed_along(qkv_raw[rows - rim_len :], "ctx", 1)
    rim = jnp.concatenate([jnp.zeros((8 - rim_len, conv_cols), f32), rim.astype(f32)], axis=0)
    rates = jnp.stack([decay_log, decay_bias])
    chunk = math.gcd(rows, CHUNK)
    core, reading, moved = pl.pallas_call(
        functools.partial(delta_kernel, key_heads=key_heads, chunk=chunk),
        out_shape=(
            jax.ShapeDtypeStruct((rows, value_cols), f32),
            jax.ShapeDtypeStruct((rows, value_cols), f32),
            jax.ShapeDtypeStruct((heads, DK, 2 * DK), bf16),
        ),
        scratch_shapes=[
            pltpu.VMEM((rows + 8, conv_cols), f32),
            pltpu.VMEM((rows, conv_cols), f32),
            pltpu.VMEM((rows, heads), f32),
            pltpu.VMEM((rows, heads), f32),
            pltpu.VMEM((heads, DK, 2 * DK), f32),
        ],
        compiler_params=pltpu.CompilerParams(vmem_limit_bytes=48 << 20),
        cost_estimate=worth(16),
        name="delta",
    )(qkv_raw, rim, taps, beta_raw, decay_raw, rates)
    everything = lax.all_gather(moved, "ctx")

    def turned(value, step):
        pairs = [(source, (source + step) % head_count) for source in range(head_count)]
        return lax.ppermute(value, "head", pairs) if step else value

    early = after(out_weight, piece_rows)
    weight_parts = [out_weight] + [turned(early, step) for step in range(1, head_count)]
    in_vmem = pl.BlockSpec(memory_space=pltpu.VMEM)
    gated = pl.pallas_call(
        finish_kernel,
        in_specs=[pl.BlockSpec(memory_space=pltpu.SMEM)] + [in_vmem] * 5,
        out_shape=jax.ShapeDtypeStruct((rows, value_cols), bf16),
        compiler_params=pltpu.CompilerParams(vmem_limit_bytes=48 << 20),
        name="finish",
    )(
        ctx_place.reshape(1),
        everything,
        core,
        reading,
        gate_raw,
        head_gain.reshape(1, -1),
    )
    tok_rows = stream.shape[0]
    head_place = lax.axis_index("head")
    gated_parts = []
    for step in range(head_count):
        goal = (head_place + step) % head_count
        part = lax.dynamic_slice_in_dim(gated, goal * tok_rows, tok_rows, axis=0)
        gated_parts.append(turned(part, step))
    mixer_out = pl.pallas_call(
        output_kernel,
        out_shape=jax.ShapeDtypeStruct(stream.shape, bf16),
        compiler_params=pltpu.CompilerParams(vmem_limit_bytes=48 << 20),
        name="output",
    )(*gated_parts, *weight_parts)
    return (moe_out, mixer_out)


def solution(mesh):
    return jax.shard_map(
        on_device,
        mesh=mesh,
        in_specs=(
            P(("ctx", "head"), None),
            P(),
            P(),
            P(("ctx", "head"), None),
            P(("ctx", "head"), None, None),
            P(("ctx", "head"), None, None),
            P(("ctx", "head"), None, None),
            P(),
            P(None, "head"),
            P(None, "head"),
            P(None, "head"),
            P(None, "head"),
            P(None, "head"),
            P(None, "head"),
            P(None, "head"),
            P(None, "head"),
            P(None, "head"),
            P("head"),
            P("head"),
            P(),
            P("head", None),
        ),
        out_specs=(P(("ctx", "head"), None), P(("ctx", "head"), None)),
        check_vma=False,
    )
```

```python
import functools
import math

import jax
import jax.numpy as jnp
from jax import lax
from jax.experimental import pallas as pl
from jax.experimental.pallas import tpu as pltpu
from jax.sharding import PartitionSpec as P

DK = 128
CHUNK = 128
GATHER_LIMIT = 32 << 20


epsilon = 1e-06
f32 = jnp.float32
bf16 = jnp.bfloat16


def passed_along(value, axis, steps):
    count = lax.axis_size(axis)
    first, last = (max(0, -steps), min(count, count - steps))
    return lax.ppermute(value, axis, [(source, source + steps) for source in range(first, last)])


def rms_rows(values, gain):
    values = values.astype(jnp.float32)
    scale = lax.rsqrt(jnp.mean(values * values, axis=-1, keepdims=True) + epsilon)
    return values * scale * gain


def after(value, *earlier):
    return lax.optimization_barrier((value, *earlier))[0]


def whole_ref(array):
    return pl.BlockSpec(array.shape, lambda *_: (0,) * array.ndim)


def worth(microseconds):
    return pl.CostEstimate(
        flops=int(microseconds * 1.15e9), bytes_accessed=int(microseconds * 1e6), transcendentals=0
    )


def contract(a, b, dims, precision=None):
    return lax.dot_general(
        a, b, (dims, ((), ())), precision=precision, preferred_element_type=f32
    )


def parts(values):
    high = values.astype(bf16)
    return high, (values - high.astype(f32)).astype(bf16)


def contract_close(a, b):
    a_high, a_low = parts(a)
    b_high, b_low = parts(b)
    doubled = jnp.concatenate([a_high, a_low], axis=1)
    if 2 * b.shape[1] <= 2 * DK:
        both = jnp.concatenate([b_high, b_low], axis=1)
        product = contract(doubled, jnp.concatenate([both, both], axis=0), ((1,), (0,)))
        return product[:, : b.shape[1]] + product[:, b.shape[1] :]
    return contract(
        doubled, jnp.concatenate([b_high, b_high], axis=0), ((1,), (0,))
    ) + contract(a_high, b_low, ((1,), (0,)))


def contract_rows(a, b):
    a_high, a_low = parts(a)
    b_high, b_low = parts(b)
    product = contract(
        jnp.concatenate([a_high, a_low], axis=1),
        jnp.concatenate(
            [jnp.concatenate([b_high, b_high], axis=1), jnp.concatenate([b_low, b_low], axis=1)],
            axis=0,
        ),
        ((1,), (1,)),
    )
    return product[:, : b.shape[0]] + product[:, b.shape[0] :]


def pair_routes(cols, picker, lines, tok_rows, slots):
    rows = cols.shape[0]
    weight_rows = contract(picker, cols, ((1,), (1,)))
    named = weight_rows > 0
    before = lax.broadcasted_iota(jnp.int32, (rows, rows), 0)
    after = lax.broadcasted_iota(jnp.int32, (rows, rows), 1)
    earlier = (before < after) & (before // tok_rows == after // tok_rows)
    rank = contract(
        jnp.where(named, 1.0, 0.0).astype(bf16),
        jnp.where(earlier, 1.0, 0.0).astype(bf16),
        ((1,), (0,)),
    )
    first_slot = lax.broadcasted_iota(jnp.int32, rank.shape, 1) // tok_rows * slots
    rank = jnp.where(named, rank.astype(jnp.int32) + first_slot, -1)
    slot = lax.broadcasted_iota(jnp.int32, (rows // tok_rows * slots, rows), 0)
    picks = [jnp.where(slot == rank[line : line + 1], 1.0, 0.0) for line in range(lines)]
    return weight_rows, picks


def collect_kernel(block_00, block_10, block_01, block_11, picker_ref, own_ref, send_ref, *, slots):
    local_experts, taken, width = own_ref.shape
    tok_rows = block_00.shape[0]
    pair = taken // 2
    for at, pair_refs in enumerate(((block_01, block_11), (block_00, block_10))):
        rows = jnp.concatenate([ref[...] for ref in pair_refs], axis=0)
        _, picks = pair_routes(
            rows[:, width:], picker_ref[...], 2 * local_experts, tok_rows, slots
        )
        picked = contract(
            jnp.concatenate(picks, axis=0).astype(bf16), rows[:, :width], ((1,), (0,))
        ).astype(bf16)
        for expert in range(local_experts):
            there = slice(at * pair, (at + 1) * pair)
            own_ref[expert, there, :] = picked[expert * pair : (expert + 1) * pair]
            line = local_experts + expert
            send_ref[expert, there, :] = picked[line * pair : (line + 1) * pair]


def expert_kernel(*refs):
    *row_refs, gate_ref, up_ref, down_ref, own_ref, send_ref = refs
    half = len(row_refs) // 2
    for sources, out_ref in ((row_refs[half:], send_ref), (row_refs[:half], own_ref)):
        rows = jnp.concatenate([ref[0] for ref in sources], axis=0)
        gate = contract(rows, gate_ref[0], ((1,), (0,)))
        up = contract(rows, up_ref[0], ((1,), (0,)))
        hidden = (gate / (1.0 + jnp.exp(-gate)) * up).astype(bf16)
        out_ref[0] = contract(hidden, down_ref[0], ((1,), (0,))).astype(bf16)


def spread_kernel(
    cols_00, cols_10, cols_01, cols_11, picker_ref, own_ref, got_ref, far_ref, near_ref, here_ref, *, slots
):
    local_experts, taken, _ = own_ref.shape
    tok_rows = cols_00.shape[0]
    pair = taken // 2
    for at, pair_refs in enumerate(((cols_01, cols_11), (cols_00, cols_10))):
        cols = jnp.concatenate([ref[...] for ref in pair_refs], axis=0)
        weight_rows, picks = pair_routes(
            cols, picker_ref[...], 2 * local_experts, tok_rows, slots
        )
        scaled = []
        for line, pick in enumerate(picks):
            result_ref = (own_ref, got_ref)[line // local_experts]
            result = result_ref[line % local_experts, at * pair : (at + 1) * pair, :]
            weight = jnp.sum(pick * weight_rows[line : line + 1], axis=1, keepdims=True)
            scaled.append((result.astype(f32) * weight).astype(bf16))
        summed = contract(
            jnp.concatenate(picks, axis=0).astype(bf16),
            jnp.concatenate(scaled, axis=0),
            ((0,), (0,)),
        ).astype(bf16)
        if at == 0:
            far_ref[...] = summed
        else:
            here_ref[...] = summed[:tok_rows]
            near_ref[...] = summed[tok_rows:]


def expert_layer_gathered(
    stream,
    moe_gain,
    router,
    expert_ids,
    expert_gate,
    expert_up,
    expert_down,
    sources,
):
    tok_rows, width = stream.shape
    local_experts, _, hidden_width = expert_gate.shape
    experts_all = local_experts * sources
    depth = sources // 8
    place = lax.axis_index(("ctx", "head"))

    def sent(value, move):
        pairs = []
        for device in range(sources):
            z, y, x, core = device // 8, device // 4 % 2, device // 2 % 2, device % 2
            z, y, x, core = move(z, y, x, core)
            pairs.append((device, ((z * 2 + y) * 2 + x) * 2 + core))
        return lax.ppermute(value, ("ctx", "head"), pairs)

    def lifted(value, steps):
        return sent(value, lambda z, y, x, core: ((z + steps) % depth, y, x, core))

    def first(value):
        return sent(value, lambda z, y, x, core: (z, y ^ (1 - core), x ^ core, core))

    def second(value):
        return sent(value, lambda z, y, x, core: (z, y ^ core, x ^ (1 - core), core))

    def swapped(value):
        return sent(value, lambda z, y, x, core: (z, y, x, 1 - core))

    normed = rms_rows(stream, moe_gain).astype(bf16)
    logits = jnp.dot(normed, router, preferred_element_type=f32)
    named = jnp.any(
        expert_ids[:, :, None] == jnp.arange(experts_all, dtype=jnp.int32)[None, None, :], axis=1
    )
    raised = jnp.where(named, jnp.exp(logits), 0.0)
    weights = raised / jnp.sum(raised, axis=1, keepdims=True)
    coarse = lax.reduce_precision(weights, 8, 7)
    packet = jnp.concatenate(
        [normed, coarse.astype(bf16), (weights - coarse).astype(bf16)], axis=1
    )

    capacity = (11 * tok_rows * expert_ids.shape[1] + 10 * experts_all - 1) // (10 * experts_all)
    slots = -(-capacity // 8) * 8
    taken = 4 * slots
    column = jnp.arange(2 * experts_all, dtype=jnp.int32)[None, :] % experts_all
    line = jnp.arange(16, dtype=jnp.int32)[:, None]
    owner = jnp.where(line < local_experts, place, place ^ 1)
    picker = (
        (line < 2 * local_experts) & (column == owner * local_experts + line % local_experts)
    ).astype(bf16)

    order = [0, *range(depth - 1, 0, -1)]
    own_rows, got_rows, outcome = {}, {}, {}
    blocks = {}
    mine = packet
    for at, steps in enumerate(order):
        if steps:
            source = packet if steps == 1 else mine
            earlier = [blocks[order[at - 1]][0]] if at > 1 else []
            if at > 1:
                earlier += blocks[order[at - 2]][1:3]
            if at > 2:
                earlier += blocks[order[at - 3]][3:]
            if earlier:
                source = after(source, *earlier)
            mine = lifted(source, 1 if steps == 1 else -1)
        near = first(mine)
        blocks[steps] = (mine, near, second(mine), second(near))

    def collect(steps, *earlier):
        own, send = pl.pallas_call(
            functools.partial(collect_kernel, slots=slots),
            out_shape=[jax.ShapeDtypeStruct((local_experts, taken, width), bf16)] * 2,
            compiler_params=pltpu.CompilerParams(vmem_limit_bytes=48 << 20),
            cost_estimate=worth(2),
            name="collect",
        )(after(blocks[steps][0], *earlier), *blocks[steps][1:], picker)
        own_rows[steps] = own
        got_rows[steps] = swapped(send)

    def run_experts(members, *earlier):
        row_spec = pl.BlockSpec((1, taken, width), lambda e: (e, 0, 0))
        out_spec = pl.BlockSpec((1, len(members) * taken, width), lambda e: (e, 0, 0))
        results, send_back = pl.pallas_call(
            expert_kernel,
            grid=(local_experts,),
            in_specs=[row_spec] * (2 * len(members))
            + [
                pl.BlockSpec((1, width, hidden_width), lambda e: (e, 0, 0)),
                pl.BlockSpec((1, width, hidden_width), lambda e: (e, 0, 0)),
                pl.BlockSpec((1, hidden_width, width), lambda e: (e, 0, 0)),
            ],
            out_specs=[out_spec] * 2,
            out_shape=[jax.ShapeDtypeStruct((local_experts, len(members) * taken, width), bf16)]
            * 2,
            compiler_params=pltpu.CompilerParams(vmem_limit_bytes=56 << 20),
            cost_estimate=worth(4 + 3 * len(members)),
            name="experts",
        )(
            after(own_rows[members[0]], *earlier),
            *[own_rows[member] for member in members[1:]],
            *[got_rows[member] for member in members],
            expert_gate,
            expert_up,
            expert_down,
        )
        got_back = swapped(send_back)
        for at, member in enumerate(members):
            outcome[member] = (at, results, got_back)

    def spread(steps):
        at, results, got_back = outcome[steps]
        result_spec = pl.BlockSpec((local_experts, taken, width), lambda g: (0, at, 0))
        cols_spec = pl.BlockSpec(
            (tok_rows, 2 * experts_all), lambda g: (0, width // (2 * experts_all))
        )
        row_shape = jax.ShapeDtypeStruct((tok_rows, width), bf16)
        far_shape = jax.ShapeDtypeStruct((2 * tok_rows, width), bf16)
        return pl.pallas_call(
            functools.partial(spread_kernel, slots=slots),
            grid=(1,),
            in_specs=[cols_spec] * 4 + [whole_ref(picker), result_spec, result_spec],
            out_specs=[whole_ref(far_shape), whole_ref(row_shape), whole_ref(row_shape)],
            out_shape=[far_shape, row_shape, row_shape],
            compiler_params=pltpu.CompilerParams(vmem_limit_bytes=48 << 20),
            cost_estimate=worth(3),
            name="spread",
        )(*blocks[steps], picker, results, got_back)

    last = order[-1]
    for steps in order[:-1]:
        collect(steps, blocks[last][0])
    run_experts(order[:-1], blocks[last][1], blocks[last][2])
    back = order[-2:0:-1]
    ready = {steps: spread(steps) for steps in back}
    collect(last, *[far for far, _, _ in ready.values()])
    run_experts([last])
    back += [last, 0]
    carried = {}
    total = 0.0
    for at, steps in enumerate(back):
        far, near, here = ready[steps] if steps in ready else spread(steps)
        across = second(far)
        if at >= 2 and back[at - 2] in carried:
            across = after(across, carried[back[at - 2]])
        across = across.astype(f32)
        near = first((near.astype(f32) + across[tok_rows:]).astype(bf16))
        here = here.astype(f32) + across[:tok_rows] + near.astype(f32)
        if steps > 2:
            here += carried.pop(steps - 1).astype(f32)
        if steps:
            carried[steps] = lifted(here.astype(bf16), -1 if steps == 1 else 1)
        else:
            total = here
    for arrived in carried.values():
        total += arrived.astype(f32)
    return total.astype(bf16)


def expert_layer_sent(
    stream, moe_gain, router, expert_ids, expert_gate, expert_up, expert_down, sources
):
    tok_rows, model_width = stream.shape
    top_count = expert_ids.shape[1]
    local_experts = expert_gate.shape[0]
    experts_all = local_experts * sources
    capacity = (11 * tok_rows * top_count + 10 * experts_all - 1) // (10 * experts_all)
    normed = rms_rows(stream, moe_gain).astype(jnp.bfloat16)
    logits = jnp.dot(normed, router, preferred_element_type=jnp.float32)
    chosen = jnp.take_along_axis(logits, expert_ids, axis=1)
    raised = jnp.exp(chosen)
    weights = raised / jnp.sum(raised, axis=1, keepdims=True)
    flat_ids = expert_ids.reshape(-1)
    matches = (flat_ids[:, None] == jnp.arange(experts_all, dtype=jnp.int32)[None, :]).astype(
        jnp.int32
    )
    slot_index = jnp.sum((jnp.cumsum(matches, axis=0) - 1) * matches, axis=1)
    places = flat_ids * capacity + slot_index
    token_rows = jnp.arange(tok_rows * top_count, dtype=jnp.int32) // top_count
    outgoing = (
        jnp.zeros((experts_all * capacity, model_width), jnp.bfloat16)
        .at[places]
        .set(normed[token_rows])
    )
    outgoing = outgoing.reshape(sources, local_experts, capacity, model_width)
    received = lax.all_to_all(outgoing, ("ctx", "head"), split_axis=0, concat_axis=0, tiled=True)
    gate_part = jnp.einsum(
        "nesd,edh->nesh", received, expert_gate, preferred_element_type=jnp.float32
    )
    up_part = jnp.einsum("nesd,edh->nesh", received, expert_up, preferred_element_type=jnp.float32)
    hidden = (jax.nn.silu(gate_part) * up_part).astype(jnp.bfloat16)
    returned = lax.all_to_all(
        jnp.einsum(
            "nesh,ehd->nesd", hidden, expert_down, preferred_element_type=jnp.float32
        ).astype(jnp.bfloat16),
        ("ctx", "head"),
        split_axis=0,
        concat_axis=0,
        tiled=True,
    )
    gathered_rows = returned.reshape(experts_all * capacity, model_width)[places].reshape(
        tok_rows, top_count, model_width
    )
    return jnp.sum(weights[:, :, None] * gathered_rows.astype(jnp.float32), axis=1).astype(
        jnp.bfloat16
    )


def unit_inverses(strict_parts):
    size = strict_parts[0].shape[0]
    row = lax.broadcasted_iota(jnp.int32, (size, size), 0)
    col = lax.broadcasted_iota(jnp.int32, (size, size), 1)
    unit = jnp.where(row == col, 1.0, 0.0)
    joining = (row // 2 == col // 2) & (row != col)
    inverses = [unit - jnp.where(joining, part, 0.0) for part in strict_parts]
    half = 2
    while half < size:
        joining = (row // (2 * half) == col // (2 * half)) & (row // half != col // half)
        corners = [jnp.where(joining, part, 0.0) for part in strict_parts]
        if half < 8:
            steps = [contract_close(c, inverse) for c, inverse in zip(corners, inverses)]
            moves = [contract_close(inverse, step) for inverse, step in zip(inverses, steps)]
            inverses = [inverse - move for inverse, move in zip(inverses, moves)]
        else:
            starts = range(0, size, 2 * half)

            def lower_rows(array):
                return jnp.concatenate([array[at + half : at + 2 * half] for at in starts], axis=0)

            zeros = jnp.zeros((half, size), f32)
            steps = [
                contract_close(lower_rows(c), inverse) for c, inverse in zip(corners, inverses)
            ]
            steps = [
                jnp.concatenate(
                    [
                        piece
                        for at in range(0, size // 2, half)
                        for piece in (zeros, step[at : at + half])
                    ],
                    axis=0,
                )
                for step in steps
            ]
            lowers = [lower_rows(inverse) for inverse in inverses]
            lowers = [lower - contract_close(lower, step) for lower, step in zip(lowers, steps)]
            inverses = [
                jnp.concatenate(
                    [
                        piece
                        for at in starts
                        for piece in (
                            inverse[at : at + half],
                            lower[at // 2 : at // 2 + half],
                        )
                    ],
                    axis=0,
                )
                for inverse, lower in zip(inverses, lowers)
            ]
        half *= 2
    return inverses


def unit_rows(rows):
    return rows * lax.rsqrt(jnp.sum(rows * rows, axis=-1, keepdims=True) + epsilon)


def delta_kernel(
    raw_ref,
    rim_ref,
    taps_ref,
    beta_ref,
    decay_ref,
    rate_ref,
    core_ref,
    reading_ref,
    moved_ref,
    extended,
    mixed,
    strengths,
    falls,
    carried,
    *,
    key_heads,
    chunk,
):
    rows, conv_cols = raw_ref.shape
    heads = moved_ref.shape[0]
    group = heads // key_heads
    tap_count = taps_ref.shape[0]
    rim = rim_ref.shape[0]
    extended[0:rim, :] = rim_ref[...]
    extended[rim : rim + rows, :] = raw_ref[...].astype(f32)
    key_at, value_at = key_heads * DK, 2 * key_heads * DK
    for start in range(0, rows, chunk):
        for first in range(0, conv_cols, DK):
            columns = slice(first, first + DK)
            summed = jnp.zeros((chunk, DK), f32)
            for tap in range(tap_count):
                offset = rim - (tap_count - 1) + start + tap
                summed += taps_ref[tap : tap + 1, columns] * extended[
                    offset : offset + chunk, columns
                ]
            value = summed / (1.0 + jnp.exp(-summed))
            if first < key_at:
                value = unit_rows(value) * DK**-0.5
            elif first < value_at:
                value = unit_rows(value)
            mixed[start : start + chunk, columns] = value
    beta = beta_ref[...]
    strengths[...] = 1.0 / (1.0 + jnp.exp(-beta))
    shifted = decay_ref[...] + rate_ref[1:2, :]
    softened = jnp.maximum(shifted, 0.0) + jnp.log1p(jnp.exp(-jnp.abs(shifted)))
    falls[...] = -jnp.exp(rate_ref[0:1, :]) * softened

    row = lax.broadcasted_iota(jnp.int32, (chunk, chunk), 0)
    col = lax.broadcasted_iota(jnp.int32, (chunk, chunk), 1)
    inclusive, strict = row >= col, row > col
    lower = jnp.where(inclusive, 1.0, 0.0)
    across = lax.broadcasted_iota(jnp.int32, (DK, 2 * DK), 1)
    down = lax.broadcasted_iota(jnp.int32, (DK, 2 * DK), 0)
    carried[...] = jnp.broadcast_to(
        jnp.where(across == down + DK, 1.0, 0.0)[None], carried.shape
    )

    def advance(step, nothing):
        here = pl.ds(pl.multiple_of(step * chunk, chunk), chunk)
        fall = falls[here, :]
        strength = strengths[here, :]
        cumulative = contract(lower, fall, ((1,), (0,)), lax.Precision.HIGHEST)
        cumulative_rows = contract(fall, lower, ((0,), (1,)), lax.Precision.HIGHEST)
        owners = range(heads)
        queries = [mixed[here, k * DK : (k + 1) * DK] for k in range(key_heads)]
        keys = [mixed[here, key_at + k * DK : key_at + (k + 1) * DK] for k in range(key_heads)]
        dots = [
            contract_rows(jnp.concatenate([key, query], axis=0), key)
            for key, query in zip(keys, queries)
        ]
        totals = [cumulative[:, head : head + 1] for head in owners]
        kept = [
            jnp.where(
                inclusive,
                jnp.exp(jnp.where(inclusive, totals[head] - cumulative_rows[head : head + 1, :], 0.0)),
                0.0,
            )
            for head in owners
        ]
        own = [strength[:, head : head + 1] for head in owners]
        solvers = unit_inverses(
            [
                own[head] * jnp.where(strict, kept[head], 0.0) * dots[head // group][:chunk]
                for head in owners
            ]
        )
        risen = [jnp.exp(total) for total in totals]
        solved = [
            contract_close(
                solvers[head],
                own[head]
                * jnp.concatenate(
                    [
                        mixed[here, value_at + head * DK : value_at + (head + 1) * DK],
                        risen[head] * keys[head // group],
                    ],
                    axis=1,
                ),
            )
            for head in owners
        ]
        states = [carried[head] for head in owners]
        read = [
            contract_close(
                jnp.concatenate(
                    [solved[head][:, DK:], risen[head] * queries[head // group]], axis=0
                ),
                states[head],
            )
            for head in owners
        ]
        updates = [
            jnp.concatenate([solved[head][:, :DK], jnp.zeros((chunk, DK), f32)], axis=1)
            - read[head][:chunk]
            for head in owners
        ]
        for head in owners:
            last = totals[head][chunk - 1 :, :]
            leaving = jnp.exp(last - totals[head]) * keys[head // group]
            carried[head] = jnp.exp(last) * states[head] + contract_close(
                leaving.T, updates[head]
            )
        for head in owners:
            result = read[head][chunk:] + contract_close(
                kept[head] * dots[head // group][chunk:], updates[head]
            )
            core_ref[here, head * DK : (head + 1) * DK] = result[:, :DK]
            reading_ref[here, head * DK : (head + 1) * DK] = result[:, DK:]
        return nothing

    lax.fori_loop(0, rows // chunk, advance, 0)
    moved_ref[...] = carried[...].astype(bf16)


def finish_kernel(
    place_ref, moved_ref, core_ref, reading_ref, gate_ref, gain_ref, gated_ref
):
    heads = moved_ref.shape[1]

    def join(earlier, states):
        return tuple(
            contract_close(moved_ref[earlier, head, :, DK:].astype(f32), state)
            + moved_ref[earlier, head, :, :DK].astype(f32)
            for head, state in enumerate(states)
        )

    states = lax.fori_loop(
        0, place_ref[0], join, tuple(jnp.zeros((DK, DK), f32) for _ in range(heads))
    )
    for head, state in enumerate(states):
        columns = slice(head * DK, (head + 1) * DK)
        core = core_ref[:, columns] + contract_close(reading_ref[:, columns], state)
        normal = (
            core
            * lax.rsqrt(jnp.mean(core * core, axis=-1, keepdims=True) + epsilon)
            * gain_ref[...]
        )
        gate = gate_ref[:, columns].astype(f32)
        gated_ref[:, columns] = (normal * (gate / (1.0 + jnp.exp(-gate)))).astype(bf16)


def output_kernel(*refs):
    *pairs, out_ref = refs
    half = len(pairs) // 2
    out_ref[...] = sum(
        contract(rows_ref[...], weight_ref[...], ((1,), (0,)))
        for rows_ref, weight_ref in zip(pairs[:half], pairs[half:])
    ).astype(bf16)


def on_device(
    stream,
    moe_gain,
    router,
    expert_ids,
    expert_gate,
    expert_up,
    expert_down,
    mixer_gain,
    query_weight,
    key_weight,
    value_weight,
    output_gate,
    beta_weight,
    decay_weight,
    query_conv,
    key_conv,
    value_conv,
    decay_log,
    decay_bias,
    head_gain,
    out_weight,
):
    ctx_count = lax.axis_size("ctx")
    head_count = lax.axis_size("head")
    sources = ctx_count * head_count
    ctx_place = lax.axis_index("ctx")
    experts = (stream, moe_gain, router, expert_ids, expert_gate, expert_up, expert_down)
    if 2 * sources * stream.size <= GATHER_LIMIT and head_count == 4 and ctx_count in (6, 8):
        moe_out = expert_layer_gathered(*experts, sources)
    else:
        moe_out = expert_layer_sent(*experts, sources)
    mixer_in = rms_rows(
        stream.astype(jnp.float32) + moe_out.astype(jnp.float32), mixer_gain
    ).astype(jnp.bfloat16)
    piece_rows = lax.all_gather(mixer_in, "head", axis=0, tiled=True)

    def project(*matrices):
        return jnp.concatenate(
            [jnp.dot(piece_rows, matrix, preferred_element_type=f32) for matrix in matrices], axis=1
        )

    qkv_raw = project(query_weight, key_weight, value_weight).astype(bf16)
    gate_raw = project(output_gate).astype(bf16)
    beta_raw = project(beta_weight)
    decay_raw = project(decay_weight)
    rows, conv_cols = qkv_raw.shape
    key_heads = query_weight.shape[1] // DK
    heads = beta_weight.shape[1]
    value_cols = value_weight.shape[1]
    taps = jnp.concatenate([query_conv, key_conv, value_conv], axis=1)
    rim_len = taps.shape[0] - 1
    rim = passed_along(qkv_raw[rows - rim_len :], "ctx", 1)
    rim = jnp.concatenate([jnp.zeros((8 - rim_len, conv_cols), f32), rim.astype(f32)], axis=0)
    rates = jnp.stack([decay_log, decay_bias])
    chunk = math.gcd(rows, CHUNK)
    core, reading, moved = pl.pallas_call(
        functools.partial(delta_kernel, key_heads=key_heads, chunk=chunk),
        out_shape=(
            jax.ShapeDtypeStruct((rows, value_cols), f32),
            jax.ShapeDtypeStruct((rows, value_cols), f32),
            jax.ShapeDtypeStruct((heads, DK, 2 * DK), bf16),
        ),
        scratch_shapes=[
            pltpu.VMEM((rows + 8, conv_cols), f32),
            pltpu.VMEM((rows, conv_cols), f32),
            pltpu.VMEM((rows, heads), f32),
            pltpu.VMEM((rows, heads), f32),
            pltpu.VMEM((heads, DK, 2 * DK), f32),
        ],
        compiler_params=pltpu.CompilerParams(vmem_limit_bytes=48 << 20),
        cost_estimate=worth(16),
        name="delta",
    )(qkv_raw, rim, taps, beta_raw, decay_raw, rates)
    everything = lax.all_gather(moved, "ctx")

    def crossed(value, step):
        pairs = [(source, source ^ step) for source in range(head_count)]
        return lax.ppermute(value, "head", pairs)

    early = after(out_weight, piece_rows)
    weight_parts = [out_weight, crossed(early, 1)]
    for step in range(2, head_count, 2):
        weight_parts.append(crossed(early, step))
        weight_parts.append(crossed(after(weight_parts[-1], everything), 1))
    in_vmem = pl.BlockSpec(memory_space=pltpu.VMEM)
    gated = pl.pallas_call(
        finish_kernel,
        in_specs=[pl.BlockSpec(memory_space=pltpu.SMEM)] + [in_vmem] * 5,
        out_shape=jax.ShapeDtypeStruct((rows, value_cols), bf16),
        compiler_params=pltpu.CompilerParams(vmem_limit_bytes=48 << 20),
        name="finish",
    )(
        ctx_place.reshape(1),
        everything,
        core,
        reading,
        gate_raw,
        head_gain.reshape(1, -1),
    )
    tok_rows = stream.shape[0]
    head_place = lax.axis_index("head")
    gated_parts = []
    for step in range(head_count):
        goal = head_place ^ step
        part = lax.dynamic_slice_in_dim(gated, goal * tok_rows, tok_rows, axis=0)
        gated_parts.append(crossed(part, step) if step else part)
    mixer_out = pl.pallas_call(
        output_kernel,
        out_shape=jax.ShapeDtypeStruct(stream.shape, bf16),
        compiler_params=pltpu.CompilerParams(vmem_limit_bytes=48 << 20),
        name="output",
    )(*gated_parts, *weight_parts)
    return (moe_out, mixer_out)


def solution(mesh):
    return jax.shard_map(
        on_device,
        mesh=mesh,
        in_specs=(
            P(("ctx", "head"), None),
            P(),
            P(),
            P(("ctx", "head"), None),
            P(("ctx", "head"), None, None),
            P(("ctx", "head"), None, None),
            P(("ctx", "head"), None, None),
            P(),
            P(None, "head"),
            P(None, "head"),
            P(None, "head"),
            P(None, "head"),
            P(None, "head"),
            P(None, "head"),
            P(None, "head"),
            P(None, "head"),
            P(None, "head"),
            P("head"),
            P("head"),
            P(),
            P("head", None),
        ),
        out_specs=(P(("ctx", "head"), None), P(("ctx", "head"), None)),
        check_vma=False,
    )
```

```python
import functools
import math

import jax
import jax.numpy as jnp
from jax import lax
from jax.experimental import pallas as pl
from jax.experimental.pallas import tpu as pltpu
from jax.sharding import PartitionSpec as P

DK = 128
CHUNK = 128
GATHER_LIMIT = 32 << 20


epsilon = 1e-06
f32 = jnp.float32
bf16 = jnp.bfloat16


def passed_along(value, axis, steps):
    count = lax.axis_size(axis)
    first, last = (max(0, -steps), min(count, count - steps))
    return lax.ppermute(value, axis, [(source, source + steps) for source in range(first, last)])


def rms_rows(values, gain):
    values = values.astype(jnp.float32)
    scale = lax.rsqrt(jnp.mean(values * values, axis=-1, keepdims=True) + epsilon)
    return values * scale * gain


def after(value, *earlier):
    return lax.optimization_barrier((value, *earlier))[0]


def whole_ref(array):
    return pl.BlockSpec(array.shape, lambda *_: (0,) * array.ndim)


def worth(microseconds):
    return pl.CostEstimate(
        flops=int(microseconds * 1.15e9), bytes_accessed=int(microseconds * 1e6), transcendentals=0
    )


def contract(a, b, dims, precision=None):
    return lax.dot_general(
        a, b, (dims, ((), ())), precision=precision, preferred_element_type=f32
    )


def parts(values):
    high = values.astype(bf16)
    return high, (values - high.astype(f32)).astype(bf16)


def contract_close(a, b):
    a_high, a_low = parts(a)
    b_high, b_low = parts(b)
    doubled = jnp.concatenate([a_high, a_low], axis=1)
    if 2 * b.shape[1] <= 2 * DK:
        both = jnp.concatenate([b_high, b_low], axis=1)
        product = contract(doubled, jnp.concatenate([both, both], axis=0), ((1,), (0,)))
        return product[:, : b.shape[1]] + product[:, b.shape[1] :]
    return contract(
        doubled, jnp.concatenate([b_high, b_high], axis=0), ((1,), (0,))
    ) + contract(a_high, b_low, ((1,), (0,)))


def contract_rows(a, b):
    a_high, a_low = parts(a)
    b_high, b_low = parts(b)
    product = contract(
        jnp.concatenate([a_high, a_low], axis=1),
        jnp.concatenate(
            [jnp.concatenate([b_high, b_high], axis=1), jnp.concatenate([b_low, b_low], axis=1)],
            axis=0,
        ),
        ((1,), (1,)),
    )
    return product[:, : b.shape[0]] + product[:, b.shape[0] :]


def pair_routes(cols, picker, lines, tok_rows, slots):
    rows = cols.shape[0]
    weight_rows = contract(picker, cols, ((1,), (1,)))
    named = weight_rows > 0
    before = lax.broadcasted_iota(jnp.int32, (rows, rows), 0)
    after = lax.broadcasted_iota(jnp.int32, (rows, rows), 1)
    earlier = (before < after) & (before // tok_rows == after // tok_rows)
    rank = contract(
        jnp.where(named, 1.0, 0.0).astype(bf16),
        jnp.where(earlier, 1.0, 0.0).astype(bf16),
        ((1,), (0,)),
    )
    first_slot = lax.broadcasted_iota(jnp.int32, rank.shape, 1) // tok_rows * slots
    rank = jnp.where(named, rank.astype(jnp.int32) + first_slot, -1)
    slot = lax.broadcasted_iota(jnp.int32, (rows // tok_rows * slots, rows), 0)
    picks = [jnp.where(slot == rank[line : line + 1], 1.0, 0.0) for line in range(lines)]
    return weight_rows, picks


def collect_kernel(block_00, block_10, block_01, block_11, picker_ref, own_ref, send_ref, *, slots):
    local_experts, taken, width = own_ref.shape
    tok_rows = block_00.shape[0]
    pair = taken // 2
    for at, pair_refs in enumerate(((block_01, block_11), (block_00, block_10))):
        rows = jnp.concatenate([ref[...] for ref in pair_refs], axis=0)
        _, picks = pair_routes(
            rows[:, width:], picker_ref[...], 2 * local_experts, tok_rows, slots
        )
        picked = contract(
            jnp.concatenate(picks, axis=0).astype(bf16), rows[:, :width], ((1,), (0,))
        ).astype(bf16)
        for expert in range(local_experts):
            there = slice(at * pair, (at + 1) * pair)
            own_ref[expert, there, :] = picked[expert * pair : (expert + 1) * pair]
            line = local_experts + expert
            send_ref[expert, there, :] = picked[line * pair : (line + 1) * pair]


def expert_kernel(*refs):
    *row_refs, gate_ref, up_ref, down_ref, own_ref, send_ref = refs
    half = len(row_refs) // 2
    for sources, out_ref in ((row_refs[half:], send_ref), (row_refs[:half], own_ref)):
        rows = jnp.concatenate([ref[0] for ref in sources], axis=0)
        gate = contract(rows, gate_ref[0], ((1,), (0,)))
        up = contract(rows, up_ref[0], ((1,), (0,)))
        hidden = (gate / (1.0 + jnp.exp(-gate)) * up).astype(bf16)
        out_ref[0] = contract(hidden, down_ref[0], ((1,), (0,))).astype(bf16)


def spread_kernel(
    cols_00, cols_10, cols_01, cols_11, picker_ref, own_ref, got_ref, far_ref, near_ref, here_ref, *, slots
):
    local_experts, taken, _ = own_ref.shape
    tok_rows = cols_00.shape[0]
    pair = taken // 2
    for at, pair_refs in enumerate(((cols_01, cols_11), (cols_00, cols_10))):
        cols = jnp.concatenate([ref[...] for ref in pair_refs], axis=0)
        weight_rows, picks = pair_routes(
            cols, picker_ref[...], 2 * local_experts, tok_rows, slots
        )
        scaled = []
        for line, pick in enumerate(picks):
            result_ref = (own_ref, got_ref)[line // local_experts]
            result = result_ref[line % local_experts, at * pair : (at + 1) * pair, :]
            weight = jnp.sum(pick * weight_rows[line : line + 1], axis=1, keepdims=True)
            scaled.append((result.astype(f32) * weight).astype(bf16))
        summed = contract(
            jnp.concatenate(picks, axis=0).astype(bf16),
            jnp.concatenate(scaled, axis=0),
            ((0,), (0,)),
        ).astype(bf16)
        if at == 0:
            far_ref[...] = summed
        else:
            here_ref[...] = summed[:tok_rows]
            near_ref[...] = summed[tok_rows:]


def expert_layer_gathered(
    stream,
    moe_gain,
    router,
    expert_ids,
    expert_gate,
    expert_up,
    expert_down,
    sources,
):
    tok_rows, width = stream.shape
    local_experts, _, hidden_width = expert_gate.shape
    experts_all = local_experts * sources
    depth = sources // 8
    place = lax.axis_index(("ctx", "head"))

    def sent(value, move):
        pairs = []
        for device in range(sources):
            z, y, x, core = device // 8, device // 4 % 2, device // 2 % 2, device % 2
            z, y, x, core = move(z, y, x, core)
            pairs.append((device, ((z * 2 + y) * 2 + x) * 2 + core))
        return lax.ppermute(value, ("ctx", "head"), pairs)

    def lifted(value, steps):
        return sent(value, lambda z, y, x, core: ((z + steps) % depth, y, x, core))

    def first(value):
        return sent(value, lambda z, y, x, core: (z, y ^ (1 - core), x ^ core, core))

    def second(value):
        return sent(value, lambda z, y, x, core: (z, y ^ core, x ^ (1 - core), core))

    def swapped(value):
        return sent(value, lambda z, y, x, core: (z, y, x, 1 - core))

    normed = rms_rows(stream, moe_gain).astype(bf16)
    logits = jnp.dot(normed, router, preferred_element_type=f32)
    named = jnp.any(
        expert_ids[:, :, None] == jnp.arange(experts_all, dtype=jnp.int32)[None, None, :], axis=1
    )
    raised = jnp.where(named, jnp.exp(logits), 0.0)
    weights = raised / jnp.sum(raised, axis=1, keepdims=True)
    coarse = lax.reduce_precision(weights, 8, 7)
    packet = jnp.concatenate(
        [normed, coarse.astype(bf16), (weights - coarse).astype(bf16)], axis=1
    )

    capacity = (11 * tok_rows * expert_ids.shape[1] + 10 * experts_all - 1) // (10 * experts_all)
    slots = -(-capacity // 8) * 8
    taken = 4 * slots
    column = jnp.arange(2 * experts_all, dtype=jnp.int32)[None, :] % experts_all
    line = jnp.arange(16, dtype=jnp.int32)[:, None]
    owner = jnp.where(line < local_experts, place, place ^ 1)
    picker = (
        (line < 2 * local_experts) & (column == owner * local_experts + line % local_experts)
    ).astype(bf16)

    order = [0, *range(depth - 1, 0, -1)]
    own_rows, got_rows, outcome = {}, {}, {}
    blocks = {}
    mine = packet
    for at, steps in enumerate(order):
        if steps:
            source = packet if steps == 1 else mine
            earlier = [blocks[order[at - 1]][0]] if at > 1 else []
            if at > 1:
                earlier += blocks[order[at - 2]][1:3]
            if earlier:
                source = after(source, *earlier)
            mine = lifted(source, 1 if steps == 1 else -1)
        near = first(mine)
        blocks[steps] = (mine, near, second(mine), second(near))

    def collect(steps, *earlier):
        rows = blocks[steps][0]
        own, send = pl.pallas_call(
            functools.partial(collect_kernel, slots=slots),
            out_shape=[jax.ShapeDtypeStruct((local_experts, taken, width), bf16)] * 2,
            compiler_params=pltpu.CompilerParams(vmem_limit_bytes=48 << 20),
            cost_estimate=worth(2),
            name="collect",
        )(after(rows, *earlier) if earlier else rows, *blocks[steps][1:], picker)
        own_rows[steps] = own
        got_rows[steps] = swapped(send)

    def run_experts(members, *earlier):
        row_spec = pl.BlockSpec((1, taken, width), lambda e: (e, 0, 0))
        out_spec = pl.BlockSpec((1, len(members) * taken, width), lambda e: (e, 0, 0))
        results, send_back = pl.pallas_call(
            expert_kernel,
            grid=(local_experts,),
            in_specs=[row_spec] * (2 * len(members))
            + [
                pl.BlockSpec((1, width, hidden_width), lambda e: (e, 0, 0)),
                pl.BlockSpec((1, width, hidden_width), lambda e: (e, 0, 0)),
                pl.BlockSpec((1, hidden_width, width), lambda e: (e, 0, 0)),
            ],
            out_specs=[out_spec] * 2,
            out_shape=[jax.ShapeDtypeStruct((local_experts, len(members) * taken, width), bf16)]
            * 2,
            compiler_params=pltpu.CompilerParams(vmem_limit_bytes=56 << 20),
            cost_estimate=worth(4 + 3 * len(members)),
            name="experts",
        )(
            after(own_rows[members[0]], *earlier),
            *[own_rows[member] for member in members[1:]],
            *[got_rows[member] for member in members],
            expert_gate,
            expert_up,
            expert_down,
        )
        got_back = swapped(send_back)
        for at, member in enumerate(members):
            outcome[member] = (at, results, got_back)

    def spread(steps):
        at, results, got_back = outcome[steps]
        result_spec = pl.BlockSpec((local_experts, taken, width), lambda g: (0, at, 0))
        cols_spec = pl.BlockSpec(
            (tok_rows, 2 * experts_all), lambda g: (0, width // (2 * experts_all))
        )
        row_shape = jax.ShapeDtypeStruct((tok_rows, width), bf16)
        far_shape = jax.ShapeDtypeStruct((2 * tok_rows, width), bf16)
        return pl.pallas_call(
            functools.partial(spread_kernel, slots=slots),
            grid=(1,),
            in_specs=[cols_spec] * 4 + [whole_ref(picker), result_spec, result_spec],
            out_specs=[whole_ref(far_shape), whole_ref(row_shape), whole_ref(row_shape)],
            out_shape=[far_shape, row_shape, row_shape],
            compiler_params=pltpu.CompilerParams(vmem_limit_bytes=48 << 20),
            cost_estimate=worth(3),
            name="spread",
        )(*blocks[steps], picker, results, got_back)

    last = order[-1]
    for steps in order[:-2]:
        collect(steps, blocks[order[-2]][0])
    collect(order[-2])
    run_experts(order[:-1], blocks[last][1], blocks[last][2])
    back = order[-2:0:-1]
    ready = {steps: spread(steps) for steps in back}
    collect(last, *[far for far, _, _ in ready.values()])
    run_experts([last])
    back += [last, 0]
    carried = {}
    total = 0.0
    for at, steps in enumerate(back):
        far, near, here = ready[steps] if steps in ready else spread(steps)
        across = second(far)
        if at == 0:
            across = after(across, outcome[last][1])
        if at >= 2 and back[at - 2] in carried:
            across = after(across, carried[back[at - 2]])
        across = across.astype(f32)
        near = first((near.astype(f32) + across[tok_rows:]).astype(bf16))
        here = here.astype(f32) + across[:tok_rows] + near.astype(f32)
        if steps > 2:
            here += carried.pop(steps - 1).astype(f32)
        if steps:
            carried[steps] = lifted(here.astype(bf16), -1 if steps == 1 else 1)
        else:
            total = here
    for arrived in carried.values():
        total += arrived.astype(f32)
    return total.astype(bf16)


def expert_layer_sent(
    stream, moe_gain, router, expert_ids, expert_gate, expert_up, expert_down, sources
):
    tok_rows, model_width = stream.shape
    top_count = expert_ids.shape[1]
    local_experts = expert_gate.shape[0]
    experts_all = local_experts * sources
    capacity = (11 * tok_rows * top_count + 10 * experts_all - 1) // (10 * experts_all)
    normed = rms_rows(stream, moe_gain).astype(jnp.bfloat16)
    logits = jnp.dot(normed, router, preferred_element_type=jnp.float32)
    chosen = jnp.take_along_axis(logits, expert_ids, axis=1)
    raised = jnp.exp(chosen)
    weights = raised / jnp.sum(raised, axis=1, keepdims=True)
    flat_ids = expert_ids.reshape(-1)
    matches = (flat_ids[:, None] == jnp.arange(experts_all, dtype=jnp.int32)[None, :]).astype(
        jnp.int32
    )
    slot_index = jnp.sum((jnp.cumsum(matches, axis=0) - 1) * matches, axis=1)
    places = flat_ids * capacity + slot_index
    token_rows = jnp.arange(tok_rows * top_count, dtype=jnp.int32) // top_count
    outgoing = (
        jnp.zeros((experts_all * capacity, model_width), jnp.bfloat16)
        .at[places]
        .set(normed[token_rows])
    )
    outgoing = outgoing.reshape(sources, local_experts, capacity, model_width)
    received = lax.all_to_all(outgoing, ("ctx", "head"), split_axis=0, concat_axis=0, tiled=True)
    gate_part = jnp.einsum(
        "nesd,edh->nesh", received, expert_gate, preferred_element_type=jnp.float32
    )
    up_part = jnp.einsum("nesd,edh->nesh", received, expert_up, preferred_element_type=jnp.float32)
    hidden = (jax.nn.silu(gate_part) * up_part).astype(jnp.bfloat16)
    returned = lax.all_to_all(
        jnp.einsum(
            "nesh,ehd->nesd", hidden, expert_down, preferred_element_type=jnp.float32
        ).astype(jnp.bfloat16),
        ("ctx", "head"),
        split_axis=0,
        concat_axis=0,
        tiled=True,
    )
    gathered_rows = returned.reshape(experts_all * capacity, model_width)[places].reshape(
        tok_rows, top_count, model_width
    )
    return jnp.sum(weights[:, :, None] * gathered_rows.astype(jnp.float32), axis=1).astype(
        jnp.bfloat16
    )


def unit_inverses(strict_parts):
    size = strict_parts[0].shape[0]
    row = lax.broadcasted_iota(jnp.int32, (size, size), 0)
    col = lax.broadcasted_iota(jnp.int32, (size, size), 1)
    unit = jnp.where(row == col, 1.0, 0.0)
    joining = (row // 2 == col // 2) & (row != col)
    inverses = [unit - jnp.where(joining, part, 0.0) for part in strict_parts]
    half = 2
    while half < size:
        joining = (row // (2 * half) == col // (2 * half)) & (row // half != col // half)
        corners = [jnp.where(joining, part, 0.0) for part in strict_parts]
        if half < 8:
            steps = [contract_close(c, inverse) for c, inverse in zip(corners, inverses)]
            moves = [contract_close(inverse, step) for inverse, step in zip(inverses, steps)]
            inverses = [inverse - move for inverse, move in zip(inverses, moves)]
        else:
            starts = range(0, size, 2 * half)

            def lower_rows(array):
                return jnp.concatenate([array[at + half : at + 2 * half] for at in starts], axis=0)

            zeros = jnp.zeros((half, size), f32)
            steps = [
                contract_close(lower_rows(c), inverse) for c, inverse in zip(corners, inverses)
            ]
            steps = [
                jnp.concatenate(
                    [
                        piece
                        for at in range(0, size // 2, half)
                        for piece in (zeros, step[at : at + half])
                    ],
                    axis=0,
                )
                for step in steps
            ]
            lowers = [lower_rows(inverse) for inverse in inverses]
            lowers = [lower - contract_close(lower, step) for lower, step in zip(lowers, steps)]
            inverses = [
                jnp.concatenate(
                    [
                        piece
                        for at in starts
                        for piece in (
                            inverse[at : at + half],
                            lower[at // 2 : at // 2 + half],
                        )
                    ],
                    axis=0,
                )
                for inverse, lower in zip(inverses, lowers)
            ]
        half *= 2
    return inverses


def unit_rows(rows):
    return rows * lax.rsqrt(jnp.sum(rows * rows, axis=-1, keepdims=True) + epsilon)


def delta_kernel(
    raw_ref,
    rim_ref,
    taps_ref,
    small_ref,
    rate_ref,
    core_ref,
    reading_ref,
    moved_ref,
    extended,
    mixed,
    strengths,
    falls,
    carried,
    *,
    key_heads,
    chunk,
):
    rows, conv_cols = raw_ref.shape
    heads = moved_ref.shape[0]
    group = heads // key_heads
    tap_count = taps_ref.shape[0]
    rim = rim_ref.shape[0]
    extended[0:rim, :] = rim_ref[...]
    extended[rim : rim + rows, :] = raw_ref[...].astype(f32)
    key_at, value_at = key_heads * DK, 2 * key_heads * DK
    for start in range(0, rows, chunk):
        for first in range(0, conv_cols, DK):
            columns = slice(first, first + DK)
            summed = jnp.zeros((chunk, DK), f32)
            for tap in range(tap_count):
                offset = rim - (tap_count - 1) + start + tap
                summed += taps_ref[tap : tap + 1, columns] * extended[
                    offset : offset + chunk, columns
                ]
            value = summed / (1.0 + jnp.exp(-summed))
            if first < key_at:
                value = unit_rows(value) * DK**-0.5
            elif first < value_at:
                value = unit_rows(value)
            mixed[start : start + chunk, columns] = value
    strengths[...] = 1.0 / (1.0 + jnp.exp(-small_ref[:, :heads]))
    shifted = small_ref[:, heads:] + rate_ref[1:2, :]
    softened = jnp.maximum(shifted, 0.0) + jnp.log1p(jnp.exp(-jnp.abs(shifted)))
    falls[...] = -jnp.exp(rate_ref[0:1, :]) * softened

    row = lax.broadcasted_iota(jnp.int32, (chunk, chunk), 0)
    col = lax.broadcasted_iota(jnp.int32, (chunk, chunk), 1)
    inclusive, strict = row >= col, row > col
    lower = jnp.where(inclusive, 1.0, 0.0)
    across = lax.broadcasted_iota(jnp.int32, (DK, 2 * DK), 1)
    down = lax.broadcasted_iota(jnp.int32, (DK, 2 * DK), 0)
    carried[...] = jnp.broadcast_to(
        jnp.where(across == down + DK, 1.0, 0.0)[None], carried.shape
    )

    def advance(step, nothing):
        here = pl.ds(pl.multiple_of(step * chunk, chunk), chunk)
        fall = falls[here, :]
        strength = strengths[here, :]
        cumulative = contract(lower, fall, ((1,), (0,)), lax.Precision.HIGHEST)
        cumulative_rows = contract(fall, lower, ((0,), (1,)), lax.Precision.HIGHEST)
        owners = range(heads)
        queries = [mixed[here, k * DK : (k + 1) * DK] for k in range(key_heads)]
        keys = [mixed[here, key_at + k * DK : key_at + (k + 1) * DK] for k in range(key_heads)]
        dots = [
            contract_rows(jnp.concatenate([key, query], axis=0), key)
            for key, query in zip(keys, queries)
        ]
        totals = [cumulative[:, head : head + 1] for head in owners]
        kept = [
            jnp.where(
                inclusive,
                jnp.exp(jnp.where(inclusive, totals[head] - cumulative_rows[head : head + 1, :], 0.0)),
                0.0,
            )
            for head in owners
        ]
        own = [strength[:, head : head + 1] for head in owners]
        solvers = unit_inverses(
            [
                own[head] * jnp.where(strict, kept[head], 0.0) * dots[head // group][:chunk]
                for head in owners
            ]
        )
        risen = [jnp.exp(total) for total in totals]
        solved = [
            contract_close(
                solvers[head],
                own[head]
                * jnp.concatenate(
                    [
                        mixed[here, value_at + head * DK : value_at + (head + 1) * DK],
                        risen[head] * keys[head // group],
                    ],
                    axis=1,
                ),
            )
            for head in owners
        ]
        states = [carried[head] for head in owners]
        read = [
            contract_close(
                jnp.concatenate(
                    [solved[head][:, DK:], risen[head] * queries[head // group]], axis=0
                ),
                states[head],
            )
            for head in owners
        ]
        updates = [
            jnp.concatenate([solved[head][:, :DK], jnp.zeros((chunk, DK), f32)], axis=1)
            - read[head][:chunk]
            for head in owners
        ]
        for head in owners:
            last = totals[head][chunk - 1 :, :]
            leaving = jnp.exp(last - totals[head]) * keys[head // group]
            carried[head] = jnp.exp(last) * states[head] + contract_close(
                leaving.T, updates[head]
            )
        for head in owners:
            result = read[head][chunk:] + contract_close(
                kept[head] * dots[head // group][chunk:], updates[head]
            )
            core_ref[here, head * DK : (head + 1) * DK] = result[:, :DK]
            reading_ref[here, head * DK : (head + 1) * DK] = result[:, DK:]
        return nothing

    lax.fori_loop(0, rows // chunk, advance, 0)
    moved_ref[...] = carried[...].astype(bf16)


def project_kernel(place_ref, *refs, blocks):
    piece_refs, weight_refs, out_refs = refs[:blocks], refs[blocks : -3], refs[-3:]
    qkv_ref, gate_ref, small_ref = out_refs
    rows = jnp.concatenate([ref[...] for ref in piece_refs], axis=0)
    tok_rows = piece_refs[0].shape[0]

    def store(out_ref, first, weight_ref):
        product = contract(rows, weight_ref[...], ((1,), (0,))).astype(out_ref.dtype)
        for step in range(blocks):
            at = pl.multiple_of((place_ref[0] ^ step) * tok_rows, tok_rows)
            out_ref[pl.ds(at, tok_rows), first : first + product.shape[1]] = product[
                step * tok_rows : (step + 1) * tok_rows
            ]

    first = 0
    for weight_ref in weight_refs[:3]:
        store(qkv_ref, first, weight_ref)
        first += weight_ref.shape[1]
    store(gate_ref, 0, weight_refs[3])
    store(small_ref, 0, weight_refs[4])


def pair_kernel(second_ref, mine_ref, other_ref, moved_ref, transfer_ref):
    for head in range(mine_ref.shape[0]):
        mine, other = mine_ref[head].astype(f32), other_ref[head].astype(f32)
        late = second_ref[0] == 1
        earlier = jnp.where(late, other, mine).astype(bf16)
        later = jnp.where(late, mine, other)
        joined = contract(later[:, DK:].astype(bf16), earlier, ((1,), (0,)))
        moved_ref[head] = (joined[:, :DK] + later[:, :DK]).astype(bf16)
        transfer_ref[head] = joined[:, DK:].astype(bf16)


def finish_kernel(
    second_ref, state_ref, other_ref, core_ref, reading_ref, gate_ref, gain_ref, gated_ref
):
    states = []
    for head in range(state_ref.shape[0]):
        state = state_ref[head]
        passed = contract(other_ref[head, :, DK:], state, ((1,), (0,))) + other_ref[
            head, :, :DK
        ].astype(f32)
        states.append(jnp.where(second_ref[0] == 1, passed, state.astype(f32)))
    for head, state in enumerate(states):
        columns = slice(head * DK, (head + 1) * DK)
        core = core_ref[:, columns] + contract_close(reading_ref[:, columns], state)
        normal = (
            core
            * lax.rsqrt(jnp.mean(core * core, axis=-1, keepdims=True) + epsilon)
            * gain_ref[...]
        )
        gate = gate_ref[:, columns].astype(f32)
        gated_ref[:, columns] = (normal * (gate / (1.0 + jnp.exp(-gate)))).astype(bf16)


def output_kernel(*refs, blocks):
    row_refs, weight_refs, out_ref = refs[:blocks], refs[blocks:-1], refs[-1]
    total = 0.0
    pieces = iter(weight_refs)
    for rows_ref in row_refs:
        at = 0
        while at < rows_ref.shape[1]:
            weight_ref = next(pieces)
            depth = weight_ref.shape[0]
            total += contract(rows_ref[:, at : at + depth], weight_ref[...], ((1,), (0,)))
            at += depth
    out_ref[...] = total.astype(bf16)


def on_device(
    stream,
    moe_gain,
    router,
    expert_ids,
    expert_gate,
    expert_up,
    expert_down,
    mixer_gain,
    query_weight,
    key_weight,
    value_weight,
    output_gate,
    beta_weight,
    decay_weight,
    query_conv,
    key_conv,
    value_conv,
    decay_log,
    decay_bias,
    head_gain,
    out_weight,
):
    ctx_count = lax.axis_size("ctx")
    head_count = lax.axis_size("head")
    sources = ctx_count * head_count
    ctx_place = lax.axis_index("ctx")
    experts = (stream, moe_gain, router, expert_ids, expert_gate, expert_up, expert_down)
    if 2 * sources * stream.size <= GATHER_LIMIT and head_count == 4 and ctx_count in (6, 8):
        moe_out = expert_layer_gathered(*experts, sources)
    else:
        moe_out = expert_layer_sent(*experts, sources)
    mixer_in = rms_rows(
        stream.astype(jnp.float32) + moe_out.astype(jnp.float32), mixer_gain
    ).astype(jnp.bfloat16)
    head_place = lax.axis_index("head")

    def crossed(value, step):
        pairs = [(source, source ^ step) for source in range(head_count)]
        return lax.ppermute(value, "head", pairs)

    def from_all(value):
        across = [crossed(value, step) for step in range(2, head_count, 2)]
        received = [value, crossed(value, 1)]
        for part in across:
            received += [part, crossed(part, 1)]
        return received

    in_vmem = pl.BlockSpec(memory_space=pltpu.VMEM)
    in_smem = pl.BlockSpec(memory_space=pltpu.SMEM)
    tok_rows = stream.shape[0]
    rows = tok_rows * head_count
    key_cols, value_cols = query_weight.shape[1], value_weight.shape[1]
    heads = beta_weight.shape[1]
    pieces = from_all(mixer_in)
    qkv_raw, gate_raw, small_raw = pl.pallas_call(
        functools.partial(project_kernel, blocks=head_count),
        in_specs=[in_smem] + [in_vmem] * (head_count + 5),
        out_shape=[
            jax.ShapeDtypeStruct((rows, 2 * key_cols + value_cols), bf16),
            jax.ShapeDtypeStruct((rows, value_cols), bf16),
            jax.ShapeDtypeStruct((rows, 2 * heads), f32),
        ],
        compiler_params=pltpu.CompilerParams(vmem_limit_bytes=48 << 20),
        cost_estimate=worth(5),
        name="project",
    )(
        head_place.reshape(1),
        *pieces,
        query_weight,
        key_weight,
        value_weight,
        output_gate,
        jnp.concatenate([beta_weight, decay_weight], axis=1),
    )
    conv_cols = qkv_raw.shape[1]
    key_heads = key_cols // DK
    taps = jnp.concatenate([query_conv, key_conv, value_conv], axis=1)
    rim_len = taps.shape[0] - 1
    rim = passed_along(qkv_raw[rows - rim_len :], "ctx", 1)
    rim = jnp.concatenate([jnp.zeros((8 - rim_len, conv_cols), f32), rim.astype(f32)], axis=0)
    rates = jnp.stack([decay_log, decay_bias])
    chunk = math.gcd(rows, CHUNK)
    core, reading, moved = pl.pallas_call(
        functools.partial(delta_kernel, key_heads=key_heads, chunk=chunk),
        out_shape=(
            jax.ShapeDtypeStruct((rows, value_cols), f32),
            jax.ShapeDtypeStruct((rows, value_cols), f32),
            jax.ShapeDtypeStruct((heads, DK, 2 * DK), bf16),
        ),
        scratch_shapes=[
            pltpu.VMEM((rows + 8, conv_cols), f32),
            pltpu.VMEM((rows, conv_cols), f32),
            pltpu.VMEM((rows, heads), f32),
            pltpu.VMEM((rows, heads), f32),
            pltpu.VMEM((heads, DK, 2 * DK), f32),
        ],
        compiler_params=pltpu.CompilerParams(vmem_limit_bytes=48 << 20),
        cost_estimate=worth(16),
        name="delta",
    )(qkv_raw, rim, taps, small_raw, rates)
    half = out_weight.shape[0] // 2
    upper = [crossed(after(out_weight[:half], pieces[-1]), step) for step in range(2, head_count, 2)]
    moved = after(moved, *upper)
    lower = [crossed(after(out_weight[half:], moved), step) for step in range(2, head_count, 2)]

    in_pair = (ctx_place % 2).reshape(1)
    other = lax.ppermute(moved, "ctx", [(place, place ^ 1) for place in range(ctx_count)])
    state_shape = jax.ShapeDtypeStruct((heads, DK, DK), bf16)
    added, transfer = pl.pallas_call(
        pair_kernel,
        in_specs=[in_smem, in_vmem, in_vmem],
        out_shape=[state_shape, state_shape],
        compiler_params=pltpu.CompilerParams(vmem_limit_bytes=48 << 20),
        name="pair",
    )(in_pair, moved, other)
    state = passed_along(added, "ctx", 2)
    for hop in range(ctx_count // 2 - 2):
        leaving = jnp.einsum("hij,hjk->hik", transfer, state, preferred_element_type=f32)
        leaving = (leaving + added.astype(f32)).astype(bf16)
        if hop == ctx_count // 2 - 3:
            leaving = after(leaving, *lower)
        state = passed_along(leaving, "ctx", 2)

    gated = pl.pallas_call(
        finish_kernel,
        in_specs=[in_smem] + [in_vmem] * 6,
        out_shape=jax.ShapeDtypeStruct((rows, value_cols), bf16),
        compiler_params=pltpu.CompilerParams(vmem_limit_bytes=48 << 20),
        name="finish",
    )(in_pair, state, other, core, reading, gate_raw, head_gain.reshape(1, -1))
    gated_parts = []
    for step in range(head_count):
        part = lax.dynamic_slice_in_dim(gated, (head_place ^ step) * tok_rows, tok_rows, axis=0)
        gated_parts.append(crossed(part, step) if step else part)
    weight_parts = [out_weight, crossed(after(out_weight, moved), 1)]
    for near_pair in zip(upper, lower):
        weight_parts += near_pair
        weight_parts += [crossed(after(part, state), 1) for part in near_pair]
    mixer_out = pl.pallas_call(
        functools.partial(output_kernel, blocks=head_count),
        out_shape=jax.ShapeDtypeStruct(stream.shape, bf16),
        compiler_params=pltpu.CompilerParams(vmem_limit_bytes=48 << 20),
        name="output",
    )(*gated_parts, *weight_parts)
    return (moe_out, mixer_out)


def solution(mesh):
    return jax.shard_map(
        on_device,
        mesh=mesh,
        in_specs=(
            P(("ctx", "head"), None),
            P(),
            P(),
            P(("ctx", "head"), None),
            P(("ctx", "head"), None, None),
            P(("ctx", "head"), None, None),
            P(("ctx", "head"), None, None),
            P(),
            P(None, "head"),
            P(None, "head"),
            P(None, "head"),
            P(None, "head"),
            P(None, "head"),
            P(None, "head"),
            P(None, "head"),
            P(None, "head"),
            P(None, "head"),
            P("head"),
            P("head"),
            P(),
            P("head", None),
        ),
        out_specs=(P(("ctx", "head"), None), P(("ctx", "head"), None)),
        check_vma=False,
    )
```

```python
import functools
import math

import jax
import jax.numpy as jnp
from jax import lax
from jax.experimental import pallas as pl
from jax.experimental.pallas import tpu as pltpu
from jax.sharding import PartitionSpec as P

DK = 128
CHUNK = 128
GATHER_LIMIT = 32 << 20


epsilon = 1e-06
f32 = jnp.float32
bf16 = jnp.bfloat16


def passed_along(value, axis, steps):
    count = lax.axis_size(axis)
    first, last = (max(0, -steps), min(count, count - steps))
    return lax.ppermute(value, axis, [(source, source + steps) for source in range(first, last)])


def rms_rows(values, gain):
    values = values.astype(jnp.float32)
    scale = lax.rsqrt(jnp.mean(values * values, axis=-1, keepdims=True) + epsilon)
    return values * scale * gain


def after(value, *earlier):
    return lax.optimization_barrier((value, *earlier))[0]


def whole_ref(array):
    return pl.BlockSpec(array.shape, lambda *_: (0,) * array.ndim)


def worth(microseconds):
    return pl.CostEstimate(
        flops=int(microseconds * 1.15e9), bytes_accessed=int(microseconds * 1e6), transcendentals=0
    )


def contract(a, b, dims, precision=None):
    return lax.dot_general(
        a, b, (dims, ((), ())), precision=precision, preferred_element_type=f32
    )


def parts(values):
    high = values.astype(bf16)
    return high, (values - high.astype(f32)).astype(bf16)


def contract_close(a, b):
    a_high, a_low = parts(a)
    b_high, b_low = parts(b)
    doubled = jnp.concatenate([a_high, a_low], axis=1)
    if 2 * b.shape[1] <= 2 * DK:
        both = jnp.concatenate([b_high, b_low], axis=1)
        product = contract(doubled, jnp.concatenate([both, both], axis=0), ((1,), (0,)))
        return product[:, : b.shape[1]] + product[:, b.shape[1] :]
    return contract(
        doubled, jnp.concatenate([b_high, b_high], axis=0), ((1,), (0,))
    ) + contract(a_high, b_low, ((1,), (0,)))


def contract_rows(a, b):
    a_high, a_low = parts(a)
    b_high, b_low = parts(b)
    product = contract(
        jnp.concatenate([a_high, a_low], axis=1),
        jnp.concatenate(
            [jnp.concatenate([b_high, b_high], axis=1), jnp.concatenate([b_low, b_low], axis=1)],
            axis=0,
        ),
        ((1,), (1,)),
    )
    return product[:, : b.shape[0]] + product[:, b.shape[0] :]


def pair_routes(cols, picker, lines, tok_rows, slots):
    rows = cols.shape[0]
    weight_rows = contract(picker, cols, ((1,), (1,)))
    named = weight_rows > 0
    before = lax.broadcasted_iota(jnp.int32, (rows, rows), 0)
    after = lax.broadcasted_iota(jnp.int32, (rows, rows), 1)
    earlier = (before < after) & (before // tok_rows == after // tok_rows)
    rank = contract(
        jnp.where(named, 1.0, 0.0).astype(bf16),
        jnp.where(earlier, 1.0, 0.0).astype(bf16),
        ((1,), (0,)),
    )
    first_slot = lax.broadcasted_iota(jnp.int32, rank.shape, 1) // tok_rows * slots
    rank = jnp.where(named, rank.astype(jnp.int32) + first_slot, -1)
    slot = lax.broadcasted_iota(jnp.int32, (rows // tok_rows * slots, rows), 0)
    picks = [jnp.where(slot == rank[line : line + 1], 1.0, 0.0) for line in range(lines)]
    return weight_rows, picks


def collect_kernel(block_00, block_10, block_01, block_11, picker_ref, own_ref, send_ref, *, slots):
    local_experts, taken, width = own_ref.shape
    tok_rows = block_00.shape[0]
    pair = taken // 2
    for at, pair_refs in enumerate(((block_01, block_11), (block_00, block_10))):
        rows = jnp.concatenate([ref[...] for ref in pair_refs], axis=0)
        _, picks = pair_routes(
            rows[:, width:], picker_ref[...], 2 * local_experts, tok_rows, slots
        )
        picked = contract(
            jnp.concatenate(picks, axis=0).astype(bf16), rows[:, :width], ((1,), (0,))
        ).astype(bf16)
        for expert in range(local_experts):
            there = slice(at * pair, (at + 1) * pair)
            own_ref[expert, there, :] = picked[expert * pair : (expert + 1) * pair]
            line = local_experts + expert
            send_ref[expert, there, :] = picked[line * pair : (line + 1) * pair]


def expert_kernel(*refs):
    *row_refs, gate_ref, up_ref, down_ref, own_ref, send_ref = refs
    half = len(row_refs) // 2
    for sources, out_ref in ((row_refs[half:], send_ref), (row_refs[:half], own_ref)):
        rows = jnp.concatenate([ref[0] for ref in sources], axis=0)
        gate = contract(rows, gate_ref[0], ((1,), (0,)))
        up = contract(rows, up_ref[0], ((1,), (0,)))
        hidden = (gate / (1.0 + jnp.exp(-gate)) * up).astype(bf16)
        out_ref[0] = contract(hidden, down_ref[0], ((1,), (0,))).astype(bf16)


def spread_kernel(
    cols_00, cols_10, cols_01, cols_11, picker_ref, own_ref, got_ref, far_ref, near_ref, here_ref, *, slots
):
    local_experts, taken, _ = own_ref.shape
    tok_rows = cols_00.shape[0]
    pair = taken // 2
    for at, pair_refs in enumerate(((cols_01, cols_11), (cols_00, cols_10))):
        cols = jnp.concatenate([ref[...] for ref in pair_refs], axis=0)
        weight_rows, picks = pair_routes(
            cols, picker_ref[...], 2 * local_experts, tok_rows, slots
        )
        scaled = []
        for line, pick in enumerate(picks):
            result_ref = (own_ref, got_ref)[line // local_experts]
            result = result_ref[line % local_experts, at * pair : (at + 1) * pair, :]
            weight = jnp.sum(pick * weight_rows[line : line + 1], axis=1, keepdims=True)
            scaled.append((result.astype(f32) * weight).astype(bf16))
        summed = contract(
            jnp.concatenate(picks, axis=0).astype(bf16),
            jnp.concatenate(scaled, axis=0),
            ((0,), (0,)),
        ).astype(bf16)
        if at == 0:
            far_ref[...] = summed
        else:
            here_ref[...] = summed[:tok_rows]
            near_ref[...] = summed[tok_rows:]


def expert_layer_gathered(
    stream,
    moe_gain,
    router,
    expert_ids,
    expert_gate,
    expert_up,
    expert_down,
    sources,
):
    tok_rows, width = stream.shape
    local_experts, _, hidden_width = expert_gate.shape
    experts_all = local_experts * sources
    depth = sources // 8
    place = lax.axis_index(("ctx", "head"))

    def sent(value, move):
        pairs = []
        for device in range(sources):
            z, y, x, core = device // 8, device // 4 % 2, device // 2 % 2, device % 2
            z, y, x, core = move(z, y, x, core)
            pairs.append((device, ((z * 2 + y) * 2 + x) * 2 + core))
        return lax.ppermute(value, ("ctx", "head"), pairs)

    def lifted(value, steps):
        return sent(value, lambda z, y, x, core: ((z + steps) % depth, y, x, core))

    def first(value):
        return sent(value, lambda z, y, x, core: (z, y ^ (1 - core), x ^ core, core))

    def second(value):
        return sent(value, lambda z, y, x, core: (z, y ^ core, x ^ (1 - core), core))

    def swapped(value):
        return sent(value, lambda z, y, x, core: (z, y, x, 1 - core))

    normed = rms_rows(stream, moe_gain).astype(bf16)
    logits = jnp.dot(normed, router, preferred_element_type=f32)
    named = jnp.any(
        expert_ids[:, :, None] == jnp.arange(experts_all, dtype=jnp.int32)[None, None, :], axis=1
    )
    raised = jnp.where(named, jnp.exp(logits), 0.0)
    weights = raised / jnp.sum(raised, axis=1, keepdims=True)
    coarse = lax.reduce_precision(weights, 8, 7)
    packet = jnp.concatenate(
        [normed, coarse.astype(bf16), (weights - coarse).astype(bf16)], axis=1
    )

    capacity = (11 * tok_rows * expert_ids.shape[1] + 10 * experts_all - 1) // (10 * experts_all)
    slots = -(-capacity // 8) * 8
    taken = 4 * slots
    column = jnp.arange(2 * experts_all, dtype=jnp.int32)[None, :] % experts_all
    line = jnp.arange(16, dtype=jnp.int32)[:, None]
    owner = jnp.where(line < local_experts, place, place ^ 1)
    picker = (
        (line < 2 * local_experts) & (column == owner * local_experts + line % local_experts)
    ).astype(bf16)

    order = [0, *range(depth - 1, 0, -1)]
    own_rows, got_rows, outcome = {}, {}, {}
    blocks = {}
    mine = packet
    for at, steps in enumerate(order):
        if steps:
            source = packet if steps == 1 else mine
            earlier = [blocks[order[at - 1]][0]] if at > 1 else []
            if at > 1:
                earlier += blocks[order[at - 2]][1:3]
            if earlier:
                source = after(source, *earlier)
            mine = lifted(source, 1 if steps == 1 else -1)
        onward = mine
        if at:
            onward = after(mine, *blocks[order[at - 1]][1:3])
        near = first(onward)
        blocks[steps] = (mine, near, second(onward), second(near))

    picked_spec = pl.BlockSpec((local_experts, taken, width), lambda g: (0, 0, 0))

    def collect(steps, *earlier):
        rows = blocks[steps][0]
        own, send = pl.pallas_call(
            functools.partial(collect_kernel, slots=slots),
            grid=(1,),
            in_specs=[whole_ref(packet)] * 4 + [whole_ref(picker)],
            out_specs=[picked_spec] * 2,
            out_shape=[jax.ShapeDtypeStruct((local_experts, taken, width), bf16)] * 2,
            compiler_params=pltpu.CompilerParams(vmem_limit_bytes=48 << 20),
            cost_estimate=worth(2),
            name="collect",
        )(after(rows, *earlier) if earlier else rows, *blocks[steps][1:], picker)
        own_rows[steps] = own
        got_rows[steps] = swapped(send)

    def run_experts(members, *earlier):
        row_spec = pl.BlockSpec((1, taken, width), lambda e: (e, 0, 0))
        out_spec = pl.BlockSpec((1, len(members) * taken, width), lambda e: (e, 0, 0))
        results, send_back = pl.pallas_call(
            expert_kernel,
            grid=(local_experts,),
            in_specs=[row_spec] * (2 * len(members))
            + [
                pl.BlockSpec((1, width, hidden_width), lambda e: (e, 0, 0)),
                pl.BlockSpec((1, width, hidden_width), lambda e: (e, 0, 0)),
                pl.BlockSpec((1, hidden_width, width), lambda e: (e, 0, 0)),
            ],
            out_specs=[out_spec] * 2,
            out_shape=[jax.ShapeDtypeStruct((local_experts, len(members) * taken, width), bf16)]
            * 2,
            compiler_params=pltpu.CompilerParams(vmem_limit_bytes=56 << 20),
            cost_estimate=worth(4 + 3 * len(members)),
            name="experts",
        )(
            after(own_rows[members[0]], *earlier),
            *[own_rows[member] for member in members[1:]],
            *[got_rows[member] for member in members],
            expert_gate,
            expert_up,
            expert_down,
        )
        got_back = swapped(send_back)
        for at, member in enumerate(members):
            outcome[member] = (at, results, got_back)

    def spread(steps):
        at, results, got_back = outcome[steps]
        result_spec = pl.BlockSpec((local_experts, taken, width), lambda g: (0, at, 0))
        cols_spec = pl.BlockSpec(
            (tok_rows, 2 * experts_all), lambda g: (0, width // (2 * experts_all))
        )
        row_shape = jax.ShapeDtypeStruct((tok_rows, width), bf16)
        far_shape = jax.ShapeDtypeStruct((2 * tok_rows, width), bf16)
        return pl.pallas_call(
            functools.partial(spread_kernel, slots=slots),
            grid=(1,),
            in_specs=[cols_spec] * 4 + [whole_ref(picker), result_spec, result_spec],
            out_specs=[whole_ref(far_shape), whole_ref(row_shape), whole_ref(row_shape)],
            out_shape=[far_shape, row_shape, row_shape],
            compiler_params=pltpu.CompilerParams(vmem_limit_bytes=48 << 20),
            cost_estimate=worth(3),
            name="spread",
        )(*blocks[steps], picker, results, got_back)

    last = order[-1]
    for steps in order[:-2]:
        collect(steps, blocks[order[-2]][0])
    collect(order[-2], *blocks[last][:3])
    run_experts(order[:-1])
    back = order[-2:0:-1]
    ready = {steps: spread(steps) for steps in back}
    collect(last, *[far for far, _, _ in ready.values()])
    run_experts([last])
    back += [last, 0]
    carried = {}
    total = 0.0
    for at, steps in enumerate(back):
        far, near, here = ready[steps] if steps in ready else spread(steps)
        across = second(far)
        if at >= 2 and back[at - 2] in carried:
            across = after(across, carried[back[at - 2]])
        across = across.astype(f32)
        near = first((near.astype(f32) + across[tok_rows:]).astype(bf16))
        here = here.astype(f32) + across[:tok_rows] + near.astype(f32)
        if steps > 2:
            here += carried.pop(steps - 1).astype(f32)
        if steps:
            carried[steps] = lifted(here.astype(bf16), -1 if steps == 1 else 1)
        else:
            total = here
    for arrived in carried.values():
        total += arrived.astype(f32)
    return total.astype(bf16)


def expert_layer_sent(
    stream, moe_gain, router, expert_ids, expert_gate, expert_up, expert_down, sources
):
    tok_rows, model_width = stream.shape
    top_count = expert_ids.shape[1]
    local_experts = expert_gate.shape[0]
    experts_all = local_experts * sources
    capacity = (11 * tok_rows * top_count + 10 * experts_all - 1) // (10 * experts_all)
    normed = rms_rows(stream, moe_gain).astype(jnp.bfloat16)
    logits = jnp.dot(normed, router, preferred_element_type=jnp.float32)
    chosen = jnp.take_along_axis(logits, expert_ids, axis=1)
    raised = jnp.exp(chosen)
    weights = raised / jnp.sum(raised, axis=1, keepdims=True)
    flat_ids = expert_ids.reshape(-1)
    matches = (flat_ids[:, None] == jnp.arange(experts_all, dtype=jnp.int32)[None, :]).astype(
        jnp.int32
    )
    slot_index = jnp.sum((jnp.cumsum(matches, axis=0) - 1) * matches, axis=1)
    places = flat_ids * capacity + slot_index
    token_rows = jnp.arange(tok_rows * top_count, dtype=jnp.int32) // top_count
    outgoing = (
        jnp.zeros((experts_all * capacity, model_width), jnp.bfloat16)
        .at[places]
        .set(normed[token_rows])
    )
    outgoing = outgoing.reshape(sources, local_experts, capacity, model_width)
    received = lax.all_to_all(outgoing, ("ctx", "head"), split_axis=0, concat_axis=0, tiled=True)
    gate_part = jnp.einsum(
        "nesd,edh->nesh", received, expert_gate, preferred_element_type=jnp.float32
    )
    up_part = jnp.einsum("nesd,edh->nesh", received, expert_up, preferred_element_type=jnp.float32)
    hidden = (jax.nn.silu(gate_part) * up_part).astype(jnp.bfloat16)
    returned = lax.all_to_all(
        jnp.einsum(
            "nesh,ehd->nesd", hidden, expert_down, preferred_element_type=jnp.float32
        ).astype(jnp.bfloat16),
        ("ctx", "head"),
        split_axis=0,
        concat_axis=0,
        tiled=True,
    )
    gathered_rows = returned.reshape(experts_all * capacity, model_width)[places].reshape(
        tok_rows, top_count, model_width
    )
    return jnp.sum(weights[:, :, None] * gathered_rows.astype(jnp.float32), axis=1).astype(
        jnp.bfloat16
    )


def unit_inverses(strict_parts):
    size = strict_parts[0].shape[0]
    row = lax.broadcasted_iota(jnp.int32, (size, size), 0)
    col = lax.broadcasted_iota(jnp.int32, (size, size), 1)
    unit = jnp.where(row == col, 1.0, 0.0)
    joining = (row // 2 == col // 2) & (row != col)
    inverses = [unit - jnp.where(joining, part, 0.0) for part in strict_parts]
    half = 2
    while half < size:
        joining = (row // (2 * half) == col // (2 * half)) & (row // half != col // half)
        corners = [jnp.where(joining, part, 0.0) for part in strict_parts]
        if half < 8:
            steps = [contract_close(c, inverse) for c, inverse in zip(corners, inverses)]
            moves = [contract_close(inverse, step) for inverse, step in zip(inverses, steps)]
            inverses = [inverse - move for inverse, move in zip(inverses, moves)]
        else:
            starts = range(0, size, 2 * half)

            def lower_rows(array):
                return jnp.concatenate([array[at + half : at + 2 * half] for at in starts], axis=0)

            zeros = jnp.zeros((half, size), f32)
            steps = [
                contract_close(lower_rows(c), inverse) for c, inverse in zip(corners, inverses)
            ]
            steps = [
                jnp.concatenate(
                    [
                        piece
                        for at in range(0, size // 2, half)
                        for piece in (zeros, step[at : at + half])
                    ],
                    axis=0,
                )
                for step in steps
            ]
            lowers = [lower_rows(inverse) for inverse in inverses]
            lowers = [lower - contract_close(lower, step) for lower, step in zip(lowers, steps)]
            inverses = [
                jnp.concatenate(
                    [
                        piece
                        for at in starts
                        for piece in (
                            inverse[at : at + half],
                            lower[at // 2 : at // 2 + half],
                        )
                    ],
                    axis=0,
                )
                for inverse, lower in zip(inverses, lowers)
            ]
        half *= 2
    return inverses


def unit_rows(rows):
    return rows * lax.rsqrt(jnp.sum(rows * rows, axis=-1, keepdims=True) + epsilon)


def delta_kernel(
    raw_ref,
    rim_ref,
    taps_ref,
    beta_ref,
    decay_ref,
    rate_ref,
    core_ref,
    reading_ref,
    moved_ref,
    extended,
    mixed,
    strengths,
    falls,
    carried,
    *,
    key_heads,
    chunk,
):
    rows, conv_cols = raw_ref.shape
    heads = moved_ref.shape[0]
    group = heads // key_heads
    tap_count = taps_ref.shape[0]
    rim = rim_ref.shape[0]
    extended[0:rim, :] = rim_ref[...]
    extended[rim : rim + rows, :] = raw_ref[...].astype(f32)
    key_at, value_at = key_heads * DK, 2 * key_heads * DK
    for start in range(0, rows, chunk):
        for first in range(0, conv_cols, DK):
            columns = slice(first, first + DK)
            summed = jnp.zeros((chunk, DK), f32)
            for tap in range(tap_count):
                offset = rim - (tap_count - 1) + start + tap
                summed += taps_ref[tap : tap + 1, columns] * extended[
                    offset : offset + chunk, columns
                ]
            value = summed / (1.0 + jnp.exp(-summed))
            if first < key_at:
                value = unit_rows(value) * DK**-0.5
            elif first < value_at:
                value = unit_rows(value)
            mixed[start : start + chunk, columns] = value
    strengths[...] = 1.0 / (1.0 + jnp.exp(-beta_ref[...]))
    shifted = decay_ref[...] + rate_ref[1:2, :]
    softened = jnp.maximum(shifted, 0.0) + jnp.log1p(jnp.exp(-jnp.abs(shifted)))
    falls[...] = -jnp.exp(rate_ref[0:1, :]) * softened

    row = lax.broadcasted_iota(jnp.int32, (chunk, chunk), 0)
    col = lax.broadcasted_iota(jnp.int32, (chunk, chunk), 1)
    inclusive, strict = row >= col, row > col
    lower = jnp.where(inclusive, 1.0, 0.0)
    across = lax.broadcasted_iota(jnp.int32, (DK, 2 * DK), 1)
    down = lax.broadcasted_iota(jnp.int32, (DK, 2 * DK), 0)
    carried[...] = jnp.broadcast_to(
        jnp.where(across == down + DK, 1.0, 0.0)[None], carried.shape
    )

    def advance(step, nothing):
        here = pl.ds(pl.multiple_of(step * chunk, chunk), chunk)
        fall = falls[here, :]
        strength = strengths[here, :]
        cumulative = contract(lower, fall, ((1,), (0,)), lax.Precision.HIGHEST)
        cumulative_rows = contract(fall, lower, ((0,), (1,)), lax.Precision.HIGHEST)
        owners = range(heads)
        queries = [mixed[here, k * DK : (k + 1) * DK] for k in range(key_heads)]
        keys = [mixed[here, key_at + k * DK : key_at + (k + 1) * DK] for k in range(key_heads)]
        dots = [
            contract_rows(jnp.concatenate([key, query], axis=0), key)
            for key, query in zip(keys, queries)
        ]
        totals = [cumulative[:, head : head + 1] for head in owners]
        kept = [
            jnp.where(
                inclusive,
                jnp.exp(jnp.where(inclusive, totals[head] - cumulative_rows[head : head + 1, :], 0.0)),
                0.0,
            )
            for head in owners
        ]
        own = [strength[:, head : head + 1] for head in owners]
        solvers = unit_inverses(
            [
                own[head] * jnp.where(strict, kept[head], 0.0) * dots[head // group][:chunk]
                for head in owners
            ]
        )
        risen = [jnp.exp(total) for total in totals]
        solved = [
            contract_close(
                solvers[head],
                own[head]
                * jnp.concatenate(
                    [
                        mixed[here, value_at + head * DK : value_at + (head + 1) * DK],
                        risen[head] * keys[head // group],
                    ],
                    axis=1,
                ),
            )
            for head in owners
        ]
        states = [carried[head] for head in owners]
        read = [
            contract_close(
                jnp.concatenate(
                    [solved[head][:, DK:], risen[head] * queries[head // group]], axis=0
                ),
                states[head],
            )
            for head in owners
        ]
        updates = [
            jnp.concatenate([solved[head][:, :DK], jnp.zeros((chunk, DK), f32)], axis=1)
            - read[head][:chunk]
            for head in owners
        ]
        for head in owners:
            last = totals[head][chunk - 1 :, :]
            leaving = jnp.exp(last - totals[head]) * keys[head // group]
            carried[head] = jnp.exp(last) * states[head] + contract_close(
                leaving.T, updates[head]
            )
        for head in owners:
            result = read[head][chunk:] + contract_close(
                kept[head] * dots[head // group][chunk:], updates[head]
            )
            core_ref[here, head * DK : (head + 1) * DK] = result[:, :DK]
            reading_ref[here, head * DK : (head + 1) * DK] = result[:, DK:]
        return nothing

    lax.fori_loop(0, rows // chunk, advance, 0)
    moved_ref[...] = carried[...].astype(bf16)


def project_kernel(place_ref, *refs, blocks):
    piece_refs, halo_refs = refs[:blocks], refs[blocks : 2 * blocks]
    weight_refs, out_refs = refs[2 * blocks : -5], refs[-5:]
    qkv_ref, gate_ref, beta_ref, decay_ref, rim_ref = out_refs
    tok_rows = piece_refs[0].shape[0]
    halo_rows = halo_refs[0].shape[0]
    halo = sum(
        jnp.where((place_ref[0] ^ step) == blocks - 1, 1.0, 0.0) * halo_refs[step][...].astype(f32)
        for step in range(blocks)
    ).astype(bf16)
    rows = jnp.concatenate([ref[...] for ref in piece_refs] + [halo], axis=0)

    def store(out_ref, first, weight_ref):
        product = contract(rows, weight_ref[...], ((1,), (0,))).astype(out_ref.dtype)
        last = first + product.shape[1]
        for step in range(blocks):
            at = pl.multiple_of((place_ref[0] ^ step) * tok_rows, tok_rows)
            out_ref[pl.ds(at, tok_rows), first:last] = product[
                step * tok_rows : (step + 1) * tok_rows
            ]
        return product[blocks * tok_rows :]

    first = 0
    for weight_ref in weight_refs[:3]:
        rim = store(qkv_ref, first, weight_ref)
        last = first + weight_ref.shape[1]
        rim_ref[:, first:last] = rim.astype(f32)
        first = last
    store(gate_ref, 0, weight_refs[3])
    store(beta_ref, 0, weight_refs[4])
    store(decay_ref, 0, weight_refs[5])


def pair_kernel(second_ref, mine_ref, other_ref, moved_ref, transfer_ref):
    for head in range(mine_ref.shape[0]):
        mine, other = mine_ref[head].astype(f32), other_ref[head].astype(f32)
        late = second_ref[0] == 1
        earlier = jnp.where(late, other, mine).astype(bf16)
        later = jnp.where(late, mine, other)
        joined = contract(later[:, DK:].astype(bf16), earlier, ((1,), (0,)))
        moved_ref[head] = (joined[:, :DK] + later[:, :DK]).astype(bf16)
        transfer_ref[head] = joined[:, DK:].astype(bf16)


def finish_kernel(
    second_ref, state_ref, other_ref, core_ref, reading_ref, gate_ref, gain_ref, gated_ref
):
    states = []
    for head in range(state_ref.shape[0]):
        state = state_ref[head]
        passed = contract(other_ref[head, :, DK:], state, ((1,), (0,))) + other_ref[
            head, :, :DK
        ].astype(f32)
        states.append(jnp.where(second_ref[0] == 1, passed, state.astype(f32)))
    for head, state in enumerate(states):
        columns = slice(head * DK, (head + 1) * DK)
        core = core_ref[:, columns] + contract_close(reading_ref[:, columns], state)
        normal = (
            core
            * lax.rsqrt(jnp.mean(core * core, axis=-1, keepdims=True) + epsilon)
            * gain_ref[...]
        )
        gate = gate_ref[:, columns].astype(f32)
        gated_ref[:, columns] = (normal * (gate / (1.0 + jnp.exp(-gate)))).astype(bf16)


def output_kernel(*refs, blocks):
    row_refs, weight_refs, out_ref = refs[:blocks], refs[blocks:-1], refs[-1]
    total = 0.0
    pieces = iter(weight_refs)
    for rows_ref in row_refs:
        at = 0
        while at < rows_ref.shape[1]:
            weight_ref = next(pieces)
            depth = weight_ref.shape[0]
            total += contract(rows_ref[:, at : at + depth], weight_ref[...], ((1,), (0,)))
            at += depth
    out_ref[...] = total.astype(bf16)


def on_device(
    stream,
    moe_gain,
    router,
    expert_ids,
    expert_gate,
    expert_up,
    expert_down,
    mixer_gain,
    query_weight,
    key_weight,
    value_weight,
    output_gate,
    beta_weight,
    decay_weight,
    query_conv,
    key_conv,
    value_conv,
    decay_log,
    decay_bias,
    head_gain,
    out_weight,
):
    ctx_count = lax.axis_size("ctx")
    head_count = lax.axis_size("head")
    sources = ctx_count * head_count
    ctx_place = lax.axis_index("ctx")
    experts = (stream, moe_gain, router, expert_ids, expert_gate, expert_up, expert_down)
    if 2 * sources * stream.size <= GATHER_LIMIT and head_count == 4 and ctx_count in (6, 8):
        moe_out = expert_layer_gathered(*experts, sources)
    else:
        moe_out = expert_layer_sent(*experts, sources)
    mixer_in = rms_rows(
        stream.astype(jnp.float32) + moe_out.astype(jnp.float32), mixer_gain
    ).astype(jnp.bfloat16)
    head_place = lax.axis_index("head")

    def crossed(value, step):
        pairs = [(source, source ^ step) for source in range(head_count)]
        return lax.ppermute(value, "head", pairs)

    def from_all(value):
        across = [crossed(value, step) for step in range(2, head_count, 2)]
        received = [value, crossed(value, 1)]
        for part in across:
            received += [part, crossed(part, 1)]
        return received

    in_vmem = pl.BlockSpec(memory_space=pltpu.VMEM)
    in_smem = pl.BlockSpec(memory_space=pltpu.SMEM)
    tok_rows, width = stream.shape
    rows = tok_rows * head_count
    key_cols, value_cols = query_weight.shape[1], value_weight.shape[1]
    heads = beta_weight.shape[1]
    rim_len = 16
    halos = from_all(passed_along(mixer_in[tok_rows - rim_len :], "ctx", 1))
    pieces = from_all(mixer_in)
    conv_cols = 2 * key_cols + value_cols
    qkv_raw, gate_raw, beta_raw, decay_raw, rim = pl.pallas_call(
        functools.partial(project_kernel, blocks=head_count),
        in_specs=[in_smem] + [in_vmem] * (2 * head_count + 6),
        out_shape=[
            jax.ShapeDtypeStruct((rows, conv_cols), bf16),
            jax.ShapeDtypeStruct((rows, value_cols), bf16),
            jax.ShapeDtypeStruct((rows, heads), f32),
            jax.ShapeDtypeStruct((rows, heads), f32),
            jax.ShapeDtypeStruct((rim_len, conv_cols), f32),
        ],
        compiler_params=pltpu.CompilerParams(vmem_limit_bytes=48 << 20),
        cost_estimate=worth(5),
        name="project",
    )(
        head_place.reshape(1),
        *pieces,
        *halos,
        query_weight,
        key_weight,
        value_weight,
        output_gate,
        beta_weight,
        decay_weight,
    )
    key_heads = key_cols // DK
    taps = jnp.concatenate([query_conv, key_conv, value_conv], axis=1)
    rates = jnp.stack([decay_log, decay_bias])
    chunk = math.gcd(rows, CHUNK)
    core, reading, moved = pl.pallas_call(
        functools.partial(delta_kernel, key_heads=key_heads, chunk=chunk),
        out_shape=(
            jax.ShapeDtypeStruct((rows, value_cols), f32),
            jax.ShapeDtypeStruct((rows, value_cols), f32),
            jax.ShapeDtypeStruct((heads, DK, 2 * DK), bf16),
        ),
        scratch_shapes=[
            pltpu.VMEM((rows + rim_len, conv_cols), f32),
            pltpu.VMEM((rows, conv_cols), f32),
            pltpu.VMEM((rows, heads), f32),
            pltpu.VMEM((rows, heads), f32),
            pltpu.VMEM((heads, DK, 2 * DK), f32),
        ],
        compiler_params=pltpu.CompilerParams(vmem_limit_bytes=48 << 20),
        cost_estimate=worth(16),
        name="delta",
    )(qkv_raw, rim, taps, beta_raw, decay_raw, rates)
    half = out_weight.shape[0] // 2
    upper = [crossed(after(out_weight[:half], pieces[-1]), step) for step in range(2, head_count, 2)]
    lower = [crossed(after(out_weight[half:], moved), step) for step in range(2, head_count, 2)]

    in_pair = (ctx_place % 2).reshape(1)
    other = lax.ppermute(moved, "ctx", [(place, place ^ 1) for place in range(ctx_count)])
    other = after(other, *upper)
    state_shape = jax.ShapeDtypeStruct((heads, DK, DK), bf16)
    added, transfer = pl.pallas_call(
        pair_kernel,
        in_specs=[in_smem, in_vmem, in_vmem],
        out_shape=[state_shape, state_shape],
        compiler_params=pltpu.CompilerParams(vmem_limit_bytes=48 << 20),
        name="pair",
    )(in_pair, moved, other)
    state = passed_along(added, "ctx", 2)
    for hop in range(ctx_count // 2 - 2):
        leaving = jnp.einsum("hij,hjk->hik", transfer, state, preferred_element_type=f32)
        leaving = (leaving + added.astype(f32)).astype(bf16)
        if hop == ctx_count // 2 - 3:
            leaving = after(leaving, *lower)
        state = passed_along(leaving, "ctx", 2)

    gated = pl.pallas_call(
        finish_kernel,
        grid=(head_count,),
        in_specs=[in_smem, whole_ref(state), whole_ref(other)]
        + [pl.BlockSpec((tok_rows, value_cols), lambda block: (block, 0))] * 3
        + [pl.BlockSpec((1, DK), lambda block: (0, 0))],
        out_specs=pl.BlockSpec((tok_rows, value_cols), lambda block: (block, 0)),
        out_shape=jax.ShapeDtypeStruct((rows, value_cols), bf16),
        compiler_params=pltpu.CompilerParams(vmem_limit_bytes=48 << 20),
        name="finish",
    )(in_pair, state, other, core, reading, gate_raw, head_gain.reshape(1, -1))
    gated_parts = []
    for step in range(head_count):
        part = lax.dynamic_slice_in_dim(gated, (head_place ^ step) * tok_rows, tok_rows, axis=0)
        gated_parts.append(crossed(part, step) if step else part)
    weight_parts = [out_weight, crossed(after(out_weight, moved), 1)]
    for near_pair in zip(upper, lower):
        weight_parts += near_pair
        weight_parts += [crossed(after(part, state), 1) for part in near_pair]
    mixer_out = pl.pallas_call(
        functools.partial(output_kernel, blocks=head_count),
        grid=(4,),
        in_specs=[whole_ref(part) for part in gated_parts]
        + [pl.BlockSpec((part.shape[0], width // 4), lambda n: (0, n)) for part in weight_parts],
        out_specs=pl.BlockSpec((tok_rows, width // 4), lambda n: (0, n)),
        out_shape=jax.ShapeDtypeStruct(stream.shape, bf16),
        compiler_params=pltpu.CompilerParams(vmem_limit_bytes=48 << 20),
        name="output",
    )(*gated_parts, *weight_parts)
    return (moe_out, mixer_out)


def solution(mesh):
    return jax.shard_map(
        on_device,
        mesh=mesh,
        in_specs=(
            P(("ctx", "head"), None),
            P(),
            P(),
            P(("ctx", "head"), None),
            P(("ctx", "head"), None, None),
            P(("ctx", "head"), None, None),
            P(("ctx", "head"), None, None),
            P(),
            P(None, "head"),
            P(None, "head"),
            P(None, "head"),
            P(None, "head"),
            P(None, "head"),
            P(None, "head"),
            P(None, "head"),
            P(None, "head"),
            P(None, "head"),
            P("head"),
            P("head"),
            P(),
            P("head", None),
        ),
        out_specs=(P(("ctx", "head"), None), P(("ctx", "head"), None)),
        check_vma=False,
    )
```

```python
import functools
import math

import jax
import jax.numpy as jnp
from jax import lax
from jax.experimental import pallas as pl
from jax.experimental.pallas import tpu as pltpu
from jax.sharding import PartitionSpec as P

DK = 128
CHUNK = 128
GATHER_LIMIT = 32 << 20


epsilon = 1e-06
f32 = jnp.float32
bf16 = jnp.bfloat16


def passed_along(value, axis, steps):
    count = lax.axis_size(axis)
    first, last = (max(0, -steps), min(count, count - steps))
    return lax.ppermute(value, axis, [(source, source + steps) for source in range(first, last)])


def rms_rows(values, gain):
    values = values.astype(jnp.float32)
    scale = lax.rsqrt(jnp.mean(values * values, axis=-1, keepdims=True) + epsilon)
    return values * scale * gain


def after(value, *earlier):
    return lax.optimization_barrier((value, *earlier))[0]


def whole_ref(array):
    return pl.BlockSpec(array.shape, lambda *_: (0,) * array.ndim)


def worth(microseconds):
    return pl.CostEstimate(
        flops=int(microseconds * 1.15e9), bytes_accessed=int(microseconds * 1e6), transcendentals=0
    )


def contract(a, b, dims, precision=None):
    return lax.dot_general(
        a, b, (dims, ((), ())), precision=precision, preferred_element_type=f32
    )


def parts(values):
    high = values.astype(bf16)
    return high, (values - high.astype(f32)).astype(bf16)


def contract_close(a, b):
    a_high, a_low = parts(a)
    b_high, b_low = parts(b)
    doubled = jnp.concatenate([a_high, a_low], axis=1)
    if 2 * b.shape[1] <= 2 * DK:
        both = jnp.concatenate([b_high, b_low], axis=1)
        product = contract(doubled, jnp.concatenate([both, both], axis=0), ((1,), (0,)))
        return product[:, : b.shape[1]] + product[:, b.shape[1] :]
    return contract(
        doubled, jnp.concatenate([b_high, b_high], axis=0), ((1,), (0,))
    ) + contract(a_high, b_low, ((1,), (0,)))


def contract_rows(a, b):
    a_high, a_low = parts(a)
    b_high, b_low = parts(b)
    product = contract(
        jnp.concatenate([a_high, a_low], axis=1),
        jnp.concatenate(
            [jnp.concatenate([b_high, b_high], axis=1), jnp.concatenate([b_low, b_low], axis=1)],
            axis=0,
        ),
        ((1,), (1,)),
    )
    return product[:, : b.shape[0]] + product[:, b.shape[0] :]


def pair_routes(cols, picker, lines, tok_rows, slots):
    rows = cols.shape[0]
    weight_rows = contract(picker, cols, ((1,), (1,)))
    named = weight_rows > 0
    before = lax.broadcasted_iota(jnp.int32, (rows, rows), 0)
    after = lax.broadcasted_iota(jnp.int32, (rows, rows), 1)
    earlier = (before < after) & (before // tok_rows == after // tok_rows)
    rank = contract(
        jnp.where(named, 1.0, 0.0).astype(bf16),
        jnp.where(earlier, 1.0, 0.0).astype(bf16),
        ((1,), (0,)),
    )
    first_slot = lax.broadcasted_iota(jnp.int32, rank.shape, 1) // tok_rows * slots
    rank = jnp.where(named, rank.astype(jnp.int32) + first_slot, -1)
    slot = lax.broadcasted_iota(jnp.int32, (rows // tok_rows * slots, rows), 0)
    picks = [jnp.where(slot == rank[line : line + 1], 1.0, 0.0) for line in range(lines)]
    return weight_rows, picks


def collect_kernel(block_00, block_10, block_01, block_11, picker_ref, own_ref, send_ref, *, slots):
    local_experts, taken, width = own_ref.shape
    tok_rows = block_00.shape[0]
    pair = taken // 2
    for at, pair_refs in enumerate(((block_01, block_11), (block_00, block_10))):
        rows = jnp.concatenate([ref[...] for ref in pair_refs], axis=0)
        _, picks = pair_routes(
            rows[:, width:], picker_ref[...], 2 * local_experts, tok_rows, slots
        )
        picked = contract(
            jnp.concatenate(picks, axis=0).astype(bf16), rows[:, :width], ((1,), (0,))
        ).astype(bf16)
        for expert in range(local_experts):
            there = slice(at * pair, (at + 1) * pair)
            own_ref[expert, there, :] = picked[expert * pair : (expert + 1) * pair]
            line = local_experts + expert
            send_ref[expert, there, :] = picked[line * pair : (line + 1) * pair]


def expert_kernel(*refs):
    *row_refs, gate_ref, up_ref, down_ref, own_ref, send_ref = refs
    half = len(row_refs) // 2
    for sources, out_ref in ((row_refs[half:], send_ref), (row_refs[:half], own_ref)):
        rows = jnp.concatenate([ref[0] for ref in sources], axis=0)
        gate = contract(rows, gate_ref[0], ((1,), (0,)))
        up = contract(rows, up_ref[0], ((1,), (0,)))
        hidden = (gate / (1.0 + jnp.exp(-gate)) * up).astype(bf16)
        out_ref[0] = contract(hidden, down_ref[0], ((1,), (0,))).astype(bf16)


def spread_kernel(*refs, slots, places):
    *cols_refs, picker_ref, own_ref, got_ref, far_ref, near_ref, here_ref = refs
    local_experts = own_ref.shape[0]
    tok_rows = cols_refs[0].shape[0]
    pair = 2 * slots
    for group, place in enumerate(places):
        cols_00, cols_10, cols_01, cols_11 = cols_refs[4 * group : 4 * group + 4]
        for at, pair_refs in enumerate(((cols_01, cols_11), (cols_00, cols_10))):
            cols = jnp.concatenate([ref[...] for ref in pair_refs], axis=0)
            weight_rows, picks = pair_routes(
                cols, picker_ref[...], 2 * local_experts, tok_rows, slots
            )
            first = (2 * place + at) * pair
            scaled = []
            for line, pick in enumerate(picks):
                result_ref = (own_ref, got_ref)[line // local_experts]
                result = result_ref[line % local_experts, first : first + pair, :]
                weight = jnp.sum(pick * weight_rows[line : line + 1], axis=1, keepdims=True)
                scaled.append((result.astype(f32) * weight).astype(bf16))
            summed = contract(
                jnp.concatenate(picks, axis=0).astype(bf16),
                jnp.concatenate(scaled, axis=0),
                ((0,), (0,)),
            ).astype(bf16)
            if at == 0:
                far_ref[group, 0] = summed[:tok_rows]
                far_ref[group, 1] = summed[tok_rows:]
            else:
                here_ref[group] = summed[:tok_rows]
                near_ref[group] = summed[tok_rows:]


def expert_layer_gathered(
    stream,
    moe_gain,
    router,
    expert_ids,
    expert_gate,
    expert_up,
    expert_down,
    sources,
    early,
):
    tok_rows, width = stream.shape
    local_experts, _, hidden_width = expert_gate.shape
    experts_all = local_experts * sources
    depth = sources // 8
    place = lax.axis_index(("ctx", "head"))

    def sent(value, move):
        pairs = []
        for device in range(sources):
            z, y, x, core = device // 8, device // 4 % 2, device // 2 % 2, device % 2
            z, y, x, core = move(z, y, x, core)
            pairs.append((device, ((z * 2 + y) * 2 + x) * 2 + core))
        return lax.ppermute(value, ("ctx", "head"), pairs)

    def lifted(value, steps):
        return sent(value, lambda z, y, x, core: ((z + steps) % depth, y, x, core))

    def first(value):
        return sent(value, lambda z, y, x, core: (z, y ^ (1 - core), x ^ core, core))

    def second(value):
        return sent(value, lambda z, y, x, core: (z, y ^ core, x ^ (1 - core), core))

    def swapped(value):
        return sent(value, lambda z, y, x, core: (z, y, x, 1 - core))

    normed = rms_rows(stream, moe_gain).astype(bf16)
    logits = jnp.dot(normed, router, preferred_element_type=f32)
    named = jnp.any(
        expert_ids[:, :, None] == jnp.arange(experts_all, dtype=jnp.int32)[None, None, :], axis=1
    )
    raised = jnp.where(named, jnp.exp(logits), 0.0)
    weights = raised / jnp.sum(raised, axis=1, keepdims=True)
    coarse = lax.reduce_precision(weights, 8, 7)
    packet = jnp.concatenate(
        [normed, coarse.astype(bf16), (weights - coarse).astype(bf16)], axis=1
    )

    capacity = (11 * tok_rows * expert_ids.shape[1] + 10 * experts_all - 1) // (10 * experts_all)
    slots = -(-capacity // 8) * 8
    taken = 4 * slots
    column = jnp.arange(2 * experts_all, dtype=jnp.int32)[None, :] % experts_all
    line = jnp.arange(16, dtype=jnp.int32)[:, None]
    owner = jnp.where(line < local_experts, place, place ^ 1)
    picker = (
        (line < 2 * local_experts) & (column == owner * local_experts + line % local_experts)
    ).astype(bf16)

    order = [0, *range(depth - 1, 0, -1)]
    own_rows, got_rows, outcome = {}, {}, {}
    blocks = {}
    mine = packet
    for at, steps in enumerate(order):
        if steps:
            source = packet if steps == 1 else mine
            earlier = [blocks[order[at - 1]][0]] if at > 1 else []
            if at > 1:
                earlier += blocks[order[at - 2]][1:3]
            if earlier:
                source = after(source, *earlier)
            mine = lifted(source, 1 if steps == 1 else -1)
        onward = mine
        if at:
            onward = after(mine, *blocks[order[at - 1]][1:3])
        near = first(onward)
        blocks[steps] = (mine, near, second(onward), second(near))

    picked_spec = pl.BlockSpec((local_experts, taken, width), lambda g: (0, 0, 0))

    def collect(steps, *earlier):
        rows = blocks[steps][0]
        own, send = pl.pallas_call(
            functools.partial(collect_kernel, slots=slots),
            grid=(1,),
            in_specs=[whole_ref(packet)] * 4 + [whole_ref(picker)],
            out_specs=[picked_spec] * 2,
            out_shape=[jax.ShapeDtypeStruct((local_experts, taken, width), bf16)] * 2,
            compiler_params=pltpu.CompilerParams(vmem_limit_bytes=24 << 20),
            cost_estimate=worth(2),
            name="collect",
        )(after(rows, *earlier) if earlier else rows, *blocks[steps][1:], picker)
        own_rows[steps] = own
        got_rows[steps] = swapped(send)

    def run_experts(members, *earlier):
        row_spec = pl.BlockSpec((1, taken, width), lambda e: (e, 0, 0))
        out_spec = pl.BlockSpec((1, len(members) * taken, width), lambda e: (e, 0, 0))
        results, send_back = pl.pallas_call(
            expert_kernel,
            grid=(local_experts,),
            in_specs=[row_spec] * (2 * len(members))
            + [
                pl.BlockSpec((1, width, hidden_width), lambda e: (e, 0, 0)),
                pl.BlockSpec((1, width, hidden_width), lambda e: (e, 0, 0)),
                pl.BlockSpec((1, hidden_width, width), lambda e: (e, 0, 0)),
            ],
            out_specs=[out_spec] * 2,
            out_shape=[jax.ShapeDtypeStruct((local_experts, len(members) * taken, width), bf16)]
            * 2,
            compiler_params=pltpu.CompilerParams(vmem_limit_bytes=40 << 20),
            cost_estimate=worth(4 + 3 * len(members)),
            name="experts",
        )(
            after(own_rows[members[0]], *earlier),
            *[own_rows[member] for member in members[1:]],
            *[got_rows[member] for member in members],
            expert_gate,
            expert_up,
            expert_down,
        )
        got_back = swapped(send_back)
        for at, member in enumerate(members):
            outcome[member] = (at, results, got_back)

    def spread(members):
        places = [outcome[member][0] for member in members]
        _, results, got_back = outcome[members[0]]
        cols_spec = pl.BlockSpec(
            (tok_rows, 2 * experts_all), lambda g: (0, width // (2 * experts_all))
        )
        row_shape = jax.ShapeDtypeStruct((len(members), tok_rows, width), bf16)
        far_shape = jax.ShapeDtypeStruct((len(members), 2, tok_rows, width), bf16)
        return pl.pallas_call(
            functools.partial(spread_kernel, slots=slots, places=places),
            grid=(1,),
            in_specs=[cols_spec] * (4 * len(members))
            + [whole_ref(picker), whole_ref(results), whole_ref(results)],
            out_specs=[whole_ref(far_shape), whole_ref(row_shape), whole_ref(row_shape)],
            out_shape=[far_shape, row_shape, row_shape],
            compiler_params=pltpu.CompilerParams(vmem_limit_bytes=28 << 20),
            cost_estimate=worth(3 * len(members)),
            name="spread",
        )(*(block for member in members for block in blocks[member]), picker, results, got_back)

    last, batch = order[-1], order[-2:0:-1]
    for steps in order[:-2]:
        collect(steps, blocks[order[-2]][0])
    collect(order[-2], *blocks[last][:3])
    run_experts(order[:-1])
    far, near, here = spread(batch)
    collect(last, far)
    run_experts([last])
    far_last, near_last, here_last = spread([last])
    far_own, near_own, here_own = spread([0])

    def joined(near, here, direct, diagonal):
        near = first((near.astype(f32) + diagonal.astype(f32)).astype(bf16))
        return here.astype(f32) + direct.astype(f32) + near.astype(f32)

    across = after(second(far), far_last, far_own)
    sums = joined(near, here, across[:, 0], across[:, 1])
    moving = lifted(sums[0].astype(bf16), 1)
    for at in range(1, len(batch)):
        moving = lifted((sums[at] + moving.astype(f32)).astype(bf16), 1)
    across = second(far_last)
    sums = joined(near_last, here_last, across[:, 0], across[:, 1])
    rising = lifted(sums[0].astype(bf16), -1)
    diagonal = after(second(far_own[0, 1]), moving)
    total = joined(near_own[0], here_own[0], second(far_own[0, 0]), diagonal)
    total += moving.astype(f32) + rising.astype(f32)
    return after(total, *early).astype(bf16)


def expert_layer_sent(
    stream, moe_gain, router, expert_ids, expert_gate, expert_up, expert_down, sources
):
    tok_rows, model_width = stream.shape
    top_count = expert_ids.shape[1]
    local_experts = expert_gate.shape[0]
    experts_all = local_experts * sources
    capacity = (11 * tok_rows * top_count + 10 * experts_all - 1) // (10 * experts_all)
    normed = rms_rows(stream, moe_gain).astype(jnp.bfloat16)
    logits = jnp.dot(normed, router, preferred_element_type=jnp.float32)
    chosen = jnp.take_along_axis(logits, expert_ids, axis=1)
    raised = jnp.exp(chosen)
    weights = raised / jnp.sum(raised, axis=1, keepdims=True)
    flat_ids = expert_ids.reshape(-1)
    matches = (flat_ids[:, None] == jnp.arange(experts_all, dtype=jnp.int32)[None, :]).astype(
        jnp.int32
    )
    slot_index = jnp.sum((jnp.cumsum(matches, axis=0) - 1) * matches, axis=1)
    places = flat_ids * capacity + slot_index
    token_rows = jnp.arange(tok_rows * top_count, dtype=jnp.int32) // top_count
    outgoing = (
        jnp.zeros((experts_all * capacity, model_width), jnp.bfloat16)
        .at[places]
        .set(normed[token_rows])
    )
    outgoing = outgoing.reshape(sources, local_experts, capacity, model_width)
    received = lax.all_to_all(outgoing, ("ctx", "head"), split_axis=0, concat_axis=0, tiled=True)
    gate_part = jnp.einsum(
        "nesd,edh->nesh", received, expert_gate, preferred_element_type=jnp.float32
    )
    up_part = jnp.einsum("nesd,edh->nesh", received, expert_up, preferred_element_type=jnp.float32)
    hidden = (jax.nn.silu(gate_part) * up_part).astype(jnp.bfloat16)
    returned = lax.all_to_all(
        jnp.einsum(
            "nesh,ehd->nesd", hidden, expert_down, preferred_element_type=jnp.float32
        ).astype(jnp.bfloat16),
        ("ctx", "head"),
        split_axis=0,
        concat_axis=0,
        tiled=True,
    )
    gathered_rows = returned.reshape(experts_all * capacity, model_width)[places].reshape(
        tok_rows, top_count, model_width
    )
    return jnp.sum(weights[:, :, None] * gathered_rows.astype(jnp.float32), axis=1).astype(
        jnp.bfloat16
    )


def unit_inverses(strict_parts):
    size = strict_parts[0].shape[0]
    row = lax.broadcasted_iota(jnp.int32, (size, size), 0)
    col = lax.broadcasted_iota(jnp.int32, (size, size), 1)
    unit = jnp.where(row == col, 1.0, 0.0)
    joining = (row // 2 == col // 2) & (row != col)
    inverses = [unit - jnp.where(joining, part, 0.0) for part in strict_parts]
    half = 2
    while half < size:
        joining = (row // (2 * half) == col // (2 * half)) & (row // half != col // half)
        corners = [jnp.where(joining, part, 0.0) for part in strict_parts]
        if half < 8:
            steps = [contract_close(c, inverse) for c, inverse in zip(corners, inverses)]
            moves = [contract_close(inverse, step) for inverse, step in zip(inverses, steps)]
            inverses = [inverse - move for inverse, move in zip(inverses, moves)]
        else:
            starts = range(0, size, 2 * half)

            def lower_rows(array):
                return jnp.concatenate([array[at + half : at + 2 * half] for at in starts], axis=0)

            zeros = jnp.zeros((half, size), f32)
            steps = [
                contract_close(lower_rows(c), inverse) for c, inverse in zip(corners, inverses)
            ]
            steps = [
                jnp.concatenate(
                    [
                        piece
                        for at in range(0, size // 2, half)
                        for piece in (zeros, step[at : at + half])
                    ],
                    axis=0,
                )
                for step in steps
            ]
            lowers = [lower_rows(inverse) for inverse in inverses]
            lowers = [lower - contract_close(lower, step) for lower, step in zip(lowers, steps)]
            inverses = [
                jnp.concatenate(
                    [
                        piece
                        for at in starts
                        for piece in (
                            inverse[at : at + half],
                            lower[at // 2 : at // 2 + half],
                        )
                    ],
                    axis=0,
                )
                for inverse, lower in zip(inverses, lowers)
            ]
        half *= 2
    return inverses


def unit_rows(rows):
    return rows * lax.rsqrt(jnp.sum(rows * rows, axis=-1, keepdims=True) + epsilon)


def delta_kernel(
    place_ref,
    near_raw,
    far_raw,
    near_beta,
    far_beta,
    near_decay,
    far_decay,
    rim_ref,
    taps_ref,
    rate_ref,
    core_ref,
    reading_ref,
    moved_ref,
    extended,
    mixed,
    strengths,
    falls,
    carried,
    *,
    key_heads,
    chunk,
    tok_rows,
):
    rows, conv_cols = near_raw.shape[0] + far_raw.shape[0], near_raw.shape[1]
    heads = moved_ref.shape[0]
    group = heads // key_heads
    tap_count = taps_ref.shape[0]
    rim = rim_ref.shape[0]
    extended[0:rim, :] = rim_ref[...]
    step = 0
    for part_refs in ((near_raw, near_beta, near_decay), (far_raw, far_beta, far_decay)):
        for first in range(0, part_refs[0].shape[0], tok_rows):
            at = pl.multiple_of((place_ref[0] ^ step) * tok_rows, tok_rows)
            part = slice(first, first + tok_rows)
            extended[pl.ds(rim + at, tok_rows), :] = part_refs[0][part, :].astype(f32)
            strengths[pl.ds(at, tok_rows), :] = 1.0 / (1.0 + jnp.exp(-part_refs[1][part, :]))
            shifted = part_refs[2][part, :] + rate_ref[1:2, :]
            softened = jnp.maximum(shifted, 0.0) + jnp.log1p(jnp.exp(-jnp.abs(shifted)))
            falls[pl.ds(at, tok_rows), :] = -jnp.exp(rate_ref[0:1, :]) * softened
            step += 1
    key_at, value_at = key_heads * DK, 2 * key_heads * DK
    for start in range(0, rows, chunk):
        for first in range(0, conv_cols, DK):
            columns = slice(first, first + DK)
            summed = jnp.zeros((chunk, DK), f32)
            for tap in range(tap_count):
                offset = rim - (tap_count - 1) + start + tap
                summed += taps_ref[tap : tap + 1, columns] * extended[
                    offset : offset + chunk, columns
                ]
            value = summed / (1.0 + jnp.exp(-summed))
            if first < key_at:
                value = unit_rows(value) * DK**-0.5
            elif first < value_at:
                value = unit_rows(value)
            mixed[start : start + chunk, columns] = value
    row = lax.broadcasted_iota(jnp.int32, (chunk, chunk), 0)
    col = lax.broadcasted_iota(jnp.int32, (chunk, chunk), 1)
    inclusive, strict = row >= col, row > col
    lower = jnp.where(inclusive, 1.0, 0.0)
    across = lax.broadcasted_iota(jnp.int32, (DK, 2 * DK), 1)
    down = lax.broadcasted_iota(jnp.int32, (DK, 2 * DK), 0)
    carried[...] = jnp.broadcast_to(
        jnp.where(across == down + DK, 1.0, 0.0)[None], carried.shape
    )

    def advance(step, nothing):
        here = pl.ds(pl.multiple_of(step * chunk, chunk), chunk)
        fall = falls[here, :]
        strength = strengths[here, :]
        cumulative = contract(lower, fall, ((1,), (0,)), lax.Precision.HIGHEST)
        cumulative_rows = contract(fall, lower, ((0,), (1,)), lax.Precision.HIGHEST)
        owners = range(heads)
        queries = [mixed[here, k * DK : (k + 1) * DK] for k in range(key_heads)]
        keys = [mixed[here, key_at + k * DK : key_at + (k + 1) * DK] for k in range(key_heads)]
        dots = [
            contract_rows(jnp.concatenate([key, query], axis=0), key)
            for key, query in zip(keys, queries)
        ]
        totals = [cumulative[:, head : head + 1] for head in owners]
        kept = [
            jnp.where(
                inclusive,
                jnp.exp(jnp.where(inclusive, totals[head] - cumulative_rows[head : head + 1, :], 0.0)),
                0.0,
            )
            for head in owners
        ]
        own = [strength[:, head : head + 1] for head in owners]
        solvers = unit_inverses(
            [
                own[head] * jnp.where(strict, kept[head], 0.0) * dots[head // group][:chunk]
                for head in owners
            ]
        )
        risen = [jnp.exp(total) for total in totals]
        solved = [
            contract_close(
                solvers[head],
                own[head]
                * jnp.concatenate(
                    [
                        mixed[here, value_at + head * DK : value_at + (head + 1) * DK],
                        risen[head] * keys[head // group],
                    ],
                    axis=1,
                ),
            )
            for head in owners
        ]
        states = [carried[head] for head in owners]
        read = [
            contract_close(
                jnp.concatenate(
                    [solved[head][:, DK:], risen[head] * queries[head // group]], axis=0
                ),
                states[head],
            )
            for head in owners
        ]
        updates = [
            jnp.concatenate([solved[head][:, :DK], jnp.zeros((chunk, DK), f32)], axis=1)
            - read[head][:chunk]
            for head in owners
        ]
        for head in owners:
            last = totals[head][chunk - 1 :, :]
            leaving = jnp.exp(last - totals[head]) * keys[head // group]
            carried[head] = jnp.exp(last) * states[head] + contract_close(
                leaving.T, updates[head]
            )
        for head in owners:
            result = read[head][chunk:] + contract_close(
                kept[head] * dots[head // group][chunk:], updates[head]
            )
            core_ref[here, head * DK : (head + 1) * DK] = result[:, :DK]
            reading_ref[here, head * DK : (head + 1) * DK] = result[:, DK:]
        return nothing

    lax.fori_loop(0, rows // chunk, advance, 0)
    moved_ref[...] = carried[...].astype(bf16)


def project_kernel(place_ref, *refs, blocks, halos):
    row_refs, halo_refs = refs[:blocks], refs[blocks : blocks + halos]
    weight_refs, out_refs = refs[blocks + halos : blocks + halos + 6], refs[blocks + halos + 6 :]
    pieces = [ref[...] for ref in row_refs]
    rows = blocks * row_refs[0].shape[0]
    if halos:
        pieces.append(
            sum(
                jnp.where((place_ref[0] ^ step) == halos - 1, 1.0, 0.0) * ref[...].astype(f32)
                for step, ref in enumerate(halo_refs)
            ).astype(bf16)
        )
    pieces = jnp.concatenate(pieces, axis=0)
    qkv_ref, gate_ref, beta_ref, decay_ref = out_refs[:4]
    first = 0
    for weight_ref in weight_refs[:3]:
        product = contract(pieces, weight_ref[...], ((1,), (0,))).astype(bf16)
        last = first + weight_ref.shape[1]
        qkv_ref[:, first:last] = product[:rows]
        if halos:
            out_refs[4][:, first:last] = product[rows:].astype(f32)
        first = last
    pieces = pieces[:rows]
    gate_ref[...] = contract(pieces, weight_refs[3][...], ((1,), (0,))).astype(bf16)
    beta_ref[...] = contract(pieces, weight_refs[4][...], ((1,), (0,)))
    decay_ref[...] = contract(pieces, weight_refs[5][...], ((1,), (0,)))


def pair_kernel(second_ref, mine_ref, other_ref, moved_ref, transfer_ref):
    for head in range(mine_ref.shape[0]):
        mine, other = mine_ref[head].astype(f32), other_ref[head].astype(f32)
        late = second_ref[0] == 1
        earlier = jnp.where(late, other, mine).astype(bf16)
        later = jnp.where(late, mine, other)
        joined = contract(later[:, DK:].astype(bf16), earlier, ((1,), (0,)))
        moved_ref[head] = (joined[:, :DK] + later[:, :DK]).astype(bf16)
        transfer_ref[head] = joined[:, DK:].astype(bf16)


def finish_kernel(
    where_ref, state_ref, other_ref, core_ref, reading_ref, gate_ref, gain_ref, gated_ref
):
    states = []
    for head in range(state_ref.shape[0]):
        state = state_ref[head]
        passed = contract(other_ref[head, :, DK:], state, ((1,), (0,))) + other_ref[
            head, :, :DK
        ].astype(f32)
        states.append(jnp.where(where_ref[0] == 1, passed, state.astype(f32)))
    for head, state in enumerate(states):
        columns = slice(head * DK, (head + 1) * DK)
        core = core_ref[:, columns] + contract_close(reading_ref[:, columns], state)
        normal = (
            core
            * lax.rsqrt(jnp.mean(core * core, axis=-1, keepdims=True) + epsilon)
            * gain_ref[...]
        )
        gate = gate_ref[:, columns].astype(f32)
        gated_ref[:, columns] = (normal * (gate / (1.0 + jnp.exp(-gate)))).astype(bf16)


def output_kernel(*refs, blocks, begun):
    row_refs, weight_refs, out_ref = refs[:blocks], refs[blocks : -1 - begun], refs[-1]
    total = refs[-2][...] if begun else 0.0
    pieces = iter(weight_refs)
    for rows_ref in row_refs:
        at = 0
        while at < rows_ref.shape[1]:
            weight_ref = next(pieces)
            depth = weight_ref.shape[0]
            total += contract(rows_ref[:, at : at + depth], weight_ref[...], ((1,), (0,)))
            at += depth
    out_ref[...] = total.astype(out_ref.dtype)


def on_device(
    stream,
    moe_gain,
    router,
    expert_ids,
    expert_gate,
    expert_up,
    expert_down,
    mixer_gain,
    query_weight,
    key_weight,
    value_weight,
    output_gate,
    beta_weight,
    decay_weight,
    query_conv,
    key_conv,
    value_conv,
    decay_log,
    decay_bias,
    head_gain,
    out_weight,
):
    ctx_count = lax.axis_size("ctx")
    head_count = lax.axis_size("head")
    sources = ctx_count * head_count
    ctx_place = lax.axis_index("ctx")
    experts = (stream, moe_gain, router, expert_ids, expert_gate, expert_up, expert_down)
    cut = out_weight.shape[0] * 5 // 128 * 16
    out_halves = (out_weight[:cut], out_weight[cut:])
    if 2 * sources * stream.size <= GATHER_LIMIT and head_count == 4 and ctx_count in (6, 8):
        moe_out = expert_layer_gathered(*experts, sources, out_halves)
    else:
        moe_out = expert_layer_sent(*experts, sources)
    mixer_in = rms_rows(
        stream.astype(jnp.float32) + moe_out.astype(jnp.float32), mixer_gain
    ).astype(jnp.bfloat16)
    head_place = lax.axis_index("head")

    def crossed(value, step):
        pairs = [(source, source ^ step) for source in range(head_count)]
        return lax.ppermute(value, "head", pairs)


    def from_chip(value, *earlier):
        return [after(value, *earlier) if earlier else value, crossed(value, 1)]

    def from_others(value, *earlier):
        received = []
        for step in range(2, head_count, 2):
            part = crossed(value, step)
            received += [part, crossed(after(part, *earlier) if earlier else part, 1)]
        return received

    in_vmem = pl.BlockSpec(memory_space=pltpu.VMEM)
    in_smem = pl.BlockSpec(memory_space=pltpu.SMEM)
    tok_rows, width = stream.shape
    rows = tok_rows * head_count
    key_cols, value_cols = query_weight.shape[1], value_weight.shape[1]
    heads = beta_weight.shape[1]
    rim_len = 16
    halo = passed_along(mixer_in[tok_rows - rim_len :], "ctx", 1)
    halos = from_chip(halo) + from_others(halo)
    conv_cols = 2 * key_cols + value_cols
    matrices = (
        query_weight, key_weight, value_weight, output_gate, beta_weight, decay_weight
    )

    def project(pieces, halos):
        count = len(pieces) * tok_rows
        shapes = [
            jax.ShapeDtypeStruct((count, conv_cols), bf16),
            jax.ShapeDtypeStruct((count, value_cols), bf16),
            jax.ShapeDtypeStruct((count, heads), f32),
            jax.ShapeDtypeStruct((count, heads), f32),
        ]
        if halos:
            shapes.append(jax.ShapeDtypeStruct((rim_len, conv_cols), f32))
        return pl.pallas_call(
            functools.partial(project_kernel, blocks=len(pieces), halos=len(halos)),
            in_specs=[in_smem] + [in_vmem] * (len(pieces) + len(halos) + 6),
            out_shape=shapes,
            compiler_params=pltpu.CompilerParams(vmem_limit_bytes=28 << 20),
            cost_estimate=worth(4),
            name="project",
        )(head_place.reshape(1), *pieces, *halos, *matrices)

    near_raw = project(from_chip(mixer_in, halo), [])
    far_pieces = from_others(mixer_in, near_raw[0], halos[2])
    far_raw = project(far_pieces, halos)
    rim = far_raw[4]
    gate_raw = jnp.concatenate([near_raw[1], far_raw[1]], axis=0)
    key_heads = key_cols // DK
    taps = jnp.concatenate([query_conv, key_conv, value_conv], axis=1)
    rates = jnp.stack([decay_log, decay_bias])
    chunk = math.gcd(rows, CHUNK)
    core, reading, moved = pl.pallas_call(
        functools.partial(delta_kernel, key_heads=key_heads, chunk=chunk, tok_rows=tok_rows),
        in_specs=[in_smem] + [in_vmem] * 9,
        out_shape=(
            jax.ShapeDtypeStruct((rows, value_cols), f32),
            jax.ShapeDtypeStruct((rows, value_cols), f32),
            jax.ShapeDtypeStruct((heads, DK, 2 * DK), bf16),
        ),
        scratch_shapes=[
            pltpu.VMEM((rows + rim_len, conv_cols), f32),
            pltpu.VMEM((rows, conv_cols), f32),
            pltpu.VMEM((rows, heads), f32),
            pltpu.VMEM((rows, heads), f32),
            pltpu.VMEM((heads, DK, 2 * DK), f32),
        ],
        compiler_params=pltpu.CompilerParams(vmem_limit_bytes=24 << 20),
        cost_estimate=worth(16),
        name="delta",
    )(
        head_place.reshape(1),
        *(array for kind in (0, 2, 3) for array in (near_raw[kind], far_raw[kind])),
        rim,
        taps,
        rates,
    )
    start_upper, start_lower = after(out_halves[0], far_pieces[-1]), after(out_halves[1], moved)
    upper = [crossed(start_upper, step) for step in range(2, head_count, 2)]
    lower = [crossed(start_lower, step) for step in range(2, head_count, 2)]

    in_pair = (ctx_place % 2).reshape(1)
    other = lax.ppermute(moved, "ctx", [(place, place ^ 1) for place in range(ctx_count)])
    other = after(other, *upper)
    state_shape = jax.ShapeDtypeStruct((heads, DK, DK), bf16)
    added, transfer = pl.pallas_call(
        pair_kernel,
        in_specs=[in_smem, in_vmem, in_vmem],
        out_shape=[state_shape, state_shape],
        compiler_params=pltpu.CompilerParams(vmem_limit_bytes=8 << 20),
        name="pair",
    )(in_pair, moved, other)
    state = passed_along(added, "ctx", 2)
    for hop in range(ctx_count // 2 - 2):
        leaving = jnp.einsum("hij,hjk->hik", transfer, state, preferred_element_type=f32)
        leaving = (leaving + added.astype(f32)).astype(bf16)
        if hop == ctx_count // 2 - 3:
            leaving = after(leaving, *lower)
        state = passed_along(leaving, "ctx", 2)

    gated = pl.pallas_call(
        finish_kernel,
        grid_spec=pltpu.PrefetchScalarGridSpec(
            num_scalar_prefetch=1,
            grid=(head_count,),
            in_specs=[whole_ref(state), whole_ref(other)]
            + [
                pl.BlockSpec((tok_rows, value_cols), lambda step, where: (where[1] ^ step, 0)),
                pl.BlockSpec((tok_rows, value_cols), lambda step, where: (where[1] ^ step, 0)),
                pl.BlockSpec((tok_rows, value_cols), lambda step, where: (step, 0)),
                pl.BlockSpec((1, DK), lambda step, where: (0, 0)),
            ],
            out_specs=pl.BlockSpec((tok_rows, value_cols), lambda step, where: (step, 0)),
        ),
        out_shape=jax.ShapeDtypeStruct((rows, value_cols), bf16),
        compiler_params=pltpu.CompilerParams(vmem_limit_bytes=12 << 20),
        name="finish",
    )(
        jnp.stack([ctx_place % 2, head_place]),
        state,
        other,
        core,
        reading,
        gate_raw,
        head_gain.reshape(1, -1),
    )
    gated_parts = []
    for step in range(head_count):
        part = gated[step * tok_rows : (step + 1) * tok_rows]
        gated_parts.append(crossed(part, step) if step else part)
    near_weights = [out_weight, crossed(after(out_weight, moved), 1)]
    far_weights = []
    for shard in zip(upper, lower):
        far_weights += shard
        far_weights += [crossed(after(part, state), 1) for part in shard]

    def multiplied(parts, weights, begun, kind):
        columns = pl.BlockSpec((tok_rows, width // 4), lambda n: (0, n))
        return pl.pallas_call(
            functools.partial(output_kernel, blocks=len(parts), begun=len(begun)),
            grid=(4,),
            in_specs=[whole_ref(part) for part in parts]
            + [pl.BlockSpec((part.shape[0], width // 4), lambda n: (0, n)) for part in weights]
            + [columns] * len(begun),
            out_specs=columns,
            out_shape=jax.ShapeDtypeStruct(stream.shape, kind),
            compiler_params=pltpu.CompilerParams(vmem_limit_bytes=20 << 20),
            cost_estimate=worth(3),
            name="output",
        )(*parts, *weights, *begun)

    begun = multiplied(gated_parts[:2], near_weights, [], f32)
    mixer_out = multiplied(gated_parts[2:], far_weights, [begun], bf16)
    return (moe_out, mixer_out)


def solution(mesh):
    return jax.shard_map(
        on_device,
        mesh=mesh,
        in_specs=(
            P(("ctx", "head"), None),
            P(),
            P(),
            P(("ctx", "head"), None),
            P(("ctx", "head"), None, None),
            P(("ctx", "head"), None, None),
            P(("ctx", "head"), None, None),
            P(),
            P(None, "head"),
            P(None, "head"),
            P(None, "head"),
            P(None, "head"),
            P(None, "head"),
            P(None, "head"),
            P(None, "head"),
            P(None, "head"),
            P(None, "head"),
            P("head"),
            P("head"),
            P(),
            P("head", None),
        ),
        out_specs=(P(("ctx", "head"), None), P(("ctx", "head"), None)),
        check_vma=False,
    )
```

```python
import functools
import math

import jax
import jax.numpy as jnp
from jax import lax
from jax.experimental import pallas as pl
from jax.experimental.pallas import tpu as pltpu
from jax.sharding import PartitionSpec as P

DK = 128
CHUNK = 128
GATHER_LIMIT = 32 << 20


epsilon = 1e-06
f32 = jnp.float32
bf16 = jnp.bfloat16


def passed_along(value, axis, steps):
    count = lax.axis_size(axis)
    first, last = (max(0, -steps), min(count, count - steps))
    return lax.ppermute(value, axis, [(source, source + steps) for source in range(first, last)])


def rms_rows(values, gain):
    values = values.astype(jnp.float32)
    scale = lax.rsqrt(jnp.mean(values * values, axis=-1, keepdims=True) + epsilon)
    return values * scale * gain


def after(value, *earlier):
    return lax.optimization_barrier((value, *earlier))[0]


def whole_ref(array):
    return pl.BlockSpec(array.shape, lambda *_: (0,) * array.ndim)


def worth(microseconds):
    return pl.CostEstimate(
        flops=int(microseconds * 1.15e9), bytes_accessed=int(microseconds * 1e6), transcendentals=0
    )


def contract(a, b, dims, precision=None):
    return lax.dot_general(
        a, b, (dims, ((), ())), precision=precision, preferred_element_type=f32
    )


def parts(values):
    high = values.astype(bf16)
    return high, (values - high.astype(f32)).astype(bf16)


def contract_close(a, b):
    a_high, a_low = parts(a)
    b_high, b_low = parts(b)
    doubled = jnp.concatenate([a_high, a_low], axis=1)
    if 2 * b.shape[1] <= 2 * DK:
        both = jnp.concatenate([b_high, b_low], axis=1)
        product = contract(doubled, jnp.concatenate([both, both], axis=0), ((1,), (0,)))
        return product[:, : b.shape[1]] + product[:, b.shape[1] :]
    return contract(
        doubled, jnp.concatenate([b_high, b_high], axis=0), ((1,), (0,))
    ) + contract(a_high, b_low, ((1,), (0,)))


def contract_rows(a, b):
    a_high, a_low = parts(a)
    b_high, b_low = parts(b)
    product = contract(
        jnp.concatenate([a_high, a_low], axis=1),
        jnp.concatenate(
            [jnp.concatenate([b_high, b_high], axis=1), jnp.concatenate([b_low, b_low], axis=1)],
            axis=0,
        ),
        ((1,), (1,)),
    )
    return product[:, : b.shape[0]] + product[:, b.shape[0] :]


def pair_routes(cols, picker, lines, tok_rows, slots):
    rows = cols.shape[0]
    weight_rows = contract(picker, cols, ((1,), (1,)))
    named = weight_rows > 0
    before = lax.broadcasted_iota(jnp.int32, (rows, rows), 0)
    after = lax.broadcasted_iota(jnp.int32, (rows, rows), 1)
    earlier = (before < after) & (before // tok_rows == after // tok_rows)
    rank = contract(
        jnp.where(named, 1.0, 0.0).astype(bf16),
        jnp.where(earlier, 1.0, 0.0).astype(bf16),
        ((1,), (0,)),
    )
    first_slot = lax.broadcasted_iota(jnp.int32, rank.shape, 1) // tok_rows * slots
    rank = jnp.where(named, rank.astype(jnp.int32) + first_slot, -1)
    slot = lax.broadcasted_iota(jnp.int32, (rows // tok_rows * slots, rows), 0)
    picks = [jnp.where(slot == rank[line : line + 1], 1.0, 0.0) for line in range(lines)]
    return weight_rows, picks


def collect_kernel(block_00, block_10, block_01, block_11, picker_ref, own_ref, send_ref, *, slots):
    local_experts, taken, width = own_ref.shape
    tok_rows = block_00.shape[0]
    pair = taken // 2
    for at, pair_refs in enumerate(((block_01, block_11), (block_00, block_10))):
        rows = jnp.concatenate([ref[...] for ref in pair_refs], axis=0)
        _, picks = pair_routes(
            rows[:, width:], picker_ref[...], 2 * local_experts, tok_rows, slots
        )
        picked = contract(
            jnp.concatenate(picks, axis=0).astype(bf16), rows[:, :width], ((1,), (0,))
        ).astype(bf16)
        for expert in range(local_experts):
            there = slice(at * pair, (at + 1) * pair)
            own_ref[expert, there, :] = picked[expert * pair : (expert + 1) * pair]
            line = local_experts + expert
            send_ref[expert, there, :] = picked[line * pair : (line + 1) * pair]


def expert_kernel(*refs):
    *row_refs, gate_ref, up_ref, down_ref, own_ref, send_ref = refs
    half = len(row_refs) // 2
    for sources, out_ref in ((row_refs[half:], send_ref), (row_refs[:half], own_ref)):
        rows = jnp.concatenate([ref[0] for ref in sources], axis=0)
        gate = contract(rows, gate_ref[0], ((1,), (0,)))
        up = contract(rows, up_ref[0], ((1,), (0,)))
        hidden = (gate / (1.0 + jnp.exp(-gate)) * up).astype(bf16)
        out_ref[0] = contract(hidden, down_ref[0], ((1,), (0,))).astype(bf16)


def spread_kernel(*refs, slots, places):
    *cols_refs, picker_ref, own_ref, got_ref, far_ref, near_ref, here_ref = refs
    local_experts = own_ref.shape[0]
    tok_rows = cols_refs[0].shape[0]
    pair = 2 * slots
    for group, place in enumerate(places):
        cols_00, cols_10, cols_01, cols_11 = cols_refs[4 * group : 4 * group + 4]
        for at, pair_refs in enumerate(((cols_01, cols_11), (cols_00, cols_10))):
            cols = jnp.concatenate([ref[...] for ref in pair_refs], axis=0)
            weight_rows, picks = pair_routes(
                cols, picker_ref[...], 2 * local_experts, tok_rows, slots
            )
            first = (2 * place + at) * pair
            scaled = []
            for line, pick in enumerate(picks):
                result_ref = (own_ref, got_ref)[line // local_experts]
                result = result_ref[line % local_experts, first : first + pair, :]
                weight = jnp.sum(pick * weight_rows[line : line + 1], axis=1, keepdims=True)
                scaled.append((result.astype(f32) * weight).astype(bf16))
            summed = contract(
                jnp.concatenate(picks, axis=0).astype(bf16),
                jnp.concatenate(scaled, axis=0),
                ((0,), (0,)),
            ).astype(bf16)
            if at == 0:
                far_ref[group, 0] = summed[:tok_rows]
                far_ref[group, 1] = summed[tok_rows:]
            else:
                here_ref[group] = summed[:tok_rows]
                near_ref[group] = summed[tok_rows:]


def expert_layer_gathered(
    stream,
    moe_gain,
    router,
    expert_ids,
    expert_gate,
    expert_up,
    expert_down,
    sources,
    early,
):
    tok_rows, width = stream.shape
    local_experts, _, hidden_width = expert_gate.shape
    experts_all = local_experts * sources
    depth = sources // 8
    place = lax.axis_index(("ctx", "head"))

    def sent(value, move):
        pairs = []
        for device in range(sources):
            z, y, x, core = device // 8, device // 4 % 2, device // 2 % 2, device % 2
            z, y, x, core = move(z, y, x, core)
            pairs.append((device, ((z * 2 + y) * 2 + x) * 2 + core))
        return lax.ppermute(value, ("ctx", "head"), pairs)

    def lifted(value, steps):
        return sent(value, lambda z, y, x, core: ((z + steps) % depth, y, x, core))

    def first(value):
        return sent(value, lambda z, y, x, core: (z, y ^ (1 - core), x ^ core, core))

    def second(value):
        return sent(value, lambda z, y, x, core: (z, y ^ core, x ^ (1 - core), core))

    def swapped(value):
        return sent(value, lambda z, y, x, core: (z, y, x, 1 - core))

    normed = rms_rows(stream, moe_gain).astype(bf16)
    logits = jnp.dot(normed, router, preferred_element_type=f32)
    named = jnp.any(
        expert_ids[:, :, None] == jnp.arange(experts_all, dtype=jnp.int32)[None, None, :], axis=1
    )
    raised = jnp.where(named, jnp.exp(logits), 0.0)
    weights = raised / jnp.sum(raised, axis=1, keepdims=True)
    coarse = lax.reduce_precision(weights, 8, 7)
    packet = jnp.concatenate(
        [normed, coarse.astype(bf16), (weights - coarse).astype(bf16)], axis=1
    )

    capacity = (11 * tok_rows * expert_ids.shape[1] + 10 * experts_all - 1) // (10 * experts_all)
    slots = -(-capacity // 8) * 8
    taken = 4 * slots
    column = jnp.arange(2 * experts_all, dtype=jnp.int32)[None, :] % experts_all
    line = jnp.arange(16, dtype=jnp.int32)[:, None]
    owner = jnp.where(line < local_experts, place, place ^ 1)
    picker = (
        (line < 2 * local_experts) & (column == owner * local_experts + line % local_experts)
    ).astype(bf16)

    order = [0, *range(depth - 1, 0, -1)]
    own_rows, got_rows, outcome = {}, {}, {}
    blocks = {}
    mine = packet
    for at, steps in enumerate(order):
        if steps:
            source = packet if steps == 1 else mine
            earlier = [blocks[order[at - 1]][0]] if at > 1 else []
            if at > 1:
                earlier += blocks[order[at - 2]][1:3]
            if earlier:
                source = after(source, *earlier)
            mine = lifted(source, 1 if steps == 1 else -1)
        onward = mine
        if at:
            onward = after(mine, *blocks[order[at - 1]][1:3])
        near = first(onward)
        blocks[steps] = (mine, near, second(onward), second(near))

    picked_spec = pl.BlockSpec((local_experts, taken, width), lambda g: (0, 0, 0))

    def collect(steps, *earlier):
        rows = blocks[steps][0]
        own, send = pl.pallas_call(
            functools.partial(collect_kernel, slots=slots),
            grid=(1,),
            in_specs=[whole_ref(packet)] * 4 + [whole_ref(picker)],
            out_specs=[picked_spec] * 2,
            out_shape=[jax.ShapeDtypeStruct((local_experts, taken, width), bf16)] * 2,
            compiler_params=pltpu.CompilerParams(vmem_limit_bytes=24 << 20),
            cost_estimate=worth(2),
            name="collect",
        )(after(rows, *earlier) if earlier else rows, *blocks[steps][1:], picker)
        own_rows[steps] = own
        got_rows[steps] = swapped(send)

    def run_experts(members, *earlier):
        row_spec = pl.BlockSpec((1, taken, width), lambda e: (e, 0, 0))
        out_spec = pl.BlockSpec((1, len(members) * taken, width), lambda e: (e, 0, 0))
        results, send_back = pl.pallas_call(
            expert_kernel,
            grid=(local_experts,),
            in_specs=[row_spec] * (2 * len(members))
            + [
                pl.BlockSpec((1, width, hidden_width), lambda e: (e, 0, 0)),
                pl.BlockSpec((1, width, hidden_width), lambda e: (e, 0, 0)),
                pl.BlockSpec((1, hidden_width, width), lambda e: (e, 0, 0)),
            ],
            out_specs=[out_spec] * 2,
            out_shape=[jax.ShapeDtypeStruct((local_experts, len(members) * taken, width), bf16)]
            * 2,
            compiler_params=pltpu.CompilerParams(vmem_limit_bytes=40 << 20),
            cost_estimate=worth(4 + 3 * len(members) if len(members) > 1 else 1),
            name="experts",
        )(
            after(own_rows[members[0]], *earlier),
            *[own_rows[member] for member in members[1:]],
            *[got_rows[member] for member in members],
            expert_gate,
            expert_up,
            expert_down,
        )
        got_back = swapped(send_back)
        for at, member in enumerate(members):
            outcome[member] = (at, results, got_back)

    def spread(members):
        places = [outcome[member][0] for member in members]
        _, results, got_back = outcome[members[0]]
        cols_spec = pl.BlockSpec(
            (tok_rows, 2 * experts_all), lambda g: (0, width // (2 * experts_all))
        )
        row_shape = jax.ShapeDtypeStruct((len(members), tok_rows, width), bf16)
        far_shape = jax.ShapeDtypeStruct((len(members), 2, tok_rows, width), bf16)
        return pl.pallas_call(
            functools.partial(spread_kernel, slots=slots, places=places),
            grid=(1,),
            in_specs=[cols_spec] * (4 * len(members))
            + [whole_ref(picker), whole_ref(results), whole_ref(results)],
            out_specs=[whole_ref(far_shape), whole_ref(row_shape), whole_ref(row_shape)],
            out_shape=[far_shape, row_shape, row_shape],
            compiler_params=pltpu.CompilerParams(vmem_limit_bytes=28 << 20),
            cost_estimate=worth(1),
            name="spread",
        )(*(block for member in members for block in blocks[member]), picker, results, got_back)

    last, batch = order[-1], order[-2:0:-1]
    for steps in order[:-2]:
        collect(steps, blocks[order[-2]][0])
    collect(order[-2], *blocks[last][:3])
    run_experts(order[:-1])
    ready = {steps: spread([steps]) for steps in batch}
    collect(last, *[far for far, _, _ in ready.values()])
    run_experts([last])
    ready[last], ready[0] = spread([last]), spread([0])

    def joined(steps, direct, diagonal):
        _, near, here = ready[steps]
        near = first((near[0].astype(f32) + diagonal.astype(f32)).astype(bf16))
        return here[0].astype(f32) + direct.astype(f32) + near.astype(f32)

    moving = []
    for at, steps in enumerate(batch):
        across = second(ready[steps][0])
        total = joined(steps, across[0, 0], across[0, 1])
        if moving:
            total += moving[-1].astype(f32)
        moving.append(lifted(total.astype(bf16), 1))
    across = after(second(ready[last][0]), moving[0])
    total = joined(last, across[0, 0], across[0, 1])
    rising = lifted(total.astype(bf16), -1)
    far = ready[0][0]
    diagonal = after(second(far[0, 1]), moving[-1])
    total = joined(0, second(far[0, 0]), diagonal)
    total += moving[-1].astype(f32) + rising.astype(f32)
    return after(total, *early).astype(bf16)


def expert_layer_sent(
    stream, moe_gain, router, expert_ids, expert_gate, expert_up, expert_down, sources
):
    tok_rows, model_width = stream.shape
    top_count = expert_ids.shape[1]
    local_experts = expert_gate.shape[0]
    experts_all = local_experts * sources
    capacity = (11 * tok_rows * top_count + 10 * experts_all - 1) // (10 * experts_all)
    normed = rms_rows(stream, moe_gain).astype(jnp.bfloat16)
    logits = jnp.dot(normed, router, preferred_element_type=jnp.float32)
    chosen = jnp.take_along_axis(logits, expert_ids, axis=1)
    raised = jnp.exp(chosen)
    weights = raised / jnp.sum(raised, axis=1, keepdims=True)
    flat_ids = expert_ids.reshape(-1)
    matches = (flat_ids[:, None] == jnp.arange(experts_all, dtype=jnp.int32)[None, :]).astype(
        jnp.int32
    )
    slot_index = jnp.sum((jnp.cumsum(matches, axis=0) - 1) * matches, axis=1)
    places = flat_ids * capacity + slot_index
    token_rows = jnp.arange(tok_rows * top_count, dtype=jnp.int32) // top_count
    outgoing = (
        jnp.zeros((experts_all * capacity, model_width), jnp.bfloat16)
        .at[places]
        .set(normed[token_rows])
    )
    outgoing = outgoing.reshape(sources, local_experts, capacity, model_width)
    received = lax.all_to_all(outgoing, ("ctx", "head"), split_axis=0, concat_axis=0, tiled=True)
    gate_part = jnp.einsum(
        "nesd,edh->nesh", received, expert_gate, preferred_element_type=jnp.float32
    )
    up_part = jnp.einsum("nesd,edh->nesh", received, expert_up, preferred_element_type=jnp.float32)
    hidden = (jax.nn.silu(gate_part) * up_part).astype(jnp.bfloat16)
    returned = lax.all_to_all(
        jnp.einsum(
            "nesh,ehd->nesd", hidden, expert_down, preferred_element_type=jnp.float32
        ).astype(jnp.bfloat16),
        ("ctx", "head"),
        split_axis=0,
        concat_axis=0,
        tiled=True,
    )
    gathered_rows = returned.reshape(experts_all * capacity, model_width)[places].reshape(
        tok_rows, top_count, model_width
    )
    return jnp.sum(weights[:, :, None] * gathered_rows.astype(jnp.float32), axis=1).astype(
        jnp.bfloat16
    )


def unit_inverses(strict_parts):
    size = strict_parts[0].shape[0]
    row = lax.broadcasted_iota(jnp.int32, (size, size), 0)
    col = lax.broadcasted_iota(jnp.int32, (size, size), 1)
    unit = jnp.where(row == col, 1.0, 0.0)
    joining = (row // 2 == col // 2) & (row != col)
    inverses = [unit - jnp.where(joining, part, 0.0) for part in strict_parts]
    half = 2
    while half < size:
        joining = (row // (2 * half) == col // (2 * half)) & (row // half != col // half)
        corners = [jnp.where(joining, part, 0.0) for part in strict_parts]
        if half < 8:
            steps = [contract_close(c, inverse) for c, inverse in zip(corners, inverses)]
            moves = [contract_close(inverse, step) for inverse, step in zip(inverses, steps)]
            inverses = [inverse - move for inverse, move in zip(inverses, moves)]
        else:
            starts = range(0, size, 2 * half)

            def lower_rows(array):
                return jnp.concatenate([array[at + half : at + 2 * half] for at in starts], axis=0)

            zeros = jnp.zeros((half, size), f32)
            steps = [
                contract_close(lower_rows(c), inverse) for c, inverse in zip(corners, inverses)
            ]
            steps = [
                jnp.concatenate(
                    [
                        piece
                        for at in range(0, size // 2, half)
                        for piece in (zeros, step[at : at + half])
                    ],
                    axis=0,
                )
                for step in steps
            ]
            lowers = [lower_rows(inverse) for inverse in inverses]
            lowers = [lower - contract_close(lower, step) for lower, step in zip(lowers, steps)]
            inverses = [
                jnp.concatenate(
                    [
                        piece
                        for at in starts
                        for piece in (
                            inverse[at : at + half],
                            lower[at // 2 : at // 2 + half],
                        )
                    ],
                    axis=0,
                )
                for inverse, lower in zip(inverses, lowers)
            ]
        half *= 2
    return inverses


def unit_rows(rows):
    return rows * lax.rsqrt(jnp.sum(rows * rows, axis=-1, keepdims=True) + epsilon)


def delta_kernel(
    place_ref,
    near_raw,
    far_raw,
    near_beta,
    far_beta,
    near_decay,
    far_decay,
    rim_ref,
    taps_ref,
    rate_ref,
    core_ref,
    reading_ref,
    moved_ref,
    extended,
    mixed,
    strengths,
    falls,
    carried,
    *,
    key_heads,
    chunk,
    tok_rows,
):
    rows, conv_cols = near_raw.shape[0] + far_raw.shape[0], near_raw.shape[1]
    heads = moved_ref.shape[0]
    group = heads // key_heads
    tap_count = taps_ref.shape[0]
    rim = rim_ref.shape[0]
    extended[0:rim, :] = rim_ref[...]
    step = 0
    for part_refs in ((near_raw, near_beta, near_decay), (far_raw, far_beta, far_decay)):
        for first in range(0, part_refs[0].shape[0], tok_rows):
            at = pl.multiple_of((place_ref[0] ^ step) * tok_rows, tok_rows)
            part = slice(first, first + tok_rows)
            extended[pl.ds(rim + at, tok_rows), :] = part_refs[0][part, :].astype(f32)
            strengths[pl.ds(at, tok_rows), :] = 1.0 / (1.0 + jnp.exp(-part_refs[1][part, :]))
            shifted = part_refs[2][part, :] + rate_ref[1:2, :]
            softened = jnp.maximum(shifted, 0.0) + jnp.log1p(jnp.exp(-jnp.abs(shifted)))
            falls[pl.ds(at, tok_rows), :] = -jnp.exp(rate_ref[0:1, :]) * softened
            step += 1
    key_at, value_at = key_heads * DK, 2 * key_heads * DK
    for start in range(0, rows, chunk):
        for first in range(0, conv_cols, DK):
            columns = slice(first, first + DK)
            summed = jnp.zeros((chunk, DK), f32)
            for tap in range(tap_count):
                offset = rim - (tap_count - 1) + start + tap
                summed += taps_ref[tap : tap + 1, columns] * extended[
                    offset : offset + chunk, columns
                ]
            value = summed / (1.0 + jnp.exp(-summed))
            if first < key_at:
                value = unit_rows(value) * DK**-0.5
            elif first < value_at:
                value = unit_rows(value)
            mixed[start : start + chunk, columns] = value
    row = lax.broadcasted_iota(jnp.int32, (chunk, chunk), 0)
    col = lax.broadcasted_iota(jnp.int32, (chunk, chunk), 1)
    inclusive, strict = row >= col, row > col
    lower = jnp.where(inclusive, 1.0, 0.0)
    across = lax.broadcasted_iota(jnp.int32, (DK, 2 * DK), 1)
    down = lax.broadcasted_iota(jnp.int32, (DK, 2 * DK), 0)
    carried[...] = jnp.broadcast_to(
        jnp.where(across == down + DK, 1.0, 0.0)[None], carried.shape
    )

    def advance(step, nothing):
        here = pl.ds(pl.multiple_of(step * chunk, chunk), chunk)
        fall = falls[here, :]
        strength = strengths[here, :]
        cumulative = contract(lower, fall, ((1,), (0,)), lax.Precision.HIGHEST)
        cumulative_rows = contract(fall, lower, ((0,), (1,)), lax.Precision.HIGHEST)
        owners = range(heads)
        queries = [mixed[here, k * DK : (k + 1) * DK] for k in range(key_heads)]
        keys = [mixed[here, key_at + k * DK : key_at + (k + 1) * DK] for k in range(key_heads)]
        dots = [
            contract_rows(jnp.concatenate([key, query], axis=0), key)
            for key, query in zip(keys, queries)
        ]
        totals = [cumulative[:, head : head + 1] for head in owners]
        kept = [
            jnp.where(
                inclusive,
                jnp.exp(jnp.where(inclusive, totals[head] - cumulative_rows[head : head + 1, :], 0.0)),
                0.0,
            )
            for head in owners
        ]
        own = [strength[:, head : head + 1] for head in owners]
        solvers = unit_inverses(
            [
                own[head] * jnp.where(strict, kept[head], 0.0) * dots[head // group][:chunk]
                for head in owners
            ]
        )
        risen = [jnp.exp(total) for total in totals]
        solved = [
            contract_close(
                solvers[head],
                own[head]
                * jnp.concatenate(
                    [
                        mixed[here, value_at + head * DK : value_at + (head + 1) * DK],
                        risen[head] * keys[head // group],
                    ],
                    axis=1,
                ),
            )
            for head in owners
        ]
        states = [carried[head] for head in owners]
        read = [
            contract_close(
                jnp.concatenate(
                    [solved[head][:, DK:], risen[head] * queries[head // group]], axis=0
                ),
                states[head],
            )
            for head in owners
        ]
        updates = [
            jnp.concatenate([solved[head][:, :DK], jnp.zeros((chunk, DK), f32)], axis=1)
            - read[head][:chunk]
            for head in owners
        ]
        for head in owners:
            last = totals[head][chunk - 1 :, :]
            leaving = jnp.exp(last - totals[head]) * keys[head // group]
            carried[head] = jnp.exp(last) * states[head] + contract_close(
                leaving.T, updates[head]
            )
        for head in owners:
            result = read[head][chunk:] + contract_close(
                kept[head] * dots[head // group][chunk:], updates[head]
            )
            core_ref[here, head * DK : (head + 1) * DK] = result[:, :DK]
            reading_ref[here, head * DK : (head + 1) * DK] = result[:, DK:]
        return nothing

    lax.fori_loop(0, rows // chunk, advance, 0)
    moved_ref[...] = carried[...].astype(bf16)


def project_kernel(place_ref, *refs, blocks, halos):
    row_refs, halo_refs = refs[:blocks], refs[blocks : blocks + halos]
    weight_refs, out_refs = refs[blocks + halos : blocks + halos + 6], refs[blocks + halos + 6 :]
    pieces = [ref[...] for ref in row_refs]
    rows = blocks * row_refs[0].shape[0]
    if halos:
        pieces.append(
            sum(
                jnp.where((place_ref[0] ^ step) == halos - 1, 1.0, 0.0) * ref[...].astype(f32)
                for step, ref in enumerate(halo_refs)
            ).astype(bf16)
        )
    pieces = jnp.concatenate(pieces, axis=0)
    qkv_ref, gate_ref, beta_ref, decay_ref = out_refs[:4]
    first = 0
    for weight_ref in weight_refs[:3]:
        product = contract(pieces, weight_ref[...], ((1,), (0,))).astype(bf16)
        last = first + weight_ref.shape[1]
        qkv_ref[:, first:last] = product[:rows]
        if halos:
            out_refs[4][:, first:last] = product[rows:].astype(f32)
        first = last
    pieces = pieces[:rows]
    gate_ref[...] = contract(pieces, weight_refs[3][...], ((1,), (0,))).astype(bf16)
    beta_ref[...] = contract(pieces, weight_refs[4][...], ((1,), (0,)))
    decay_ref[...] = contract(pieces, weight_refs[5][...], ((1,), (0,)))


def pair_kernel(second_ref, mine_ref, other_ref, joined_ref):
    late = second_ref[0] == 1
    for head in range(mine_ref.shape[0]):
        mine, other = mine_ref[head].astype(f32), other_ref[head].astype(f32)
        earlier = jnp.where(late, other, mine).astype(bf16)
        later = jnp.where(late, mine, other)
        joined = contract(later[:, DK:].astype(bf16), earlier, ((1,), (0,)))
        joined_ref[head, :, :DK] = (joined[:, :DK] + later[:, :DK]).astype(bf16)
        joined_ref[head, :, DK:] = joined[:, DK:].astype(bf16)


def finish_kernel(
    where_ref,
    near_pairs_ref,
    far_pairs_ref,
    other_ref,
    core_ref,
    reading_ref,
    near_gate,
    far_gate,
    gain_ref,
    gated_ref,
):
    states = []
    for head in range(other_ref.shape[0]):
        state = contract(near_pairs_ref[head, :, DK:], far_pairs_ref[head], ((1,), (0,)))
        state += near_pairs_ref[head, :, :DK].astype(f32)
        passed = contract(other_ref[head, :, DK:], state.astype(bf16), ((1,), (0,)))
        passed += other_ref[head, :, :DK].astype(f32)
        states.append(jnp.where(where_ref[0] == 1, passed, state))
    gates = jnp.where(pl.program_id(0) < 2, near_gate[...].astype(f32), far_gate[...].astype(f32))
    for head, state in enumerate(states):
        columns = slice(head * DK, (head + 1) * DK)
        core = core_ref[:, columns] + contract_close(reading_ref[:, columns], state)
        normal = (
            core
            * lax.rsqrt(jnp.mean(core * core, axis=-1, keepdims=True) + epsilon)
            * gain_ref[...]
        )
        gate = gates[:, columns]
        gated_ref[:, columns] = (normal * (gate / (1.0 + jnp.exp(-gate)))).astype(bf16)


def output_kernel(*refs, blocks, begun):
    row_refs, weight_refs, out_ref = refs[:blocks], refs[blocks : -1 - begun], refs[-1]
    total = refs[-2][...] if begun else 0.0
    pieces = iter(weight_refs)
    for rows_ref in row_refs:
        at = 0
        while at < rows_ref.shape[1]:
            weight_ref = next(pieces)
            depth = weight_ref.shape[0]
            total += contract(rows_ref[:, at : at + depth], weight_ref[...], ((1,), (0,)))
            at += depth
    out_ref[...] = total.astype(out_ref.dtype)


def on_device(
    stream,
    moe_gain,
    router,
    expert_ids,
    expert_gate,
    expert_up,
    expert_down,
    mixer_gain,
    query_weight,
    key_weight,
    value_weight,
    output_gate,
    beta_weight,
    decay_weight,
    query_conv,
    key_conv,
    value_conv,
    decay_log,
    decay_bias,
    head_gain,
    out_weight,
):
    ctx_count = lax.axis_size("ctx")
    head_count = lax.axis_size("head")
    sources = ctx_count * head_count
    ctx_place = lax.axis_index("ctx")
    experts = (stream, moe_gain, router, expert_ids, expert_gate, expert_up, expert_down)
    cut = out_weight.shape[0] // 2
    out_halves = (out_weight[:cut], out_weight[cut:])
    if 2 * sources * stream.size <= GATHER_LIMIT and head_count == 4 and ctx_count in (6, 8):
        moe_out = expert_layer_gathered(*experts, sources, out_halves)
    else:
        moe_out = expert_layer_sent(*experts, sources)
    mixer_in = rms_rows(
        stream.astype(jnp.float32) + moe_out.astype(jnp.float32), mixer_gain
    ).astype(jnp.bfloat16)
    head_place = lax.axis_index("head")

    def crossed(value, step):
        pairs = [(source, source ^ step) for source in range(head_count)]
        return lax.ppermute(value, "head", pairs)


    def from_chip(value, *earlier):
        return [after(value, *earlier) if earlier else value, crossed(value, 1)]

    def from_others(value, *earlier):
        received = []
        for step in range(2, head_count, 2):
            part = crossed(value, step)
            received += [part, crossed(after(part, *earlier) if earlier else part, 1)]
        return received

    in_vmem = pl.BlockSpec(memory_space=pltpu.VMEM)
    in_smem = pl.BlockSpec(memory_space=pltpu.SMEM)
    tok_rows, width = stream.shape
    rows = tok_rows * head_count
    key_cols, value_cols = query_weight.shape[1], value_weight.shape[1]
    heads = beta_weight.shape[1]
    rim_len = 16
    halo = passed_along(mixer_in[tok_rows - rim_len :], "ctx", 1)
    halos = from_chip(halo) + from_others(halo)
    conv_cols = 2 * key_cols + value_cols
    matrices = (
        query_weight, key_weight, value_weight, output_gate, beta_weight, decay_weight
    )

    def project(pieces, halos):
        count = len(pieces) * tok_rows
        shapes = [
            jax.ShapeDtypeStruct((count, conv_cols), bf16),
            jax.ShapeDtypeStruct((count, value_cols), bf16),
            jax.ShapeDtypeStruct((count, heads), f32),
            jax.ShapeDtypeStruct((count, heads), f32),
        ]
        if halos:
            shapes.append(jax.ShapeDtypeStruct((rim_len, conv_cols), f32))
        return pl.pallas_call(
            functools.partial(project_kernel, blocks=len(pieces), halos=len(halos)),
            in_specs=[in_smem] + [in_vmem] * (len(pieces) + len(halos) + 6),
            out_shape=shapes,
            compiler_params=pltpu.CompilerParams(vmem_limit_bytes=28 << 20),
            cost_estimate=worth(4),
            name="project",
        )(head_place.reshape(1), *pieces, *halos, *matrices)

    near_raw = project(from_chip(mixer_in, halo), [])
    far_pieces = from_others(mixer_in, near_raw[0], halos[2])
    far_raw = project(far_pieces, halos)
    rim = far_raw[4]
    key_heads = key_cols // DK
    taps = jnp.concatenate([query_conv, key_conv, value_conv], axis=1)
    rates = jnp.stack([decay_log, decay_bias])
    chunk = math.gcd(rows, CHUNK)
    core, reading, moved = pl.pallas_call(
        functools.partial(delta_kernel, key_heads=key_heads, chunk=chunk, tok_rows=tok_rows),
        in_specs=[in_smem] + [in_vmem] * 9,
        out_shape=(
            jax.ShapeDtypeStruct((rows, value_cols), f32),
            jax.ShapeDtypeStruct((rows, value_cols), f32),
            jax.ShapeDtypeStruct((heads, DK, 2 * DK), bf16),
        ),
        scratch_shapes=[
            pltpu.VMEM((rows + rim_len, conv_cols), f32),
            pltpu.VMEM((rows, conv_cols), f32),
            pltpu.VMEM((rows, heads), f32),
            pltpu.VMEM((rows, heads), f32),
            pltpu.VMEM((heads, DK, 2 * DK), f32),
        ],
        compiler_params=pltpu.CompilerParams(vmem_limit_bytes=24 << 20),
        cost_estimate=worth(16),
        name="delta",
    )(
        head_place.reshape(1),
        *(array for kind in (0, 2, 3) for array in (near_raw[kind], far_raw[kind])),
        rim,
        taps,
        rates,
    )
    start_upper, start_lower = after(out_halves[0], far_pieces[-1]), after(out_halves[1], moved)
    upper = [crossed(start_upper, step) for step in range(2, head_count, 2)]
    lower = [crossed(start_lower, step) for step in range(2, head_count, 2)]

    in_pair = (ctx_place % 2).reshape(1)
    other = lax.ppermute(moved, "ctx", [(place, place ^ 1) for place in range(ctx_count)])
    other = after(other, *upper)
    window = pl.pallas_call(
        pair_kernel,
        in_specs=[in_smem, in_vmem, in_vmem],
        out_shape=jax.ShapeDtypeStruct(moved.shape, bf16),
        compiler_params=pltpu.CompilerParams(vmem_limit_bytes=8 << 20),
        name="pair",
    )(in_pair, moved, other)

    def composed(later, earlier, columns):
        product = jnp.einsum(
            "hij,hjk->hik",
            later[:, :, DK:],
            earlier[:, :, :columns],
            preferred_element_type=f32,
        )
        added = (product[:, :, :DK] + later[:, :, :DK].astype(f32)).astype(bf16)
        return jnp.concatenate([added, product[:, :, DK:].astype(bf16)], axis=2)

    reach, near_pairs, far_pairs = 1, None, jnp.zeros((heads, DK, DK), bf16)
    while reach < ctx_count // 2:
        last = 2 * reach >= ctx_count // 2
        if last and near_pairs is not None:
            far_pairs = passed_along(window[:, :, :DK], "ctx", 2 * reach)
        else:
            arrived = passed_along(window, "ctx", 2 * reach)
            if near_pairs is None:
                near_pairs = arrived
            else:
                near_pairs = composed(near_pairs, arrived, 2 * DK)
            window = composed(window, arrived, DK if 4 * reach >= ctx_count // 2 else 2 * DK)
        reach *= 2
    far_pairs = after(far_pairs, *lower)

    gated = pl.pallas_call(
        finish_kernel,
        grid_spec=pltpu.PrefetchScalarGridSpec(
            num_scalar_prefetch=1,
            grid=(head_count,),
            in_specs=[whole_ref(near_pairs), whole_ref(far_pairs), whole_ref(other)]
            + [
                pl.BlockSpec((tok_rows, value_cols), lambda step, where: (where[1] ^ step, 0)),
                pl.BlockSpec((tok_rows, value_cols), lambda step, where: (where[1] ^ step, 0)),
                pl.BlockSpec((tok_rows, value_cols), lambda step, where: (step % 2, 0)),
                pl.BlockSpec((tok_rows, value_cols), lambda step, where: (step % 2, 0)),
                pl.BlockSpec((1, DK), lambda step, where: (0, 0)),
            ],
            out_specs=pl.BlockSpec((tok_rows, value_cols), lambda step, where: (step, 0)),
        ),
        out_shape=jax.ShapeDtypeStruct((rows, value_cols), bf16),
        compiler_params=pltpu.CompilerParams(vmem_limit_bytes=12 << 20),
        name="finish",
    )(
        jnp.stack([ctx_place % 2, head_place]),
        near_pairs,
        far_pairs,
        other,
        core,
        reading,
        near_raw[1],
        far_raw[1],
        head_gain.reshape(1, -1),
    )
    gated_parts = []
    for step in range(head_count):
        part = gated[step * tok_rows : (step + 1) * tok_rows]
        gated_parts.append(crossed(part, step) if step else part)
    near_weights = [out_weight, crossed(after(out_weight, moved), 1)]
    far_weights = []
    for shard in zip(upper, lower):
        far_weights += shard
        far_weights += [crossed(after(part, far_pairs), 1) for part in shard]

    def multiplied(parts, weights, begun, kind):
        columns = pl.BlockSpec((tok_rows, width // 4), lambda n: (0, n))
        return pl.pallas_call(
            functools.partial(output_kernel, blocks=len(parts), begun=len(begun)),
            grid=(4,),
            in_specs=[whole_ref(part) for part in parts]
            + [pl.BlockSpec((part.shape[0], width // 4), lambda n: (0, n)) for part in weights]
            + [columns] * len(begun),
            out_specs=columns,
            out_shape=jax.ShapeDtypeStruct(stream.shape, kind),
            compiler_params=pltpu.CompilerParams(vmem_limit_bytes=20 << 20),
            cost_estimate=worth(3),
            name="output",
        )(*parts, *weights, *begun)

    begun = multiplied(gated_parts[:2], near_weights, [], f32)
    mixer_out = multiplied(gated_parts[2:], far_weights, [begun], bf16)
    return (moe_out, mixer_out)


def solution(mesh):
    return jax.shard_map(
        on_device,
        mesh=mesh,
        in_specs=(
            P(("ctx", "head"), None),
            P(),
            P(),
            P(("ctx", "head"), None),
            P(("ctx", "head"), None, None),
            P(("ctx", "head"), None, None),
            P(("ctx", "head"), None, None),
            P(),
            P(None, "head"),
            P(None, "head"),
            P(None, "head"),
            P(None, "head"),
            P(None, "head"),
            P(None, "head"),
            P(None, "head"),
            P(None, "head"),
            P(None, "head"),
            P("head"),
            P("head"),
            P(),
            P("head", None),
        ),
        out_specs=(P(("ctx", "head"), None), P(("ctx", "head"), None)),
        check_vma=False,
    )
```

```python
import functools
import math

import jax
import jax.numpy as jnp
from jax import lax
from jax.experimental import pallas as pl
from jax.experimental.pallas import tpu as pltpu
from jax.sharding import PartitionSpec as P

DK = 128
CHUNK = 128
GATHER_LIMIT = 32 << 20


epsilon = 1e-06
f32 = jnp.float32
bf16 = jnp.bfloat16


def passed_along(value, axis, steps):
    count = lax.axis_size(axis)
    first, last = (max(0, -steps), min(count, count - steps))
    return lax.ppermute(value, axis, [(source, source + steps) for source in range(first, last)])


def rms_rows(values, gain):
    values = values.astype(jnp.float32)
    scale = lax.rsqrt(jnp.mean(values * values, axis=-1, keepdims=True) + epsilon)
    return values * scale * gain


def after(value, *earlier):
    return lax.optimization_barrier((value, *earlier))[0]


def whole_ref(array):
    return pl.BlockSpec(array.shape, lambda *_: (0,) * array.ndim)


def worth(microseconds):
    return pl.CostEstimate(
        flops=int(microseconds * 1.15e9), bytes_accessed=int(microseconds * 1e6), transcendentals=0
    )


def contract(a, b, dims, precision=None):
    return lax.dot_general(
        a, b, (dims, ((), ())), precision=precision, preferred_element_type=f32
    )


def parts(values):
    high = values.astype(bf16)
    return high, (values - high.astype(f32)).astype(bf16)


def contract_close(a, b):
    a_high, a_low = parts(a)
    b_high, b_low = parts(b)
    doubled = jnp.concatenate([a_high, a_low], axis=1)
    if 2 * b.shape[1] <= 2 * DK:
        both = jnp.concatenate([b_high, b_low], axis=1)
        product = contract(doubled, jnp.concatenate([both, both], axis=0), ((1,), (0,)))
        return product[:, : b.shape[1]] + product[:, b.shape[1] :]
    return contract(
        doubled, jnp.concatenate([b_high, b_high], axis=0), ((1,), (0,))
    ) + contract(a_high, b_low, ((1,), (0,)))


def contract_rows(a, b):
    a_high, a_low = parts(a)
    b_high, b_low = parts(b)
    product = contract(
        jnp.concatenate([a_high, a_low], axis=1),
        jnp.concatenate(
            [jnp.concatenate([b_high, b_high], axis=1), jnp.concatenate([b_low, b_low], axis=1)],
            axis=0,
        ),
        ((1,), (1,)),
    )
    return product[:, : b.shape[0]] + product[:, b.shape[0] :]


def pair_routes(cols, picker, lines, tok_rows, slots):
    rows = cols.shape[0]
    weight_rows = contract(picker, cols, ((1,), (1,)))
    named = weight_rows > 0
    before = lax.broadcasted_iota(jnp.int32, (rows, rows), 0)
    after = lax.broadcasted_iota(jnp.int32, (rows, rows), 1)
    earlier = (before < after) & (before // tok_rows == after // tok_rows)
    rank = contract(
        jnp.where(named, 1.0, 0.0).astype(bf16),
        jnp.where(earlier, 1.0, 0.0).astype(bf16),
        ((1,), (0,)),
    )
    first_slot = lax.broadcasted_iota(jnp.int32, rank.shape, 1) // tok_rows * slots
    rank = jnp.where(named, rank.astype(jnp.int32) + first_slot, -1)
    slot = lax.broadcasted_iota(jnp.int32, (rows // tok_rows * slots, rows), 0)
    picks = [jnp.where(slot == rank[line : line + 1], 1.0, 0.0) for line in range(lines)]
    return weight_rows, picks


def collect_kernel(block_00, block_10, block_01, block_11, picker_ref, own_ref, send_ref, *, slots):
    local_experts, taken, width = own_ref.shape
    tok_rows = block_00.shape[0]
    pair = taken // 2
    for at, pair_refs in enumerate(((block_01, block_11), (block_00, block_10))):
        rows = jnp.concatenate([ref[...] for ref in pair_refs], axis=0)
        _, picks = pair_routes(
            rows[:, width:], picker_ref[...], 2 * local_experts, tok_rows, slots
        )
        picked = contract(
            jnp.concatenate(picks, axis=0).astype(bf16), rows[:, :width], ((1,), (0,))
        ).astype(bf16)
        for expert in range(local_experts):
            there = slice(at * pair, (at + 1) * pair)
            own_ref[expert, there, :] = picked[expert * pair : (expert + 1) * pair]
            line = local_experts + expert
            send_ref[expert, there, :] = picked[line * pair : (line + 1) * pair]


def expert_kernel(*refs):
    *row_refs, gate_ref, up_ref, down_ref, own_ref, send_ref = refs
    half = len(row_refs) // 2
    for sources, out_ref in ((row_refs[half:], send_ref), (row_refs[:half], own_ref)):
        rows = jnp.concatenate([ref[0] for ref in sources], axis=0)
        gate = contract(rows, gate_ref[0], ((1,), (0,)))
        up = contract(rows, up_ref[0], ((1,), (0,)))
        hidden = (gate / (1.0 + jnp.exp(-gate)) * up).astype(bf16)
        out_ref[0] = contract(hidden, down_ref[0], ((1,), (0,))).astype(bf16)


def spread_kernel(*refs, slots, places):
    *cols_refs, picker_ref, own_ref, got_ref, far_ref, near_ref, here_ref = refs
    local_experts = own_ref.shape[0]
    tok_rows = cols_refs[0].shape[0]
    pair = 2 * slots
    for group, place in enumerate(places):
        cols_00, cols_10, cols_01, cols_11 = cols_refs[4 * group : 4 * group + 4]
        for at, pair_refs in enumerate(((cols_01, cols_11), (cols_00, cols_10))):
            cols = jnp.concatenate([ref[...] for ref in pair_refs], axis=0)
            weight_rows, picks = pair_routes(
                cols, picker_ref[...], 2 * local_experts, tok_rows, slots
            )
            first = (2 * place + at) * pair
            scaled = []
            for line, pick in enumerate(picks):
                result_ref = (own_ref, got_ref)[line // local_experts]
                result = result_ref[line % local_experts, first : first + pair, :]
                weight = jnp.sum(pick * weight_rows[line : line + 1], axis=1, keepdims=True)
                scaled.append((result.astype(f32) * weight).astype(bf16))
            summed = contract(
                jnp.concatenate(picks, axis=0).astype(bf16),
                jnp.concatenate(scaled, axis=0),
                ((0,), (0,)),
            ).astype(bf16)
            if at == 0:
                far_ref[group, 0] = summed[:tok_rows]
                far_ref[group, 1] = summed[tok_rows:]
            else:
                here_ref[group] = summed[:tok_rows]
                near_ref[group] = summed[tok_rows:]


def expert_layer_gathered(
    stream,
    moe_gain,
    router,
    expert_ids,
    expert_gate,
    expert_up,
    expert_down,
    sources,
    early,
):
    tok_rows, width = stream.shape
    local_experts, _, hidden_width = expert_gate.shape
    experts_all = local_experts * sources
    depth = sources // 8
    place = lax.axis_index(("ctx", "head"))

    def sent(value, move):
        pairs = []
        for device in range(sources):
            z, y, x, core = device // 8, device // 4 % 2, device // 2 % 2, device % 2
            z, y, x, core = move(z, y, x, core)
            pairs.append((device, ((z * 2 + y) * 2 + x) * 2 + core))
        return lax.ppermute(value, ("ctx", "head"), pairs)

    def lifted(value, steps):
        return sent(value, lambda z, y, x, core: ((z + steps) % depth, y, x, core))

    def first(value):
        return sent(value, lambda z, y, x, core: (z, y ^ (1 - core), x ^ core, core))

    def second(value):
        return sent(value, lambda z, y, x, core: (z, y ^ core, x ^ (1 - core), core))

    def swapped(value):
        return sent(value, lambda z, y, x, core: (z, y, x, 1 - core))

    normed = rms_rows(stream, moe_gain).astype(bf16)
    logits = jnp.dot(normed, router, preferred_element_type=f32)
    named = jnp.any(
        expert_ids[:, :, None] == jnp.arange(experts_all, dtype=jnp.int32)[None, None, :], axis=1
    )
    raised = jnp.where(named, jnp.exp(logits), 0.0)
    weights = raised / jnp.sum(raised, axis=1, keepdims=True)
    coarse = lax.reduce_precision(weights, 8, 7)
    packet = jnp.concatenate(
        [normed, coarse.astype(bf16), (weights - coarse).astype(bf16)], axis=1
    )

    capacity = (11 * tok_rows * expert_ids.shape[1] + 10 * experts_all - 1) // (10 * experts_all)
    slots = -(-capacity // 8) * 8
    taken = 4 * slots
    column = jnp.arange(2 * experts_all, dtype=jnp.int32)[None, :] % experts_all
    line = jnp.arange(16, dtype=jnp.int32)[:, None]
    owner = jnp.where(line < local_experts, place, place ^ 1)
    picker = (
        (line < 2 * local_experts) & (column == owner * local_experts + line % local_experts)
    ).astype(bf16)

    order = [0, *range(depth - 1, 0, -1)]
    own_rows, got_rows, outcome = {}, {}, {}
    blocks = {}
    mine = packet
    for at, steps in enumerate(order):
        if steps:
            source = packet if steps == 1 else mine
            earlier = [blocks[order[at - 1]][0]] if at > 1 else []
            if at > 1:
                earlier += blocks[order[at - 2]][1:3]
            if earlier:
                source = after(source, *earlier)
            mine = lifted(source, 1 if steps == 1 else -1)
        onward = mine
        if at:
            onward = after(mine, *blocks[order[at - 1]][1:3])
        near = first(onward)
        blocks[steps] = (mine, near, second(onward), second(near))

    picked_spec = pl.BlockSpec((local_experts, taken, width), lambda g: (0, 0, 0))

    def collect(steps, *earlier):
        rows = blocks[steps][0]
        own, send = pl.pallas_call(
            functools.partial(collect_kernel, slots=slots),
            grid=(1,),
            in_specs=[whole_ref(packet)] * 4 + [whole_ref(picker)],
            out_specs=[picked_spec] * 2,
            out_shape=[jax.ShapeDtypeStruct((local_experts, taken, width), bf16)] * 2,
            compiler_params=pltpu.CompilerParams(vmem_limit_bytes=24 << 20),
            cost_estimate=worth(2),
            name="collect",
        )(after(rows, *earlier) if earlier else rows, *blocks[steps][1:], picker)
        own_rows[steps] = own
        got_rows[steps] = swapped(send)

    def run_experts(members, *earlier):
        row_spec = pl.BlockSpec((1, taken, width), lambda e: (e, 0, 0))
        out_spec = pl.BlockSpec((1, len(members) * taken, width), lambda e: (e, 0, 0))
        results, send_back = pl.pallas_call(
            expert_kernel,
            grid=(local_experts,),
            in_specs=[row_spec] * (2 * len(members))
            + [
                pl.BlockSpec((1, width, hidden_width), lambda e: (e, 0, 0)),
                pl.BlockSpec((1, width, hidden_width), lambda e: (e, 0, 0)),
                pl.BlockSpec((1, hidden_width, width), lambda e: (e, 0, 0)),
            ],
            out_specs=[out_spec] * 2,
            out_shape=[jax.ShapeDtypeStruct((local_experts, len(members) * taken, width), bf16)]
            * 2,
            compiler_params=pltpu.CompilerParams(vmem_limit_bytes=40 << 20),
            cost_estimate=worth(4 + 3 * len(members) if len(members) > 1 else 1),
            name="experts",
        )(
            after(own_rows[members[0]], *earlier),
            *[own_rows[member] for member in members[1:]],
            *[got_rows[member] for member in members],
            expert_gate,
            expert_up,
            expert_down,
        )
        got_back = swapped(send_back)
        for at, member in enumerate(members):
            outcome[member] = (at, results, got_back)

    def spread(members):
        places = [outcome[member][0] for member in members]
        _, results, got_back = outcome[members[0]]
        cols_spec = pl.BlockSpec(
            (tok_rows, 2 * experts_all), lambda g: (0, width // (2 * experts_all))
        )
        row_shape = jax.ShapeDtypeStruct((len(members), tok_rows, width), bf16)
        far_shape = jax.ShapeDtypeStruct((len(members), 2, tok_rows, width), bf16)
        return pl.pallas_call(
            functools.partial(spread_kernel, slots=slots, places=places),
            grid=(1,),
            in_specs=[cols_spec] * (4 * len(members))
            + [whole_ref(picker), whole_ref(results), whole_ref(results)],
            out_specs=[whole_ref(far_shape), whole_ref(row_shape), whole_ref(row_shape)],
            out_shape=[far_shape, row_shape, row_shape],
            compiler_params=pltpu.CompilerParams(vmem_limit_bytes=28 << 20),
            cost_estimate=worth(1),
            name="spread",
        )(*(block for member in members for block in blocks[member]), picker, results, got_back)

    last, batch = order[-1], order[-2:0:-1]
    for steps in order[:-2]:
        collect(steps, blocks[order[-2]][0])
    collect(order[-2], *blocks[last][:3])
    run_experts(order[:-1])
    ready = {steps: spread([steps]) for steps in batch}
    collect(last, *[far for far, _, _ in ready.values()])
    run_experts([last])
    ready[last], ready[0] = spread([last]), spread([0])

    def joined(steps, direct, diagonal):
        _, near, here = ready[steps]
        near = first((near[0].astype(f32) + diagonal.astype(f32)).astype(bf16))
        return here[0].astype(f32) + direct.astype(f32) + near.astype(f32)

    moving = []
    for at, steps in enumerate(batch):
        across = second(ready[steps][0])
        total = joined(steps, across[0, 0], across[0, 1])
        if moving:
            total += moving[-1].astype(f32)
        moving.append(lifted(total.astype(bf16), 1))
    across = after(second(ready[last][0]), moving[0])
    total = joined(last, across[0, 0], across[0, 1])
    rising = lifted(total.astype(bf16), -1)
    far = after(ready[0][0], across)
    diagonal = after(second(far[0, 1]), moving[-1])
    total = joined(0, second(far[0, 0]), diagonal)
    total += moving[-1].astype(f32) + rising.astype(f32)
    return after(total, *early).astype(bf16)


def expert_layer_sent(
    stream, moe_gain, router, expert_ids, expert_gate, expert_up, expert_down, sources
):
    tok_rows, model_width = stream.shape
    top_count = expert_ids.shape[1]
    local_experts = expert_gate.shape[0]
    experts_all = local_experts * sources
    capacity = (11 * tok_rows * top_count + 10 * experts_all - 1) // (10 * experts_all)
    normed = rms_rows(stream, moe_gain).astype(jnp.bfloat16)
    logits = jnp.dot(normed, router, preferred_element_type=jnp.float32)
    chosen = jnp.take_along_axis(logits, expert_ids, axis=1)
    raised = jnp.exp(chosen)
    weights = raised / jnp.sum(raised, axis=1, keepdims=True)
    flat_ids = expert_ids.reshape(-1)
    matches = (flat_ids[:, None] == jnp.arange(experts_all, dtype=jnp.int32)[None, :]).astype(
        jnp.int32
    )
    slot_index = jnp.sum((jnp.cumsum(matches, axis=0) - 1) * matches, axis=1)
    places = flat_ids * capacity + slot_index
    token_rows = jnp.arange(tok_rows * top_count, dtype=jnp.int32) // top_count
    outgoing = (
        jnp.zeros((experts_all * capacity, model_width), jnp.bfloat16)
        .at[places]
        .set(normed[token_rows])
    )
    outgoing = outgoing.reshape(sources, local_experts, capacity, model_width)
    received = lax.all_to_all(outgoing, ("ctx", "head"), split_axis=0, concat_axis=0, tiled=True)
    gate_part = jnp.einsum(
        "nesd,edh->nesh", received, expert_gate, preferred_element_type=jnp.float32
    )
    up_part = jnp.einsum("nesd,edh->nesh", received, expert_up, preferred_element_type=jnp.float32)
    hidden = (jax.nn.silu(gate_part) * up_part).astype(jnp.bfloat16)
    returned = lax.all_to_all(
        jnp.einsum(
            "nesh,ehd->nesd", hidden, expert_down, preferred_element_type=jnp.float32
        ).astype(jnp.bfloat16),
        ("ctx", "head"),
        split_axis=0,
        concat_axis=0,
        tiled=True,
    )
    gathered_rows = returned.reshape(experts_all * capacity, model_width)[places].reshape(
        tok_rows, top_count, model_width
    )
    return jnp.sum(weights[:, :, None] * gathered_rows.astype(jnp.float32), axis=1).astype(
        jnp.bfloat16
    )


def unit_inverses(strict_parts):
    size = strict_parts[0].shape[0]
    row = lax.broadcasted_iota(jnp.int32, (size, size), 0)
    col = lax.broadcasted_iota(jnp.int32, (size, size), 1)
    unit = jnp.where(row == col, 1.0, 0.0)
    joining = (row // 2 == col // 2) & (row != col)
    inverses = [unit - jnp.where(joining, part, 0.0) for part in strict_parts]
    half = 2
    while half < size:
        joining = (row // (2 * half) == col // (2 * half)) & (row // half != col // half)
        corners = [jnp.where(joining, part, 0.0) for part in strict_parts]
        if half < 8:
            steps = [contract_close(c, inverse) for c, inverse in zip(corners, inverses)]
            moves = [contract_close(inverse, step) for inverse, step in zip(inverses, steps)]
            inverses = [inverse - move for inverse, move in zip(inverses, moves)]
        else:
            starts = range(0, size, 2 * half)

            def lower_rows(array):
                return jnp.concatenate([array[at + half : at + 2 * half] for at in starts], axis=0)

            zeros = jnp.zeros((half, size), f32)
            steps = [
                contract_close(lower_rows(c), inverse) for c, inverse in zip(corners, inverses)
            ]
            steps = [
                jnp.concatenate(
                    [
                        piece
                        for at in range(0, size // 2, half)
                        for piece in (zeros, step[at : at + half])
                    ],
                    axis=0,
                )
                for step in steps
            ]
            lowers = [lower_rows(inverse) for inverse in inverses]
            lowers = [lower - contract_close(lower, step) for lower, step in zip(lowers, steps)]
            inverses = [
                jnp.concatenate(
                    [
                        piece
                        for at in starts
                        for piece in (
                            inverse[at : at + half],
                            lower[at // 2 : at // 2 + half],
                        )
                    ],
                    axis=0,
                )
                for inverse, lower in zip(inverses, lowers)
            ]
        half *= 2
    return inverses


def unit_rows(rows):
    return rows * lax.rsqrt(jnp.sum(rows * rows, axis=-1, keepdims=True) + epsilon)


def delta_kernel(
    place_ref,
    near_raw,
    far_raw,
    near_beta,
    far_beta,
    near_decay,
    far_decay,
    rim_ref,
    taps_ref,
    rate_ref,
    core_ref,
    reading_ref,
    moved_ref,
    extended,
    mixed,
    strengths,
    falls,
    carried,
    *,
    key_heads,
    chunk,
    tok_rows,
):
    rows, conv_cols = near_raw.shape[0] + far_raw.shape[0], near_raw.shape[1]
    heads = moved_ref.shape[0]
    group = heads // key_heads
    tap_count = taps_ref.shape[0]
    rim = rim_ref.shape[0]
    extended[0:rim, :] = rim_ref[...]
    step = 0
    for part_refs in ((near_raw, near_beta, near_decay), (far_raw, far_beta, far_decay)):
        for first in range(0, part_refs[0].shape[0], tok_rows):
            at = pl.multiple_of((place_ref[0] ^ step) * tok_rows, tok_rows)
            part = slice(first, first + tok_rows)
            extended[pl.ds(rim + at, tok_rows), :] = part_refs[0][part, :].astype(f32)
            strengths[pl.ds(at, tok_rows), :] = 1.0 / (1.0 + jnp.exp(-part_refs[1][part, :]))
            shifted = part_refs[2][part, :] + rate_ref[1:2, :]
            softened = jnp.maximum(shifted, 0.0) + jnp.log1p(jnp.exp(-jnp.abs(shifted)))
            falls[pl.ds(at, tok_rows), :] = -jnp.exp(rate_ref[0:1, :]) * softened
            step += 1
    key_at, value_at = key_heads * DK, 2 * key_heads * DK
    for start in range(0, rows, chunk):
        for first in range(0, conv_cols, DK):
            columns = slice(first, first + DK)
            summed = jnp.zeros((chunk, DK), f32)
            for tap in range(tap_count):
                offset = rim - (tap_count - 1) + start + tap
                summed += taps_ref[tap : tap + 1, columns] * extended[
                    offset : offset + chunk, columns
                ]
            value = summed / (1.0 + jnp.exp(-summed))
            if first < key_at:
                value = unit_rows(value) * DK**-0.5
            elif first < value_at:
                value = unit_rows(value)
            mixed[start : start + chunk, columns] = value
    row = lax.broadcasted_iota(jnp.int32, (chunk, chunk), 0)
    col = lax.broadcasted_iota(jnp.int32, (chunk, chunk), 1)
    inclusive, strict = row >= col, row > col
    lower = jnp.where(inclusive, 1.0, 0.0)
    across = lax.broadcasted_iota(jnp.int32, (DK, 2 * DK), 1)
    down = lax.broadcasted_iota(jnp.int32, (DK, 2 * DK), 0)
    carried[...] = jnp.broadcast_to(
        jnp.where(across == down + DK, 1.0, 0.0)[None], carried.shape
    )

    def advance(step, nothing):
        here = pl.ds(pl.multiple_of(step * chunk, chunk), chunk)
        fall = falls[here, :]
        strength = strengths[here, :]
        cumulative = contract(lower, fall, ((1,), (0,)), lax.Precision.HIGHEST)
        cumulative_rows = contract(fall, lower, ((0,), (1,)), lax.Precision.HIGHEST)
        owners = range(heads)
        queries = [mixed[here, k * DK : (k + 1) * DK] for k in range(key_heads)]
        keys = [mixed[here, key_at + k * DK : key_at + (k + 1) * DK] for k in range(key_heads)]
        dots = [
            contract_rows(jnp.concatenate([key, query], axis=0), key)
            for key, query in zip(keys, queries)
        ]
        totals = [cumulative[:, head : head + 1] for head in owners]
        kept = [
            jnp.where(
                inclusive,
                jnp.exp(jnp.where(inclusive, totals[head] - cumulative_rows[head : head + 1, :], 0.0)),
                0.0,
            )
            for head in owners
        ]
        own = [strength[:, head : head + 1] for head in owners]
        solvers = unit_inverses(
            [
                own[head] * jnp.where(strict, kept[head], 0.0) * dots[head // group][:chunk]
                for head in owners
            ]
        )
        risen = [jnp.exp(total) for total in totals]
        solved = [
            contract_close(
                solvers[head],
                own[head]
                * jnp.concatenate(
                    [
                        mixed[here, value_at + head * DK : value_at + (head + 1) * DK],
                        risen[head] * keys[head // group],
                    ],
                    axis=1,
                ),
            )
            for head in owners
        ]
        states = [carried[head] for head in owners]
        read = [
            contract_close(
                jnp.concatenate(
                    [solved[head][:, DK:], risen[head] * queries[head // group]], axis=0
                ),
                states[head],
            )
            for head in owners
        ]
        updates = [
            jnp.concatenate([solved[head][:, :DK], jnp.zeros((chunk, DK), f32)], axis=1)
            - read[head][:chunk]
            for head in owners
        ]
        for head in owners:
            last = totals[head][chunk - 1 :, :]
            leaving = jnp.exp(last - totals[head]) * keys[head // group]
            carried[head] = jnp.exp(last) * states[head] + contract_close(
                leaving.T, updates[head]
            )
        for head in owners:
            result = read[head][chunk:] + contract_close(
                kept[head] * dots[head // group][chunk:], updates[head]
            )
            core_ref[here, head * DK : (head + 1) * DK] = result[:, :DK]
            reading_ref[here, head * DK : (head + 1) * DK] = result[:, DK:]
        return nothing

    lax.fori_loop(0, rows // chunk, advance, 0)
    moved_ref[...] = carried[...].astype(bf16)


def project_kernel(place_ref, *refs, blocks, halos):
    row_refs, halo_refs = refs[:blocks], refs[blocks : blocks + halos]
    weight_refs, out_refs = refs[blocks + halos : blocks + halos + 6], refs[blocks + halos + 6 :]
    pieces = [ref[...] for ref in row_refs]
    rows = blocks * row_refs[0].shape[0]
    if halos:
        pieces.append(
            sum(
                jnp.where((place_ref[0] ^ step) == halos - 1, 1.0, 0.0) * ref[...].astype(f32)
                for step, ref in enumerate(halo_refs)
            ).astype(bf16)
        )
    pieces = jnp.concatenate(pieces, axis=0)
    qkv_ref, gate_ref, beta_ref, decay_ref = out_refs[:4]
    first = 0
    for weight_ref in weight_refs[:3]:
        product = contract(pieces, weight_ref[...], ((1,), (0,))).astype(bf16)
        last = first + weight_ref.shape[1]
        qkv_ref[:, first:last] = product[:rows]
        if halos:
            out_refs[4][:, first:last] = product[rows:].astype(f32)
        first = last
    pieces = pieces[:rows]
    gate_ref[...] = contract(pieces, weight_refs[3][...], ((1,), (0,))).astype(bf16)
    beta_ref[...] = contract(pieces, weight_refs[4][...], ((1,), (0,)))
    decay_ref[...] = contract(pieces, weight_refs[5][...], ((1,), (0,)))


def pair_kernel(second_ref, mine_ref, other_ref, joined_ref):
    late = second_ref[0] == 1
    for head in range(mine_ref.shape[0]):
        mine, other = mine_ref[head].astype(f32), other_ref[head].astype(f32)
        earlier = jnp.where(late, other, mine).astype(bf16)
        later = jnp.where(late, mine, other)
        joined = contract(later[:, DK:].astype(bf16), earlier, ((1,), (0,)))
        joined_ref[head, :, :DK] = (joined[:, :DK] + later[:, :DK]).astype(bf16)
        joined_ref[head, :, DK:] = joined[:, DK:].astype(bf16)


def finish_kernel(
    where_ref,
    near_pairs_ref,
    far_pairs_ref,
    other_ref,
    core_ref,
    reading_ref,
    near_gate,
    far_gate,
    gain_ref,
    gated_ref,
):
    states = []
    for head in range(other_ref.shape[0]):
        state = contract(near_pairs_ref[head, :, DK:], far_pairs_ref[head], ((1,), (0,)))
        state += near_pairs_ref[head, :, :DK].astype(f32)
        passed = contract(other_ref[head, :, DK:], state.astype(bf16), ((1,), (0,)))
        passed += other_ref[head, :, :DK].astype(f32)
        states.append(jnp.where(where_ref[0] == 1, passed, state))
    gates = jnp.where(pl.program_id(0) < 2, near_gate[...].astype(f32), far_gate[...].astype(f32))
    for head, state in enumerate(states):
        columns = slice(head * DK, (head + 1) * DK)
        core = core_ref[:, columns] + contract_close(reading_ref[:, columns], state)
        normal = (
            core
            * lax.rsqrt(jnp.mean(core * core, axis=-1, keepdims=True) + epsilon)
            * gain_ref[...]
        )
        gate = gates[:, columns]
        gated_ref[:, columns] = (normal * (gate / (1.0 + jnp.exp(-gate)))).astype(bf16)


def output_kernel(*refs, blocks, begun):
    row_refs, weight_refs, out_ref = refs[:blocks], refs[blocks : -1 - begun], refs[-1]
    total = refs[-2][...] if begun else 0.0
    pieces = iter(weight_refs)
    for rows_ref in row_refs:
        at = 0
        while at < rows_ref.shape[1]:
            weight_ref = next(pieces)
            depth = weight_ref.shape[0]
            total += contract(rows_ref[:, at : at + depth], weight_ref[...], ((1,), (0,)))
            at += depth
    out_ref[...] = total.astype(out_ref.dtype)


def on_device(
    stream,
    moe_gain,
    router,
    expert_ids,
    expert_gate,
    expert_up,
    expert_down,
    mixer_gain,
    query_weight,
    key_weight,
    value_weight,
    output_gate,
    beta_weight,
    decay_weight,
    query_conv,
    key_conv,
    value_conv,
    decay_log,
    decay_bias,
    head_gain,
    out_weight,
):
    ctx_count = lax.axis_size("ctx")
    head_count = lax.axis_size("head")
    sources = ctx_count * head_count
    ctx_place = lax.axis_index("ctx")
    experts = (stream, moe_gain, router, expert_ids, expert_gate, expert_up, expert_down)
    cut = out_weight.shape[0] // 2
    out_halves = (out_weight[:cut], out_weight[cut:])
    if 2 * sources * stream.size <= GATHER_LIMIT and head_count == 4 and ctx_count in (6, 8):
        moe_out = expert_layer_gathered(*experts, sources, out_halves)
    else:
        moe_out = expert_layer_sent(*experts, sources)
    mixer_in = rms_rows(
        stream.astype(jnp.float32) + moe_out.astype(jnp.float32), mixer_gain
    ).astype(jnp.bfloat16)
    head_place = lax.axis_index("head")

    def crossed(value, step):
        pairs = [(source, source ^ step) for source in range(head_count)]
        return lax.ppermute(value, "head", pairs)


    def from_chip(value, *earlier):
        return [after(value, *earlier) if earlier else value, crossed(value, 1)]

    def from_others(value, *earlier):
        received = []
        for step in range(2, head_count, 2):
            part = crossed(value, step)
            received += [part, crossed(after(part, *earlier) if earlier else part, 1)]
        return received

    in_vmem = pl.BlockSpec(memory_space=pltpu.VMEM)
    in_smem = pl.BlockSpec(memory_space=pltpu.SMEM)
    tok_rows, width = stream.shape
    rows = tok_rows * head_count
    key_cols, value_cols = query_weight.shape[1], value_weight.shape[1]
    heads = beta_weight.shape[1]
    rim_len = 16
    halo = passed_along(mixer_in[tok_rows - rim_len :], "ctx", 1)
    halos = from_chip(halo) + from_others(halo)
    conv_cols = 2 * key_cols + value_cols
    matrices = (
        query_weight, key_weight, value_weight, output_gate, beta_weight, decay_weight
    )

    def project(pieces, halos):
        count = len(pieces) * tok_rows
        shapes = [
            jax.ShapeDtypeStruct((count, conv_cols), bf16),
            jax.ShapeDtypeStruct((count, value_cols), bf16),
            jax.ShapeDtypeStruct((count, heads), f32),
            jax.ShapeDtypeStruct((count, heads), f32),
        ]
        if halos:
            shapes.append(jax.ShapeDtypeStruct((rim_len, conv_cols), f32))
        return pl.pallas_call(
            functools.partial(project_kernel, blocks=len(pieces), halos=len(halos)),
            in_specs=[in_smem] + [in_vmem] * (len(pieces) + len(halos) + 6),
            out_shape=shapes,
            compiler_params=pltpu.CompilerParams(vmem_limit_bytes=28 << 20),
            cost_estimate=worth(4),
            name="project",
        )(head_place.reshape(1), *pieces, *halos, *matrices)

    near_raw = project(from_chip(mixer_in, halo), [])
    far_pieces = from_others(mixer_in, halos[2])
    far_raw = project(far_pieces, halos)
    rim = far_raw[4]
    key_heads = key_cols // DK
    taps = jnp.concatenate([query_conv, key_conv, value_conv], axis=1)
    rates = jnp.stack([decay_log, decay_bias])
    chunk = math.gcd(rows, CHUNK)
    core, reading, moved = pl.pallas_call(
        functools.partial(delta_kernel, key_heads=key_heads, chunk=chunk, tok_rows=tok_rows),
        in_specs=[in_smem] + [in_vmem] * 9,
        out_shape=(
            jax.ShapeDtypeStruct((rows, value_cols), f32),
            jax.ShapeDtypeStruct((rows, value_cols), f32),
            jax.ShapeDtypeStruct((heads, DK, 2 * DK), bf16),
        ),
        scratch_shapes=[
            pltpu.VMEM((rows + rim_len, conv_cols), f32),
            pltpu.VMEM((rows, conv_cols), f32),
            pltpu.VMEM((rows, heads), f32),
            pltpu.VMEM((rows, heads), f32),
            pltpu.VMEM((heads, DK, 2 * DK), f32),
        ],
        compiler_params=pltpu.CompilerParams(vmem_limit_bytes=24 << 20),
        cost_estimate=worth(16),
        name="delta",
    )(
        head_place.reshape(1),
        *(array for kind in (0, 2, 3) for array in (near_raw[kind], far_raw[kind])),
        rim,
        taps,
        rates,
    )
    start_upper, start_lower = after(out_halves[0], far_pieces[-1]), after(out_halves[1], moved)
    upper = [crossed(start_upper, step) for step in range(2, head_count, 2)]
    lower = [crossed(start_lower, step) for step in range(2, head_count, 2)]

    in_pair = (ctx_place % 2).reshape(1)
    other = lax.ppermute(moved, "ctx", [(place, place ^ 1) for place in range(ctx_count)])
    other = after(other, *upper)
    window = pl.pallas_call(
        pair_kernel,
        in_specs=[in_smem, in_vmem, in_vmem],
        out_shape=jax.ShapeDtypeStruct(moved.shape, bf16),
        compiler_params=pltpu.CompilerParams(vmem_limit_bytes=8 << 20),
        name="pair",
    )(in_pair, moved, other)

    def composed(later, earlier, columns):
        product = jnp.einsum(
            "hij,hjk->hik",
            later[:, :, DK:],
            earlier[:, :, :columns],
            preferred_element_type=f32,
        )
        added = (product[:, :, :DK] + later[:, :, :DK].astype(f32)).astype(bf16)
        return jnp.concatenate([added, product[:, :, DK:].astype(bf16)], axis=2)

    reach, near_pairs, far_pairs = 1, None, jnp.zeros((heads, DK, DK), bf16)
    while reach < ctx_count // 2:
        last = 2 * reach >= ctx_count // 2
        if last and near_pairs is not None:
            far_pairs = passed_along(window[:, :, :DK], "ctx", 2 * reach)
        else:
            arrived = passed_along(window, "ctx", 2 * reach)
            if near_pairs is None:
                near_pairs = arrived
            else:
                near_pairs = composed(near_pairs, arrived, 2 * DK)
            window = composed(window, arrived, DK if 4 * reach >= ctx_count // 2 else 2 * DK)
        reach *= 2
    far_pairs = after(far_pairs, *lower)

    gated = pl.pallas_call(
        finish_kernel,
        grid_spec=pltpu.PrefetchScalarGridSpec(
            num_scalar_prefetch=1,
            grid=(head_count,),
            in_specs=[whole_ref(near_pairs), whole_ref(far_pairs), whole_ref(other)]
            + [
                pl.BlockSpec((tok_rows, value_cols), lambda step, where: (where[1] ^ step, 0)),
                pl.BlockSpec((tok_rows, value_cols), lambda step, where: (where[1] ^ step, 0)),
                pl.BlockSpec((tok_rows, value_cols), lambda step, where: (step % 2, 0)),
                pl.BlockSpec((tok_rows, value_cols), lambda step, where: (step % 2, 0)),
                pl.BlockSpec((1, DK), lambda step, where: (0, 0)),
            ],
            out_specs=pl.BlockSpec((tok_rows, value_cols), lambda step, where: (step, 0)),
        ),
        out_shape=jax.ShapeDtypeStruct((rows, value_cols), bf16),
        compiler_params=pltpu.CompilerParams(vmem_limit_bytes=12 << 20),
        name="finish",
    )(
        jnp.stack([ctx_place % 2, head_place]),
        near_pairs,
        far_pairs,
        other,
        core,
        reading,
        near_raw[1],
        far_raw[1],
        head_gain.reshape(1, -1),
    )
    gated_parts = []
    for step in range(head_count):
        part = gated[step * tok_rows : (step + 1) * tok_rows]
        gated_parts.append(crossed(part, step) if step else part)
    near_weights = [out_weight, crossed(after(out_weight, moved), 1)]
    far_weights = []
    for shard in zip(upper, lower):
        far_weights += shard
        far_weights += [crossed(after(part, far_pairs), 1) for part in shard]

    def multiplied(parts, weights, begun, kind):
        columns = pl.BlockSpec((tok_rows, width // 4), lambda n: (0, n))
        return pl.pallas_call(
            functools.partial(output_kernel, blocks=len(parts), begun=len(begun)),
            grid=(4,),
            in_specs=[whole_ref(part) for part in parts]
            + [pl.BlockSpec((part.shape[0], width // 4), lambda n: (0, n)) for part in weights]
            + [columns] * len(begun),
            out_specs=columns,
            out_shape=jax.ShapeDtypeStruct(stream.shape, kind),
            compiler_params=pltpu.CompilerParams(vmem_limit_bytes=20 << 20),
            cost_estimate=worth(3),
            name="output",
        )(*parts, *weights, *begun)

    begun = multiplied(gated_parts[:2], near_weights, [], f32)
    mixer_out = multiplied(gated_parts[2:], far_weights, [begun], bf16)
    return (moe_out, mixer_out)


def solution(mesh):
    return jax.shard_map(
        on_device,
        mesh=mesh,
        in_specs=(
            P(("ctx", "head"), None),
            P(),
            P(),
            P(("ctx", "head"), None),
            P(("ctx", "head"), None, None),
            P(("ctx", "head"), None, None),
            P(("ctx", "head"), None, None),
            P(),
            P(None, "head"),
            P(None, "head"),
            P(None, "head"),
            P(None, "head"),
            P(None, "head"),
            P(None, "head"),
            P(None, "head"),
            P(None, "head"),
            P(None, "head"),
            P("head"),
            P("head"),
            P(),
            P("head", None),
        ),
        out_specs=(P(("ctx", "head"), None), P(("ctx", "head"), None)),
        check_vma=False,
    )
```

```python
import functools
import math

import jax
import jax.numpy as jnp
from jax import lax
from jax.experimental import pallas as pl
from jax.experimental.pallas import tpu as pltpu
from jax.sharding import PartitionSpec as P

DK = 128
CHUNK = 128
GATHER_LIMIT = 32 << 20


epsilon = 1e-06
f32 = jnp.float32
bf16 = jnp.bfloat16


def passed_along(value, axis, steps):
    count = lax.axis_size(axis)
    first, last = (max(0, -steps), min(count, count - steps))
    return lax.ppermute(value, axis, [(source, source + steps) for source in range(first, last)])


def rms_rows(values, gain):
    values = values.astype(jnp.float32)
    scale = lax.rsqrt(jnp.mean(values * values, axis=-1, keepdims=True) + epsilon)
    return values * scale * gain


def after(value, *earlier):
    return lax.optimization_barrier((value, *earlier))[0]


def whole_ref(array):
    return pl.BlockSpec(array.shape, lambda *_: (0,) * array.ndim)


def worth(microseconds):
    return pl.CostEstimate(
        flops=int(microseconds * 1.15e9), bytes_accessed=int(microseconds * 1e6), transcendentals=0
    )


def contract(a, b, dims, precision=None):
    return lax.dot_general(
        a, b, (dims, ((), ())), precision=precision, preferred_element_type=f32
    )


def parts(values):
    high = values.astype(bf16)
    return high, (values - high.astype(f32)).astype(bf16)


def contract_close(a, b):
    a_high, a_low = parts(a)
    b_high, b_low = parts(b)
    doubled = jnp.concatenate([a_high, a_low], axis=1)
    if 2 * b.shape[1] <= 2 * DK:
        both = jnp.concatenate([b_high, b_low], axis=1)
        product = contract(doubled, jnp.concatenate([both, both], axis=0), ((1,), (0,)))
        return product[:, : b.shape[1]] + product[:, b.shape[1] :]
    return contract(
        doubled, jnp.concatenate([b_high, b_high], axis=0), ((1,), (0,))
    ) + contract(a_high, b_low, ((1,), (0,)))


def contract_rows(a, b):
    a_high, a_low = parts(a)
    b_high, b_low = parts(b)
    product = contract(
        jnp.concatenate([a_high, a_low], axis=1),
        jnp.concatenate(
            [jnp.concatenate([b_high, b_high], axis=1), jnp.concatenate([b_low, b_low], axis=1)],
            axis=0,
        ),
        ((1,), (1,)),
    )
    return product[:, : b.shape[0]] + product[:, b.shape[0] :]


def pair_routes(cols, picker, lines, tok_rows, slots):
    rows = cols.shape[0]
    weight_rows = contract(picker, cols, ((1,), (1,)))
    named = weight_rows > 0
    before = lax.broadcasted_iota(jnp.int32, (rows, rows), 0)
    after = lax.broadcasted_iota(jnp.int32, (rows, rows), 1)
    earlier = (before < after) & (before // tok_rows == after // tok_rows)
    rank = contract(
        jnp.where(named, 1.0, 0.0).astype(bf16),
        jnp.where(earlier, 1.0, 0.0).astype(bf16),
        ((1,), (0,)),
    )
    first_slot = lax.broadcasted_iota(jnp.int32, rank.shape, 1) // tok_rows * slots
    rank = jnp.where(named, rank.astype(jnp.int32) + first_slot, -1)
    slot = lax.broadcasted_iota(jnp.int32, (rows // tok_rows * slots, rows), 0)
    picks = [jnp.where(slot == rank[line : line + 1], 1.0, 0.0) for line in range(lines)]
    return weight_rows, picks


def collect_kernel(block_00, block_10, block_01, block_11, picker_ref, own_ref, send_ref, *, slots):
    local_experts, taken, width = own_ref.shape
    tok_rows = block_00.shape[0]
    pair = taken // 2
    for at, pair_refs in enumerate(((block_01, block_11), (block_00, block_10))):
        rows = jnp.concatenate([ref[...] for ref in pair_refs], axis=0)
        _, picks = pair_routes(
            rows[:, width:], picker_ref[...], 2 * local_experts, tok_rows, slots
        )
        picked = contract(
            jnp.concatenate(picks, axis=0).astype(bf16), rows[:, :width], ((1,), (0,))
        ).astype(bf16)
        for expert in range(local_experts):
            there = slice(at * pair, (at + 1) * pair)
            own_ref[expert, there, :] = picked[expert * pair : (expert + 1) * pair]
            line = local_experts + expert
            send_ref[expert, there, :] = picked[line * pair : (line + 1) * pair]


def expert_kernel(*refs):
    *row_refs, gate_ref, up_ref, down_ref, own_ref, send_ref = refs
    half = len(row_refs) // 2
    for sources, out_ref in ((row_refs[half:], send_ref), (row_refs[:half], own_ref)):
        rows = jnp.concatenate([ref[0] for ref in sources], axis=0)
        gate = contract(rows, gate_ref[0], ((1,), (0,)))
        up = contract(rows, up_ref[0], ((1,), (0,)))
        hidden = (gate / (1.0 + jnp.exp(-gate)) * up).astype(bf16)
        out_ref[0] = contract(hidden, down_ref[0], ((1,), (0,))).astype(bf16)


def spread_kernel(*refs, slots, places):
    *cols_refs, picker_ref, own_ref, got_ref, far_ref, near_ref, here_ref = refs
    local_experts = own_ref.shape[0]
    tok_rows = cols_refs[0].shape[0]
    pair = 2 * slots
    for group, place in enumerate(places):
        cols_00, cols_10, cols_01, cols_11 = cols_refs[4 * group : 4 * group + 4]
        for at, pair_refs in enumerate(((cols_01, cols_11), (cols_00, cols_10))):
            cols = jnp.concatenate([ref[...] for ref in pair_refs], axis=0)
            weight_rows, picks = pair_routes(
                cols, picker_ref[...], 2 * local_experts, tok_rows, slots
            )
            first = (2 * place + at) * pair
            scaled = []
            for line, pick in enumerate(picks):
                result_ref = (own_ref, got_ref)[line // local_experts]
                result = result_ref[line % local_experts, first : first + pair, :]
                weight = jnp.sum(pick * weight_rows[line : line + 1], axis=1, keepdims=True)
                scaled.append((result.astype(f32) * weight).astype(bf16))
            summed = contract(
                jnp.concatenate(picks, axis=0).astype(bf16),
                jnp.concatenate(scaled, axis=0),
                ((0,), (0,)),
            ).astype(bf16)
            if at == 0:
                far_ref[group, 0] = summed[:tok_rows]
                far_ref[group, 1] = summed[tok_rows:]
            else:
                here_ref[group] = summed[:tok_rows]
                near_ref[group] = summed[tok_rows:]


def expert_layer_gathered(
    stream,
    moe_gain,
    router,
    expert_ids,
    expert_gate,
    expert_up,
    expert_down,
    sources,
    early,
):
    tok_rows, width = stream.shape
    local_experts, _, hidden_width = expert_gate.shape
    experts_all = local_experts * sources
    depth = sources // 8
    place = lax.axis_index(("ctx", "head"))

    def sent(value, move):
        pairs = []
        for device in range(sources):
            z, y, x, core = device // 8, device // 4 % 2, device // 2 % 2, device % 2
            z, y, x, core = move(z, y, x, core)
            pairs.append((device, ((z * 2 + y) * 2 + x) * 2 + core))
        return lax.ppermute(value, ("ctx", "head"), pairs)

    def lifted(value, steps):
        return sent(value, lambda z, y, x, core: ((z + steps) % depth, y, x, core))

    def first(value):
        return sent(value, lambda z, y, x, core: (z, y ^ (1 - core), x ^ core, core))

    def second(value):
        return sent(value, lambda z, y, x, core: (z, y ^ core, x ^ (1 - core), core))

    def swapped(value):
        return sent(value, lambda z, y, x, core: (z, y, x, 1 - core))

    normed = rms_rows(stream, moe_gain).astype(bf16)
    logits = jnp.dot(normed, router, preferred_element_type=f32)
    named = jnp.any(
        expert_ids[:, :, None] == jnp.arange(experts_all, dtype=jnp.int32)[None, None, :], axis=1
    )
    raised = jnp.where(named, jnp.exp(logits), 0.0)
    weights = raised / jnp.sum(raised, axis=1, keepdims=True)
    coarse = lax.reduce_precision(weights, 8, 7)
    packet = jnp.concatenate(
        [normed, coarse.astype(bf16), (weights - coarse).astype(bf16)], axis=1
    )

    capacity = (11 * tok_rows * expert_ids.shape[1] + 10 * experts_all - 1) // (10 * experts_all)
    slots = -(-capacity // 8) * 8
    taken = 4 * slots
    column = jnp.arange(2 * experts_all, dtype=jnp.int32)[None, :] % experts_all
    line = jnp.arange(16, dtype=jnp.int32)[:, None]
    owner = jnp.where(line < local_experts, place, place ^ 1)
    picker = (
        (line < 2 * local_experts) & (column == owner * local_experts + line % local_experts)
    ).astype(bf16)

    order = [0, *range(depth - 1, 0, -1)]
    own_rows, got_rows, outcome = {}, {}, {}
    blocks = {}
    mine = packet
    for at, steps in enumerate(order):
        if steps:
            source = packet if steps == 1 else mine
            earlier = [blocks[order[at - 1]][0]] if at > 1 else []
            if at > 1:
                earlier += blocks[order[at - 2]][1:3]
            if earlier:
                source = after(source, *earlier)
            mine = lifted(source, 1 if steps == 1 else -1)
        onward = mine
        if at:
            onward = after(mine, *blocks[order[at - 1]][1:3])
        near = first(onward)
        blocks[steps] = (mine, near, second(onward), second(near))

    picked_spec = pl.BlockSpec((local_experts, taken, width), lambda g: (0, 0, 0))

    def collect(steps, *earlier):
        rows = blocks[steps][0]
        own, send = pl.pallas_call(
            functools.partial(collect_kernel, slots=slots),
            grid=(1,),
            in_specs=[whole_ref(packet)] * 4 + [whole_ref(picker)],
            out_specs=[picked_spec] * 2,
            out_shape=[jax.ShapeDtypeStruct((local_experts, taken, width), bf16)] * 2,
            compiler_params=pltpu.CompilerParams(vmem_limit_bytes=24 << 20),
            cost_estimate=worth(2),
            name="collect",
        )(after(rows, *earlier) if earlier else rows, *blocks[steps][1:], picker)
        own_rows[steps] = own
        got_rows[steps] = swapped(send)

    def run_experts(members, *earlier):
        row_spec = pl.BlockSpec((1, taken, width), lambda e: (e, 0, 0))
        out_spec = pl.BlockSpec((1, len(members) * taken, width), lambda e: (e, 0, 0))
        results, send_back = pl.pallas_call(
            expert_kernel,
            grid=(local_experts,),
            in_specs=[row_spec] * (2 * len(members))
            + [
                pl.BlockSpec((1, width, hidden_width), lambda e: (e, 0, 0)),
                pl.BlockSpec((1, width, hidden_width), lambda e: (e, 0, 0)),
                pl.BlockSpec((1, hidden_width, width), lambda e: (e, 0, 0)),
            ],
            out_specs=[out_spec] * 2,
            out_shape=[jax.ShapeDtypeStruct((local_experts, len(members) * taken, width), bf16)]
            * 2,
            compiler_params=pltpu.CompilerParams(vmem_limit_bytes=40 << 20),
            cost_estimate=worth(4 + 3 * len(members) if len(members) > 1 else 1),
            name="experts",
        )(
            after(own_rows[members[0]], *earlier),
            *[own_rows[member] for member in members[1:]],
            *[got_rows[member] for member in members],
            expert_gate,
            expert_up,
            expert_down,
        )
        got_back = swapped(send_back)
        for at, member in enumerate(members):
            outcome[member] = (at, results, got_back)

    def spread(members):
        places = [outcome[member][0] for member in members]
        _, results, got_back = outcome[members[0]]
        cols_spec = pl.BlockSpec(
            (tok_rows, 2 * experts_all), lambda g: (0, width // (2 * experts_all))
        )
        row_shape = jax.ShapeDtypeStruct((len(members), tok_rows, width), bf16)
        far_shape = jax.ShapeDtypeStruct((len(members), 2, tok_rows, width), bf16)
        return pl.pallas_call(
            functools.partial(spread_kernel, slots=slots, places=places),
            grid=(1,),
            in_specs=[cols_spec] * (4 * len(members))
            + [whole_ref(picker), whole_ref(results), whole_ref(results)],
            out_specs=[whole_ref(far_shape), whole_ref(row_shape), whole_ref(row_shape)],
            out_shape=[far_shape, row_shape, row_shape],
            compiler_params=pltpu.CompilerParams(vmem_limit_bytes=28 << 20),
            cost_estimate=worth(1),
            name="spread",
        )(*(block for member in members for block in blocks[member]), picker, results, got_back)

    last, batch = order[-1], order[-2:0:-1]
    for steps in order[:-2]:
        collect(steps, blocks[order[-2]][0])
    collect(order[-2], *blocks[last][:3])
    run_experts(order[:-1])
    ready = {steps: spread([steps]) for steps in batch}
    collect(last, *[far for far, _, _ in ready.values()])
    run_experts([last])
    ready[last], ready[0] = spread([last]), spread([0])

    def joined(steps, direct, diagonal):
        _, near, here = ready[steps]
        near = first((near[0].astype(f32) + diagonal.astype(f32)).astype(bf16))
        return here[0].astype(f32) + direct.astype(f32) + near.astype(f32)

    moving = []
    for at, steps in enumerate(batch):
        across = second(ready[steps][0])
        total = joined(steps, across[0, 0], across[0, 1])
        if moving:
            total += moving[-1].astype(f32)
        moving.append(lifted(total.astype(bf16), 1))
    across = after(second(ready[last][0]), moving[0])
    total = joined(last, across[0, 0], across[0, 1])
    rising = lifted(total.astype(bf16), -1)
    far = ready[0][0]
    diagonal = after(second(far[0, 1]), moving[-1])
    total = joined(0, second(far[0, 0]), diagonal)
    total += moving[-1].astype(f32) + rising.astype(f32)
    return after(total, *early).astype(bf16)


def expert_layer_sent(
    stream, moe_gain, router, expert_ids, expert_gate, expert_up, expert_down, sources
):
    tok_rows, model_width = stream.shape
    top_count = expert_ids.shape[1]
    local_experts = expert_gate.shape[0]
    experts_all = local_experts * sources
    capacity = (11 * tok_rows * top_count + 10 * experts_all - 1) // (10 * experts_all)
    normed = rms_rows(stream, moe_gain).astype(jnp.bfloat16)
    logits = jnp.dot(normed, router, preferred_element_type=jnp.float32)
    chosen = jnp.take_along_axis(logits, expert_ids, axis=1)
    raised = jnp.exp(chosen)
    weights = raised / jnp.sum(raised, axis=1, keepdims=True)
    flat_ids = expert_ids.reshape(-1)
    matches = (flat_ids[:, None] == jnp.arange(experts_all, dtype=jnp.int32)[None, :]).astype(
        jnp.int32
    )
    slot_index = jnp.sum((jnp.cumsum(matches, axis=0) - 1) * matches, axis=1)
    places = flat_ids * capacity + slot_index
    token_rows = jnp.arange(tok_rows * top_count, dtype=jnp.int32) // top_count
    outgoing = (
        jnp.zeros((experts_all * capacity, model_width), jnp.bfloat16)
        .at[places]
        .set(normed[token_rows])
    )
    outgoing = outgoing.reshape(sources, local_experts, capacity, model_width)
    received = lax.all_to_all(outgoing, ("ctx", "head"), split_axis=0, concat_axis=0, tiled=True)
    gate_part = jnp.einsum(
        "nesd,edh->nesh", received, expert_gate, preferred_element_type=jnp.float32
    )
    up_part = jnp.einsum("nesd,edh->nesh", received, expert_up, preferred_element_type=jnp.float32)
    hidden = (jax.nn.silu(gate_part) * up_part).astype(jnp.bfloat16)
    returned = lax.all_to_all(
        jnp.einsum(
            "nesh,ehd->nesd", hidden, expert_down, preferred_element_type=jnp.float32
        ).astype(jnp.bfloat16),
        ("ctx", "head"),
        split_axis=0,
        concat_axis=0,
        tiled=True,
    )
    gathered_rows = returned.reshape(experts_all * capacity, model_width)[places].reshape(
        tok_rows, top_count, model_width
    )
    return jnp.sum(weights[:, :, None] * gathered_rows.astype(jnp.float32), axis=1).astype(
        jnp.bfloat16
    )


def unit_inverses(strict_parts):
    size = strict_parts[0].shape[0]
    row = lax.broadcasted_iota(jnp.int32, (size, size), 0)
    col = lax.broadcasted_iota(jnp.int32, (size, size), 1)
    unit = jnp.where(row == col, 1.0, 0.0)
    joining = (row // 2 == col // 2) & (row != col)
    inverses = [unit - jnp.where(joining, part, 0.0) for part in strict_parts]
    half = 2
    while half < size:
        joining = (row // (2 * half) == col // (2 * half)) & (row // half != col // half)
        corners = [jnp.where(joining, part, 0.0) for part in strict_parts]
        if half < 8:
            steps = [contract_close(c, inverse) for c, inverse in zip(corners, inverses)]
            moves = [contract_close(inverse, step) for inverse, step in zip(inverses, steps)]
            inverses = [inverse - move for inverse, move in zip(inverses, moves)]
        else:
            starts = range(0, size, 2 * half)

            def lower_rows(array):
                return jnp.concatenate([array[at + half : at + 2 * half] for at in starts], axis=0)

            zeros = jnp.zeros((half, size), f32)
            steps = [
                contract_close(lower_rows(c), inverse) for c, inverse in zip(corners, inverses)
            ]
            steps = [
                jnp.concatenate(
                    [
                        piece
                        for at in range(0, size // 2, half)
                        for piece in (zeros, step[at : at + half])
                    ],
                    axis=0,
                )
                for step in steps
            ]
            lowers = [lower_rows(inverse) for inverse in inverses]
            lowers = [lower - contract_close(lower, step) for lower, step in zip(lowers, steps)]
            inverses = [
                jnp.concatenate(
                    [
                        piece
                        for at in starts
                        for piece in (
                            inverse[at : at + half],
                            lower[at // 2 : at // 2 + half],
                        )
                    ],
                    axis=0,
                )
                for inverse, lower in zip(inverses, lowers)
            ]
        half *= 2
    return inverses


def unit_rows(rows):
    return rows * lax.rsqrt(jnp.sum(rows * rows, axis=-1, keepdims=True) + epsilon)


def delta_kernel(
    place_ref,
    near_raw,
    far_raw,
    near_beta,
    far_beta,
    near_decay,
    far_decay,
    rim_ref,
    taps_ref,
    rate_ref,
    core_ref,
    reading_ref,
    moved_ref,
    extended,
    mixed,
    strengths,
    falls,
    carried,
    *,
    key_heads,
    chunk,
    tok_rows,
):
    rows, conv_cols = near_raw.shape[0] + far_raw.shape[0], near_raw.shape[1]
    heads = moved_ref.shape[0]
    group = heads // key_heads
    tap_count = taps_ref.shape[0]
    rim = rim_ref.shape[0]
    extended[0:rim, :] = rim_ref[...]
    step = 0
    for part_refs in ((near_raw, near_beta, near_decay), (far_raw, far_beta, far_decay)):
        for first in range(0, part_refs[0].shape[0], tok_rows):
            at = pl.multiple_of((place_ref[0] ^ step) * tok_rows, tok_rows)
            part = slice(first, first + tok_rows)
            extended[pl.ds(rim + at, tok_rows), :] = part_refs[0][part, :].astype(f32)
            strengths[pl.ds(at, tok_rows), :] = 1.0 / (1.0 + jnp.exp(-part_refs[1][part, :]))
            shifted = part_refs[2][part, :] + rate_ref[1:2, :]
            softened = jnp.maximum(shifted, 0.0) + jnp.log1p(jnp.exp(-jnp.abs(shifted)))
            falls[pl.ds(at, tok_rows), :] = -jnp.exp(rate_ref[0:1, :]) * softened
            step += 1
    key_at, value_at = key_heads * DK, 2 * key_heads * DK
    for start in range(0, rows, chunk):
        for first in range(0, conv_cols, DK):
            columns = slice(first, first + DK)
            summed = jnp.zeros((chunk, DK), f32)
            for tap in range(tap_count):
                offset = rim - (tap_count - 1) + start + tap
                summed += taps_ref[tap : tap + 1, columns] * extended[
                    offset : offset + chunk, columns
                ]
            value = summed / (1.0 + jnp.exp(-summed))
            if first < key_at:
                value = unit_rows(value) * DK**-0.5
            elif first < value_at:
                value = unit_rows(value)
            mixed[start : start + chunk, columns] = value
    row = lax.broadcasted_iota(jnp.int32, (chunk, chunk), 0)
    col = lax.broadcasted_iota(jnp.int32, (chunk, chunk), 1)
    inclusive, strict = row >= col, row > col
    lower = jnp.where(inclusive, 1.0, 0.0)
    across = lax.broadcasted_iota(jnp.int32, (DK, 2 * DK), 1)
    down = lax.broadcasted_iota(jnp.int32, (DK, 2 * DK), 0)
    carried[...] = jnp.broadcast_to(
        jnp.where(across == down + DK, 1.0, 0.0)[None], carried.shape
    )

    def advance(step, nothing):
        here = pl.ds(pl.multiple_of(step * chunk, chunk), chunk)
        fall = falls[here, :]
        strength = strengths[here, :]
        cumulative = contract(lower, fall, ((1,), (0,)), lax.Precision.HIGHEST)
        cumulative_rows = contract(fall, lower, ((0,), (1,)), lax.Precision.HIGHEST)
        owners = range(heads)
        queries = [mixed[here, k * DK : (k + 1) * DK] for k in range(key_heads)]
        keys = [mixed[here, key_at + k * DK : key_at + (k + 1) * DK] for k in range(key_heads)]
        dots = [
            contract_rows(jnp.concatenate([key, query], axis=0), key)
            for key, query in zip(keys, queries)
        ]
        totals = [cumulative[:, head : head + 1] for head in owners]
        kept = [
            jnp.where(
                inclusive,
                jnp.exp(jnp.where(inclusive, totals[head] - cumulative_rows[head : head + 1, :], 0.0)),
                0.0,
            )
            for head in owners
        ]
        own = [strength[:, head : head + 1] for head in owners]
        solvers = unit_inverses(
            [
                own[head] * jnp.where(strict, kept[head], 0.0) * dots[head // group][:chunk]
                for head in owners
            ]
        )
        risen = [jnp.exp(total) for total in totals]
        solved = [
            contract_close(
                solvers[head],
                own[head]
                * jnp.concatenate(
                    [
                        mixed[here, value_at + head * DK : value_at + (head + 1) * DK],
                        risen[head] * keys[head // group],
                    ],
                    axis=1,
                ),
            )
            for head in owners
        ]
        states = [carried[head] for head in owners]
        read = [
            contract_close(
                jnp.concatenate(
                    [solved[head][:, DK:], risen[head] * queries[head // group]], axis=0
                ),
                states[head],
            )
            for head in owners
        ]
        updates = [
            jnp.concatenate([solved[head][:, :DK], jnp.zeros((chunk, DK), f32)], axis=1)
            - read[head][:chunk]
            for head in owners
        ]
        for head in owners:
            last = totals[head][chunk - 1 :, :]
            leaving = jnp.exp(last - totals[head]) * keys[head // group]
            carried[head] = jnp.exp(last) * states[head] + contract_close(
                leaving.T, updates[head]
            )
        for head in owners:
            result = read[head][chunk:] + contract_close(
                kept[head] * dots[head // group][chunk:], updates[head]
            )
            core_ref[here, head * DK : (head + 1) * DK] = result[:, :DK]
            reading_ref[here, head * DK : (head + 1) * DK] = result[:, DK:]
        return nothing

    lax.fori_loop(0, rows // chunk, advance, 0)
    moved_ref[...] = carried[...].astype(bf16)


def project_kernel(place_ref, *refs, blocks, halos):
    row_refs, halo_refs = refs[:blocks], refs[blocks : blocks + halos]
    weight_refs, out_refs = refs[blocks + halos : blocks + halos + 6], refs[blocks + halos + 6 :]
    pieces = [ref[...] for ref in row_refs]
    rows = blocks * row_refs[0].shape[0]
    if halos:
        pieces.append(
            sum(
                jnp.where((place_ref[0] ^ step) == halos - 1, 1.0, 0.0) * ref[...].astype(f32)
                for step, ref in enumerate(halo_refs)
            ).astype(bf16)
        )
    pieces = jnp.concatenate(pieces, axis=0)
    qkv_ref, gate_ref, beta_ref, decay_ref = out_refs[:4]
    first = 0
    for weight_ref in weight_refs[:3]:
        product = contract(pieces, weight_ref[...], ((1,), (0,))).astype(bf16)
        last = first + weight_ref.shape[1]
        qkv_ref[:, first:last] = product[:rows]
        if halos:
            out_refs[4][:, first:last] = product[rows:].astype(f32)
        first = last
    pieces = pieces[:rows]
    gate_ref[...] = contract(pieces, weight_refs[3][...], ((1,), (0,))).astype(bf16)
    beta_ref[...] = contract(pieces, weight_refs[4][...], ((1,), (0,)))
    decay_ref[...] = contract(pieces, weight_refs[5][...], ((1,), (0,)))


def pair_kernel(second_ref, mine_ref, other_ref, joined_ref):
    late = second_ref[0] == 1
    for head in range(mine_ref.shape[0]):
        mine, other = mine_ref[head].astype(f32), other_ref[head].astype(f32)
        earlier = jnp.where(late, other, mine).astype(bf16)
        later = jnp.where(late, mine, other)
        joined = contract(later[:, DK:].astype(bf16), earlier, ((1,), (0,)))
        joined_ref[head, :, :DK] = (joined[:, :DK] + later[:, :DK]).astype(bf16)
        joined_ref[head, :, DK:] = joined[:, DK:].astype(bf16)


def finish_kernel(
    where_ref,
    near_pairs_ref,
    far_pairs_ref,
    other_ref,
    core_ref,
    reading_ref,
    near_gate,
    far_gate,
    gain_ref,
    gated_ref,
):
    states = []
    for head in range(other_ref.shape[0]):
        state = contract(near_pairs_ref[head, :, DK:], far_pairs_ref[head], ((1,), (0,)))
        state += near_pairs_ref[head, :, :DK].astype(f32)
        passed = contract(other_ref[head, :, DK:], state.astype(bf16), ((1,), (0,)))
        passed += other_ref[head, :, :DK].astype(f32)
        states.append(jnp.where(where_ref[0] == 1, passed, state))
    gates = jnp.where(pl.program_id(0) < 2, near_gate[...].astype(f32), far_gate[...].astype(f32))
    for head, state in enumerate(states):
        columns = slice(head * DK, (head + 1) * DK)
        core = core_ref[:, columns] + contract_close(reading_ref[:, columns], state)
        normal = (
            core
            * lax.rsqrt(jnp.mean(core * core, axis=-1, keepdims=True) + epsilon)
            * gain_ref[...]
        )
        gate = gates[:, columns]
        gated_ref[:, columns] = (normal * (gate / (1.0 + jnp.exp(-gate)))).astype(bf16)


def output_kernel(*refs, blocks, begun):
    row_refs, weight_refs, out_ref = refs[:blocks], refs[blocks : -1 - begun], refs[-1]
    total = refs[-2][...] if begun else 0.0
    pieces = iter(weight_refs)
    for rows_ref in row_refs:
        at = 0
        while at < rows_ref.shape[1]:
            weight_ref = next(pieces)
            depth = weight_ref.shape[0]
            total += contract(rows_ref[:, at : at + depth], weight_ref[...], ((1,), (0,)))
            at += depth
    out_ref[...] = total.astype(out_ref.dtype)


def on_device(
    stream,
    moe_gain,
    router,
    expert_ids,
    expert_gate,
    expert_up,
    expert_down,
    mixer_gain,
    query_weight,
    key_weight,
    value_weight,
    output_gate,
    beta_weight,
    decay_weight,
    query_conv,
    key_conv,
    value_conv,
    decay_log,
    decay_bias,
    head_gain,
    out_weight,
):
    ctx_count = lax.axis_size("ctx")
    head_count = lax.axis_size("head")
    sources = ctx_count * head_count
    ctx_place = lax.axis_index("ctx")
    experts = (stream, moe_gain, router, expert_ids, expert_gate, expert_up, expert_down)
    cut = out_weight.shape[0] // 2
    out_halves = (out_weight[:cut], out_weight[cut:])
    if 2 * sources * stream.size <= GATHER_LIMIT and head_count == 4 and ctx_count in (6, 8):
        moe_out = expert_layer_gathered(*experts, sources, out_halves)
    else:
        moe_out = expert_layer_sent(*experts, sources)
    mixer_in = rms_rows(
        stream.astype(jnp.float32) + moe_out.astype(jnp.float32), mixer_gain
    ).astype(jnp.bfloat16)
    head_place = lax.axis_index("head")

    def crossed(value, step):
        pairs = [(source, source ^ step) for source in range(head_count)]
        return lax.ppermute(value, "head", pairs)


    def from_chip(value, *earlier):
        return [after(value, *earlier) if earlier else value, crossed(value, 1)]

    def from_others(value, *earlier):
        received = []
        for step in range(2, head_count, 2):
            part = crossed(value, step)
            received += [part, crossed(after(part, *earlier) if earlier else part, 1)]
        return received

    in_vmem = pl.BlockSpec(memory_space=pltpu.VMEM)
    in_smem = pl.BlockSpec(memory_space=pltpu.SMEM)
    tok_rows, width = stream.shape
    rows = tok_rows * head_count
    key_cols, value_cols = query_weight.shape[1], value_weight.shape[1]
    heads = beta_weight.shape[1]
    rim_len = 16
    halo = passed_along(mixer_in[tok_rows - rim_len :], "ctx", 1)
    halos = from_chip(halo) + from_others(halo)
    conv_cols = 2 * key_cols + value_cols
    matrices = (
        query_weight, key_weight, value_weight, output_gate, beta_weight, decay_weight
    )

    def project(pieces, halos):
        count = len(pieces) * tok_rows
        shapes = [
            jax.ShapeDtypeStruct((count, conv_cols), bf16),
            jax.ShapeDtypeStruct((count, value_cols), bf16),
            jax.ShapeDtypeStruct((count, heads), f32),
            jax.ShapeDtypeStruct((count, heads), f32),
        ]
        if halos:
            shapes.append(jax.ShapeDtypeStruct((rim_len, conv_cols), f32))
        return pl.pallas_call(
            functools.partial(project_kernel, blocks=len(pieces), halos=len(halos)),
            in_specs=[in_smem] + [in_vmem] * (len(pieces) + len(halos) + 6),
            out_shape=shapes,
            compiler_params=pltpu.CompilerParams(vmem_limit_bytes=52 << 20),
            cost_estimate=worth(4),
            name="project",
        )(head_place.reshape(1), *pieces, *halos, *matrices)

    near_raw = project(from_chip(mixer_in, halo), [])
    far_pieces = from_others(mixer_in, near_raw[0], halos[2])
    far_raw = project(far_pieces, halos)
    rim = far_raw[4]
    key_heads = key_cols // DK
    taps = jnp.concatenate([query_conv, key_conv, value_conv], axis=1)
    rates = jnp.stack([decay_log, decay_bias])
    chunk = math.gcd(rows, CHUNK)
    core, reading, moved = pl.pallas_call(
        functools.partial(delta_kernel, key_heads=key_heads, chunk=chunk, tok_rows=tok_rows),
        in_specs=[in_smem] + [in_vmem] * 9,
        out_shape=(
            jax.ShapeDtypeStruct((rows, value_cols), f32),
            jax.ShapeDtypeStruct((rows, value_cols), f32),
            jax.ShapeDtypeStruct((heads, DK, 2 * DK), bf16),
        ),
        scratch_shapes=[
            pltpu.VMEM((rows + rim_len, conv_cols), f32),
            pltpu.VMEM((rows, conv_cols), f32),
            pltpu.VMEM((rows, heads), f32),
            pltpu.VMEM((rows, heads), f32),
            pltpu.VMEM((heads, DK, 2 * DK), f32),
        ],
        compiler_params=pltpu.CompilerParams(vmem_limit_bytes=24 << 20),
        cost_estimate=worth(16),
        name="delta",
    )(
        head_place.reshape(1),
        *(array for kind in (0, 2, 3) for array in (near_raw[kind], far_raw[kind])),
        rim,
        taps,
        rates,
    )
    start_upper, start_lower = after(out_halves[0], far_pieces[-1]), after(out_halves[1], moved)
    upper = [crossed(start_upper, step) for step in range(2, head_count, 2)]
    lower = [crossed(start_lower, step) for step in range(2, head_count, 2)]

    in_pair = (ctx_place % 2).reshape(1)
    other = lax.ppermute(moved, "ctx", [(place, place ^ 1) for place in range(ctx_count)])
    other = after(other, *upper)
    window = pl.pallas_call(
        pair_kernel,
        in_specs=[in_smem, in_vmem, in_vmem],
        out_shape=jax.ShapeDtypeStruct(moved.shape, bf16),
        compiler_params=pltpu.CompilerParams(vmem_limit_bytes=8 << 20),
        name="pair",
    )(in_pair, moved, other)

    def composed(later, earlier, columns):
        product = jnp.einsum(
            "hij,hjk->hik",
            later[:, :, DK:],
            earlier[:, :, :columns],
            preferred_element_type=f32,
        )
        added = (product[:, :, :DK] + later[:, :, :DK].astype(f32)).astype(bf16)
        return jnp.concatenate([added, product[:, :, DK:].astype(bf16)], axis=2)

    reach, near_pairs, far_pairs = 1, None, jnp.zeros((heads, DK, DK), bf16)
    while reach < ctx_count // 2:
        last = 2 * reach >= ctx_count // 2
        if last and near_pairs is not None:
            far_pairs = passed_along(window[:, :, :DK], "ctx", 2 * reach)
        else:
            arrived = passed_along(window, "ctx", 2 * reach)
            if near_pairs is None:
                near_pairs = arrived
            else:
                near_pairs = composed(near_pairs, arrived, 2 * DK)
            window = composed(window, arrived, DK if 4 * reach >= ctx_count // 2 else 2 * DK)
        reach *= 2
    far_pairs = after(far_pairs, *lower)

    gated = pl.pallas_call(
        finish_kernel,
        grid_spec=pltpu.PrefetchScalarGridSpec(
            num_scalar_prefetch=1,
            grid=(head_count,),
            in_specs=[whole_ref(near_pairs), whole_ref(far_pairs), whole_ref(other)]
            + [
                pl.BlockSpec((tok_rows, value_cols), lambda step, where: (where[1] ^ step, 0)),
                pl.BlockSpec((tok_rows, value_cols), lambda step, where: (where[1] ^ step, 0)),
                pl.BlockSpec((tok_rows, value_cols), lambda step, where: (step % 2, 0)),
                pl.BlockSpec((tok_rows, value_cols), lambda step, where: (step % 2, 0)),
                pl.BlockSpec((1, DK), lambda step, where: (0, 0)),
            ],
            out_specs=pl.BlockSpec((tok_rows, value_cols), lambda step, where: (step, 0)),
        ),
        out_shape=jax.ShapeDtypeStruct((rows, value_cols), bf16),
        compiler_params=pltpu.CompilerParams(vmem_limit_bytes=12 << 20),
        name="finish",
    )(
        jnp.stack([ctx_place % 2, head_place]),
        near_pairs,
        far_pairs,
        other,
        core,
        reading,
        near_raw[1],
        far_raw[1],
        head_gain.reshape(1, -1),
    )
    gated_parts = []
    for step in range(head_count):
        part = gated[step * tok_rows : (step + 1) * tok_rows]
        gated_parts.append(crossed(part, step) if step else part)
    near_weights = [out_weight, crossed(after(out_weight, moved), 1)]
    far_weights = []
    for shard in zip(upper, lower):
        far_weights += shard
        far_weights += [crossed(after(part, far_pairs), 1) for part in shard]

    def multiplied(parts, weights, begun, kind):
        columns = pl.BlockSpec((tok_rows, width // 4), lambda n: (0, n))
        return pl.pallas_call(
            functools.partial(output_kernel, blocks=len(parts), begun=len(begun)),
            grid=(4,),
            in_specs=[whole_ref(part) for part in parts]
            + [pl.BlockSpec((part.shape[0], width // 4), lambda n: (0, n)) for part in weights]
            + [columns] * len(begun),
            out_specs=columns,
            out_shape=jax.ShapeDtypeStruct(stream.shape, kind),
            compiler_params=pltpu.CompilerParams(vmem_limit_bytes=20 << 20),
            cost_estimate=worth(3),
            name="output",
        )(*parts, *weights, *begun)

    begun = multiplied(gated_parts[:2], near_weights, [], f32)
    mixer_out = multiplied(gated_parts[2:], far_weights, [begun], bf16)
    return (moe_out, mixer_out)


def solution(mesh):
    return jax.shard_map(
        on_device,
        mesh=mesh,
        in_specs=(
            P(("ctx", "head"), None),
            P(),
            P(),
            P(("ctx", "head"), None),
            P(("ctx", "head"), None, None),
            P(("ctx", "head"), None, None),
            P(("ctx", "head"), None, None),
            P(),
            P(None, "head"),
            P(None, "head"),
            P(None, "head"),
            P(None, "head"),
            P(None, "head"),
            P(None, "head"),
            P(None, "head"),
            P(None, "head"),
            P(None, "head"),
            P("head"),
            P("head"),
            P(),
            P("head", None),
        ),
        out_specs=(P(("ctx", "head"), None), P(("ctx", "head"), None)),
        check_vma=False,
    )
```
